32 devices in a mesh: fsdp: 4 (over x, core), seq: 4 (over z), tp: 2 (over y).
Axes of the slice: x: 2, y: 2, z: 4, core: 2. Of those that a mesh axis runs over, the one named last changes fastest.
Arguments:
- tokens: bfloat16 [4096, 2560], P(('fsdp', 'seq', 'tp')), may hold values from -6 to 6
- doc_lengths: int32 [4, 3], P('fsdp'), may hold values from 1 to 769, 1024 in all within a row
- w_query: bfloat16 [2560, 2560], P(('fsdp', 'seq'), 'tp'), may hold values from -0.15625 to 0.15625
- w_key: bfloat16 [2560, 640], P(('fsdp', 'seq'), 'tp'), may hold values from -0.15625 to 0.15625
- w_value: bfloat16 [2560, 640], P(('fsdp', 'seq'), 'tp'), may hold values from -0.125 to 0.125
- w_out: bfloat16 [2560, 2560], P('tp', ('fsdp', 'seq')), may hold values from -1 to 1
- w_gate: bfloat16 [2560, 6912], P(('fsdp', 'seq'), 'tp'), may hold values from -0.125 to 0.125
- w_up: bfloat16 [2560, 6912], P(('fsdp', 'seq'), 'tp'), may hold values from -0.125 to 0.125
- w_down: bfloat16 [6912, 2560], P('tp', ('fsdp', 'seq')), may hold values from -0.078125 to 0.078125
- norm_gains: bfloat16 [2, 2560], P(None, ('fsdp', 'seq')), may hold values from 0.5 to 1.5
- cotangent: bfloat16 [4096, 2560], P(('fsdp', 'seq', 'tp')), may hold values from -6 to 6
Outputs:
- mixed_out: bfloat16 [4096, 2560], P(('fsdp', 'seq', 'tp'))
- grad_tokens: float32 [4096, 2560], P(('fsdp', 'seq', 'tp'))
- grad_query: float32 [2560, 2560], P(('fsdp', 'seq'), 'tp')
- grad_key: float32 [2560, 640], P(('fsdp', 'seq'), 'tp')
- grad_value: float32 [2560, 640], P(('fsdp', 'seq'), 'tp')
- grad_out: float32 [2560, 2560], P('tp', ('fsdp', 'seq'))
- grad_gate: float32 [2560, 6912], P(('fsdp', 'seq'), 'tp')
- grad_up: float32 [2560, 6912], P(('fsdp', 'seq'), 'tp')
- grad_down: float32 [6912, 2560], P('tp', ('fsdp', 'seq'))
- grad_gains: float32 [2, 2560], P(None, ('fsdp', 'seq'))
The draws below stay inside these ranges and needn't reach their ends.
Inputs may be any that keep to these rules, and one draw needn't show every extreme that they name: `doc_lengths`: in each sequence the document lengths sum to 1024 and the longest has exactly 769 tokens.
All inputs are finite; a program needn't handle non-finite values.
Results may differ from the reference program's by a relative error of at most 0.022.
Values may be sent and summed in bfloat16 or wider, within the bound.
No kernel may reach another device: no remote copies, remote signals or barrier semaphores. Data moves between devices by JAX's collectives and lax.ppermute only.
A program may use at most 192 MiB of HBM per device.

```python
import math
import jax
import jax.numpy as jnp
import numpy as np
from jax import lax

D = 2560
HEADS = 32
KV_HEADS = 8
HEAD_DIM = 80
FF = 6912
BLOCK = 256
DOCS = 3
GROUP = 4
SPAN = 256
SEQ_LEN = 1024
SEQS = 4
TOKENS = 4096


def block_levels(key, dims, shards, least, top_value):
    gain, own = 1.0, jax.random.fold_in(key, 6)
    for axis_at, parts in shards:
        draws = jnp.exp(jax.random.uniform(jax.random.fold_in(own, axis_at), (parts,), jnp.float32, least / len(shards), top_value / len(shards)))
        gain = gain * jnp.repeat(draws, dims[axis_at] // parts).reshape([-1 if axis == axis_at else 1 for axis in range(len(dims))])
    return gain


def profile(number_of, total, reach, lean):
    portions = [(1 << 20) // math.isqrt(grade ** lean) + 1 for grade in range(2, number_of + 1)]
    spare, counts = total - reach - (number_of - 1), [1] * (number_of - 1)
    while spare > 0:
        movable = [i for i in range(number_of - 1) if counts[i] < reach]
        pool, left = sum([portions[i] for i in movable]), spare
        for i in movable:
            extra = min(reach - counts[i], max(1, left * portions[i] // pool), spare)
            counts[i] = counts[i] + extra
            spare = spare - extra
    return np.array([reach] + counts)


def uneven(stream_key, amount, total, limit, skew):
    if amount == 2:
        one = jax.random.randint(stream_key, (), max(1, total - limit), min(limit, total - 1) + 1)
        return jnp.stack([one, total - one])
    tallies = jnp.asarray(profile(amount, total, limit, skew), jnp.int32)
    couples = (amount - 1) // 2
    giver, taker = tallies[1:1 + 2 * couples:2], tallies[2:2 + 2 * couples:2]
    slack = jnp.minimum(giver - 1, limit - taker)
    moved = jax.random.randint(jax.random.fold_in(stream_key, 1), (couples,), 0, 1 << 20) % (slack + 1)
    tallies = tallies.at[1:1 + 2 * couples:2].set(giver - moved).at[2:2 + 2 * couples:2].set(taker + moved)
    return tallies[jax.random.permutation(jax.random.fold_in(stream_key, 2), amount)]


def scatter_about(own_key, shape, spread, most, split=(), kind=jnp.bfloat16):
    result = spread * jax.random.normal(own_key, shape, jnp.float32)
    if split:
        result = result * block_levels(own_key, shape, split, -0.22, 0.18)
    return jnp.clip(result, -most, most).astype(kind)


def setup_inputs(seed: int = 0) -> dict:
    streams_of = jax.random.split(jax.random.key(seed), 12)
    tokens = scatter_about(streams_of[0], (TOKENS, D), 1.0, 6.0, ((0, 32),))
    doc_lengths = jax.vmap(lambda own: uneven(own, DOCS, SEQ_LEN, SEQ_LEN - SPAN + 1, 0))(jax.random.split(streams_of[1], SEQS)).reshape((SEQS, DOCS)).astype(jnp.int32)
    w_query = scatter_about(streams_of[2], (D, HEADS * HEAD_DIM), (D // 2) ** -0.5, 0.15625, ((0, 16), (1, 2)))
    w_key = scatter_about(streams_of[3], (D, KV_HEADS * HEAD_DIM), (D // 2) ** -0.5, 0.15625, ((0, 16), (1, 2)))
    w_value = scatter_about(streams_of[4], (D, KV_HEADS * HEAD_DIM), D ** -0.5, 0.125, ((0, 16), (1, 2)))
    w_out = scatter_about(streams_of[5], (HEADS * HEAD_DIM, D), (HEADS * HEAD_DIM // 64) ** -0.5, 1.0, ((0, 2), (1, 16)))
    w_gate = scatter_about(streams_of[6], (D, FF), D ** -0.5, 0.125, ((0, 16), (1, 2)))
    w_up = scatter_about(streams_of[7], (D, FF), D ** -0.5, 0.125, ((0, 16), (1, 2)))
    w_down = scatter_about(streams_of[8], (FF, D), FF ** -0.5, 0.078125, ((0, 2), (1, 16)))
    norm_gains = jnp.clip(1.0 + 0.1 * jax.random.normal(streams_of[9], (2, D), jnp.float32), 0.5, 1.5).astype(jnp.bfloat16)
    cotangent = scatter_about(streams_of[10], (TOKENS, D), 1.0, 6.0, ((0, 32),))
    return {"tokens": tokens, "doc_lengths": doc_lengths, "w_query": w_query, "w_key": w_key, "w_value": w_value, "w_out": w_out, "w_gate": w_gate, "w_up": w_up, "w_down": w_down, "norm_gains": norm_gains, "cotangent": cotangent}


@jax.custom_vjp
def low(v):
    return lax.optimization_barrier(v.astype(jnp.bfloat16)).astype(jnp.float32)

@jax.custom_vjp
def low_back(v):
    return v

def low_keep(v):
    return (low(v), None)

def low_pass(kept, grad):
    return (grad,)

def back_keep(v):
    return (v, None)

def back_low(kept, grad):
    return (low(grad),)
low.defvjp(low_keep, low_pass)
low_back.defvjp(back_keep, back_low)
norm_eps = 1e-05
rope_base = 10000.0
mask_fill = -1000000000.0
highest = lax.Precision.HIGHEST

def matmul(left, right):
    return jnp.dot(left, right, precision=highest, preferred_element_type=jnp.float32)

def rope_tables(positions):
    half_dim = HEAD_DIM // 2
    freq_row = rope_base ** (-jnp.arange(half_dim, dtype=jnp.float32) * 2.0 / HEAD_DIM)
    angles = positions.astype(jnp.float32)[:, None] * freq_row[None, :]
    return (jnp.cos(angles), jnp.sin(angles))

def rotate(values, cos_tab, sin_tab):
    half_dim = HEAD_DIM // 2
    first_half = values[..., :half_dim]
    second_half = values[..., half_dim:]
    cos_wide = cos_tab[:, None, :]
    sin_wide = sin_tab[:, None, :]
    return jnp.concatenate([first_half * cos_wide - second_half * sin_wide, second_half * cos_wide + first_half * sin_wide], axis=-1)

def document_ids(lengths, positions):
    doc_ends = jnp.cumsum(lengths).astype(jnp.int32)
    return lax.optimization_barrier(jnp.sum((positions[:, None] >= doc_ends[None, :DOCS - 1]).astype(jnp.int32), axis=1)).astype(jnp.int32)

def rms_scale(row_values):
    return lax.rsqrt(lax.optimization_barrier(jnp.mean(row_values * row_values, axis=-1, keepdims=True)) + norm_eps)

def block_layer(inputs, lengths, w_query, w_key, w_value, w_out, w_gate, w_up, w_down, norm_gains):
    length = inputs.shape[0]
    score_scale = 1.0 / math.sqrt(HEAD_DIM)
    normed_one = low(inputs * rms_scale(inputs) * norm_gains[0])
    positions = jnp.arange(length, dtype=jnp.int32)
    cos_tab, sin_tab = rope_tables(positions)
    queries = low(rotate(low_back(matmul(normed_one, w_query)).reshape(length, HEADS, HEAD_DIM), cos_tab, sin_tab))
    keys_rot = low(rotate(low_back(matmul(normed_one, w_key)).reshape(length, KV_HEADS, HEAD_DIM), cos_tab, sin_tab))
    values_low = low(low_back(matmul(normed_one, w_value))).reshape(length, KV_HEADS, HEAD_DIM)
    doc_ids = document_ids(lengths, positions)
    key_blocks = positions // BLOCK
    query_rows = min(512, length)

    def attend(start_row):
        query_part = lax.dynamic_slice_in_dim(queries, start_row, query_rows, 0).reshape(query_rows, KV_HEADS, GROUP, HEAD_DIM)
        scores = jnp.einsum('ckgd,nkd->kgcn', query_part, keys_rot, precision=highest) * score_scale
        scores = low_back(scores)
        query_pos = start_row + jnp.arange(query_rows, dtype=jnp.int32)
        query_doc = lax.dynamic_slice_in_dim(doc_ids, start_row, query_rows, 0)
        allowed = (key_blocks[None, :] <= (query_pos // BLOCK)[:, None]) & (doc_ids[None, :] == query_doc[:, None])
        scores = jnp.where(allowed[None, None], scores, mask_fill)
        row_max = lax.optimization_barrier(jnp.max(scores, axis=-1, keepdims=True))
        exp_scores = jnp.exp(scores - row_max)
        attn_prob = low(exp_scores / lax.optimization_barrier(jnp.sum(exp_scores, axis=-1, keepdims=True)))
        mixed_heads = jnp.einsum('kgcn,nkd->ckgd', attn_prob, values_low, precision=highest)
        return mixed_heads.reshape(query_rows, HEADS * HEAD_DIM)
    starts = (jnp.arange(length // query_rows, dtype=jnp.int32) * query_rows).astype(jnp.int32)
    attended = lax.map(jax.checkpoint(attend), starts).reshape(length, HEADS * HEAD_DIM)
    attended = low(low_back(attended))
    residual = inputs + low_back(matmul(attended, w_out))
    normed_two = low(residual * rms_scale(residual) * norm_gains[1])
    gate_pre = low_back(matmul(normed_two, w_gate))
    up_pre = low_back(matmul(normed_two, w_up))
    hidden = low(jax.nn.silu(gate_pre) * up_pre)
    return residual + low_back(matmul(hidden, w_down))

def reference(tokens, doc_lengths, w_query, w_key, w_value, w_out, w_gate, w_up, w_down, norm_gains, cotangent):
    weight_list = tuple((weight.astype(jnp.float32) for weight in (w_query, w_key, w_value, w_out, w_gate, w_up, w_down, norm_gains)))
    inputs = tokens.astype(jnp.float32).reshape(SEQS, SEQ_LEN, D)

    def forward(inputs, *weights):

        def one_sequence(seq_pair):
            return block_layer(seq_pair[0], seq_pair[1], *weights)
        return lax.map(jax.checkpoint(one_sequence), (inputs, doc_lengths))
    outputs, pullback = jax.vjp(forward, inputs, *weight_list)
    gradients = pullback(cotangent.astype(jnp.float32).reshape(SEQS, SEQ_LEN, D))
    return (outputs.reshape(TOKENS, D).astype(jnp.bfloat16), gradients[0].reshape(TOKENS, D), gradients[1], gradients[2], gradients[3], gradients[4], gradients[5], gradients[6], gradients[7], gradients[8])
```

```python
import math

import jax
import jax.numpy as jnp
from jax import lax
from jax.sharding import PartitionSpec as P

D = 2560
HEAD_DIM = 80
BLOCK = 256
DOCS = 3
GROUP = 4


norm_eps = 1e-05
rope_base = 10000.0
mask_fill = -1000000000.0


def rope_tables(positions):
    half_dim = HEAD_DIM // 2
    freq_row = rope_base ** (-jnp.arange(half_dim, dtype=jnp.float32) * 2.0 / HEAD_DIM)
    angles = positions.astype(jnp.float32)[:, None] * freq_row[None, :]
    return (jnp.cos(angles), jnp.sin(angles))


def rotate(values, cos_tab, sin_tab):
    half_dim = HEAD_DIM // 2
    first_half = values[..., :half_dim]
    second_half = values[..., half_dim:]
    cos_wide = cos_tab[:, None, :]
    sin_wide = sin_tab[:, None, :]
    return jnp.concatenate(
        [
            first_half * cos_wide - second_half * sin_wide,
            second_half * cos_wide + first_half * sin_wide,
        ],
        axis=-1,
    )


def document_ids(lengths, positions):
    doc_ends = jnp.cumsum(lengths)
    return jnp.sum((positions[:, None] >= doc_ends[None, : DOCS - 1]).astype(jnp.int32), axis=1)


def rms_scale(row_values):
    return lax.rsqrt(jnp.mean(row_values * row_values, axis=-1, keepdims=True) + norm_eps)


def per_device(
    tokens, doc_lengths, w_query, w_key, w_value, w_out, w_gate, w_up, w_down, norm_gains, cotangent
):
    tp_count = lax.axis_size("tp")
    seq_count = lax.axis_size("seq")
    tp_index = lax.axis_index("tp")
    seq_index = lax.axis_index("seq")
    local_rows = tokens.shape[0]
    span_len = local_rows * tp_count
    seq_length = span_len * seq_count
    score_scale = 1.0 / math.sqrt(HEAD_DIM)
    key_step = math.gcd(512, seq_length)
    gathered = (
        lax.all_gather(w_query, ("fsdp", "seq"), axis=0, tiled=True),
        lax.all_gather(w_key, ("fsdp", "seq"), axis=0, tiled=True),
        lax.all_gather(w_value, ("fsdp", "seq"), axis=0, tiled=True),
        lax.all_gather(w_out, ("fsdp", "seq"), axis=1, tiled=True),
        lax.all_gather(w_gate, ("fsdp", "seq"), axis=0, tiled=True),
        lax.all_gather(w_up, ("fsdp", "seq"), axis=0, tiled=True),
        lax.all_gather(w_down, ("fsdp", "seq"), axis=1, tiled=True),
        lax.all_gather(norm_gains, ("fsdp", "seq"), axis=1, tiled=True),
    )
    query_full, key_full, value_full, out_full, gate_full, up_full, down_full, gains_low = gathered
    gain_one = gains_low[0].astype(jnp.float32)
    gain_two = gains_low[1].astype(jnp.float32)
    query_heads = query_full.shape[1] // HEAD_DIM
    kv_local = key_full.shape[1] // HEAD_DIM
    span_in = lax.all_gather(tokens, "tp", axis=0, tiled=True)
    span_float = span_in.astype(jnp.float32)
    inv_one = rms_scale(span_float)
    normed_one = (span_float * inv_one * gain_one).astype(jnp.bfloat16)
    span_start = seq_index * span_len
    positions = span_start + jnp.arange(span_len, dtype=jnp.int32)
    cos_tab, sin_tab = rope_tables(positions)
    query_raw = jnp.dot(normed_one, query_full, preferred_element_type=jnp.float32).reshape(
        span_len, query_heads, HEAD_DIM
    )
    key_raw = jnp.dot(normed_one, key_full, preferred_element_type=jnp.float32).reshape(
        span_len, kv_local, HEAD_DIM
    )
    value_raw = jnp.dot(normed_one, value_full, preferred_element_type=jnp.float32).reshape(
        span_len, kv_local, HEAD_DIM
    )
    query_rot = rotate(query_raw, cos_tab, sin_tab).astype(jnp.bfloat16)
    key_rot = rotate(key_raw, cos_tab, sin_tab).astype(jnp.bfloat16)
    value_low = value_raw.astype(jnp.bfloat16)
    query_group = query_rot.reshape(span_len, kv_local, GROUP, HEAD_DIM)
    key_all, value_all = (
        lax.all_gather(key_rot, "seq", axis=0, tiled=True),
        lax.all_gather(value_low, "seq", axis=0, tiled=True),
    )
    key_positions = jnp.arange(seq_length, dtype=jnp.int32)
    doc_keys = document_ids(doc_lengths[0], key_positions)
    doc_query = lax.dynamic_slice_in_dim(doc_keys, span_start, span_len, 0)
    key_blocks = key_positions // BLOCK
    query_block = positions // BLOCK
    blocks_used = (span_start + span_len + key_step - 1) // key_step
    stat_shape = (kv_local, GROUP, span_len)
    head_shape = (span_len, kv_local, GROUP, HEAD_DIM)

    def masked_scores(block_index):
        key_start = block_index * key_step
        key_part = lax.dynamic_slice_in_dim(key_all, key_start, key_step, 0)
        scores = (
            jnp.einsum("ckgd,nkd->kgcn", query_group, key_part, preferred_element_type=jnp.float32)
            * score_scale
        )
        block_part = lax.dynamic_slice_in_dim(key_blocks, key_start, key_step, 0)
        doc_part = lax.dynamic_slice_in_dim(doc_keys, key_start, key_step, 0)
        allowed = (block_part[None, :] <= query_block[:, None]) & (
            doc_part[None, :] == doc_query[:, None]
        )
        return (jnp.where(allowed[None, None], scores, mask_fill), key_start, key_part)

    def total_step(block_index, carry):
        row_max, row_sum = carry
        scores = masked_scores(block_index)[0]
        new_max = jnp.maximum(row_max, jnp.max(scores, axis=-1))
        row_sum = row_sum * jnp.exp(row_max - new_max) + jnp.sum(
            jnp.exp(scores - new_max[..., None]), axis=-1
        )
        return (new_max, row_sum)

    row_max, row_sum = lax.fori_loop(
        0,
        blocks_used,
        total_step,
        (jnp.full(stat_shape, mask_fill, jnp.float32), jnp.zeros(stat_shape, jnp.float32)),
    )
    log_total = row_max + jnp.log(row_sum)

    def out_step(block_index, running):
        scores, key_start, key_part = masked_scores(block_index)
        attn_prob = jnp.exp(scores - log_total[..., None]).astype(jnp.bfloat16)
        value_part = lax.dynamic_slice_in_dim(value_all, key_start, key_step, 0)
        return running + jnp.einsum(
            "kgcn,nkd->ckgd", attn_prob, value_part, preferred_element_type=jnp.float32
        )

    attended = lax.fori_loop(0, blocks_used, out_step, jnp.zeros(head_shape, jnp.float32))
    attended_low = attended.reshape(span_len, query_heads * HEAD_DIM).astype(jnp.bfloat16)
    attn_branch = lax.psum_scatter(
        jnp.dot(attended_low, out_full, preferred_element_type=jnp.float32).astype(jnp.bfloat16),
        "tp",
        scatter_dimension=0,
        tiled=True,
    ).astype(jnp.float32)
    token_rows = tokens.astype(jnp.float32)
    residual = token_rows + attn_branch
    inv_two = rms_scale(residual)
    normed_two = (residual * inv_two * gain_two).astype(jnp.bfloat16)
    span_two = lax.all_gather(normed_two, "tp", axis=0, tiled=True)
    gate_pre = jnp.dot(span_two, gate_full, preferred_element_type=jnp.float32)
    up_pre = jnp.dot(span_two, up_full, preferred_element_type=jnp.float32)
    sig_gate = jax.nn.sigmoid(gate_pre)
    silu_gate = gate_pre * sig_gate
    hidden_low = (silu_gate * up_pre).astype(jnp.bfloat16)
    mlp_branch = lax.psum_scatter(
        jnp.dot(hidden_low, down_full, preferred_element_type=jnp.float32).astype(jnp.bfloat16),
        "tp",
        scatter_dimension=0,
        tiled=True,
    ).astype(jnp.float32)
    mixed_out = (residual + mlp_branch).astype(jnp.bfloat16)
    cot_span = lax.all_gather(cotangent, "tp", axis=0, tiled=True)
    grad_down_w = jnp.einsum("cf,cd->fd", hidden_low, cot_span, preferred_element_type=jnp.float32)
    grad_hidden = jnp.einsum("cd,fd->cf", cot_span, down_full, preferred_element_type=jnp.float32)
    grad_gate_pre = (
        grad_hidden * up_pre * (sig_gate * (1.0 + gate_pre * (1.0 - sig_gate)))
    ).astype(jnp.bfloat16)
    grad_up_pre = (grad_hidden * silu_gate).astype(jnp.bfloat16)
    grad_gate_w = jnp.einsum(
        "cd,cf->df", span_two, grad_gate_pre, preferred_element_type=jnp.float32
    )
    grad_up_w = jnp.einsum("cd,cf->df", span_two, grad_up_pre, preferred_element_type=jnp.float32)
    grad_normed_two = lax.psum_scatter(
        (
            jnp.einsum("cf,df->cd", grad_gate_pre, gate_full, preferred_element_type=jnp.float32)
            + jnp.einsum("cf,df->cd", grad_up_pre, up_full, preferred_element_type=jnp.float32)
        ).astype(jnp.bfloat16),
        "tp",
        scatter_dimension=0,
        tiled=True,
    ).astype(jnp.float32)
    gain_two_term = jnp.sum(grad_normed_two * residual * inv_two, axis=0)
    scaled_two = grad_normed_two * gain_two
    grad_residual = (
        cotangent.astype(jnp.float32)
        + inv_two * scaled_two
        - residual
        * (inv_two * inv_two * inv_two)
        * jnp.mean(scaled_two * residual, axis=-1, keepdims=True)
    )
    grad_span = lax.all_gather(grad_residual.astype(jnp.bfloat16), "tp", axis=0, tiled=True)
    grad_out_w = jnp.einsum(
        "ce,cd->ed", attended_low, grad_span, preferred_element_type=jnp.float32
    )
    grad_attended = (
        jnp.einsum("cd,ed->ce", grad_span, out_full, preferred_element_type=jnp.float32)
        .astype(jnp.bfloat16)
        .reshape(head_shape)
    )

    def prob_grads(block_index):
        scores, key_start, key_part = masked_scores(block_index)
        probs_full = jnp.exp(scores - log_total[..., None])
        value_part = lax.dynamic_slice_in_dim(value_all, key_start, key_step, 0)
        grad_prob = jnp.einsum(
            "ckgd,nkd->kgcn", grad_attended, value_part, preferred_element_type=jnp.float32
        )
        return (probs_full, grad_prob, key_start, key_part)

    def delta_step(block_index, running):
        grads_here = prob_grads(block_index)
        return running + jnp.sum(grads_here[0] * grads_here[1], axis=-1)

    row_delta = lax.fori_loop(0, blocks_used, delta_step, jnp.zeros(stat_shape, jnp.float32))

    def grad_step(block_index, carry):
        query_acc, key_acc, value_acc = carry
        probs_full, grad_prob, key_start, key_part = prob_grads(block_index)
        grad_scores = (probs_full * (grad_prob - row_delta[..., None])).astype(jnp.bfloat16)
        query_acc = query_acc + jnp.einsum(
            "kgcn,nkd->ckgd", grad_scores, key_part, preferred_element_type=jnp.float32
        )
        key_term = (
            jnp.einsum(
                "kgcn,ckgd->nkd", grad_scores, query_group, preferred_element_type=jnp.float32
            )
            * score_scale
        )
        value_term = jnp.einsum(
            "kgcn,ckgd->nkd",
            probs_full.astype(jnp.bfloat16),
            grad_attended,
            preferred_element_type=jnp.float32,
        )
        key_old = lax.dynamic_slice_in_dim(key_acc, key_start, key_step, 0)
        value_old = lax.dynamic_slice_in_dim(value_acc, key_start, key_step, 0)
        key_acc = lax.dynamic_update_slice_in_dim(key_acc, key_old + key_term, key_start, 0)
        value_acc = lax.dynamic_update_slice_in_dim(value_acc, value_old + value_term, key_start, 0)
        return (query_acc, key_acc, value_acc)

    kv_zeros = jnp.zeros((seq_length, kv_local, HEAD_DIM), jnp.float32)
    query_acc, key_acc, value_acc = lax.fori_loop(
        0, blocks_used, grad_step, (jnp.zeros(head_shape, jnp.float32), kv_zeros, kv_zeros)
    )
    key_own, value_own = (
        lax.psum_scatter(
            key_acc.astype(jnp.bfloat16), "seq", scatter_dimension=0, tiled=True
        ).astype(jnp.float32),
        lax.psum_scatter(
            value_acc.astype(jnp.bfloat16), "seq", scatter_dimension=0, tiled=True
        ).astype(jnp.float32),
    )
    grad_query_rot = (query_acc * score_scale).reshape(span_len, query_heads, HEAD_DIM)
    grad_query_raw = (
        rotate(grad_query_rot, cos_tab, -sin_tab)
        .reshape(span_len, query_heads * HEAD_DIM)
        .astype(jnp.bfloat16)
    )
    grad_key_raw = (
        rotate(key_own, cos_tab, -sin_tab)
        .reshape(span_len, kv_local * HEAD_DIM)
        .astype(jnp.bfloat16)
    )
    grad_value_raw = value_own.reshape(span_len, kv_local * HEAD_DIM).astype(jnp.bfloat16)
    grad_query_w = jnp.einsum(
        "cd,ce->de", normed_one, grad_query_raw, preferred_element_type=jnp.float32
    )
    grad_key_w = jnp.einsum(
        "cd,ce->de", normed_one, grad_key_raw, preferred_element_type=jnp.float32
    )
    grad_value_w = jnp.einsum(
        "cd,ce->de", normed_one, grad_value_raw, preferred_element_type=jnp.float32
    )
    normed_part = jnp.einsum(
        "ce,de->cd", grad_query_raw, query_full, preferred_element_type=jnp.float32
    )
    normed_part = normed_part + jnp.einsum(
        "ce,de->cd", grad_key_raw, key_full, preferred_element_type=jnp.float32
    )
    normed_part = normed_part + jnp.einsum(
        "ce,de->cd", grad_value_raw, value_full, preferred_element_type=jnp.float32
    )
    gain_one_term = jnp.sum(normed_part * span_float * inv_one, axis=0)
    gain_block = jnp.broadcast_to(jnp.stack([gain_one_term, gain_two_term])[None], (tp_count, 2, D))
    grad_normed_one, gains_summed = (
        lax.psum_scatter(
            normed_part.astype(jnp.bfloat16), "tp", scatter_dimension=0, tiled=True
        ).astype(jnp.float32),
        lax.psum_scatter(
            gain_block.astype(jnp.bfloat16), "tp", scatter_dimension=0, tiled=True
        ).astype(jnp.float32),
    )
    gains_total = gains_summed[0]
    inv_rows = lax.dynamic_slice_in_dim(inv_one, tp_index * local_rows, local_rows, 0)
    scaled_one = grad_normed_one * gain_one
    grad_tokens = (
        grad_residual
        + inv_rows * scaled_one
        - token_rows
        * (inv_rows * inv_rows * inv_rows)
        * jnp.mean(scaled_one * token_rows, axis=-1, keepdims=True)
    )
    summed = (
        lax.psum_scatter(
            grad_query_w.astype(jnp.bfloat16), ("fsdp", "seq"), scatter_dimension=0, tiled=True
        ).astype(jnp.float32),
        lax.psum_scatter(
            grad_key_w.astype(jnp.bfloat16), ("fsdp", "seq"), scatter_dimension=0, tiled=True
        ).astype(jnp.float32),
        lax.psum_scatter(
            grad_value_w.astype(jnp.bfloat16), ("fsdp", "seq"), scatter_dimension=0, tiled=True
        ).astype(jnp.float32),
        lax.psum_scatter(
            grad_out_w.astype(jnp.bfloat16), ("fsdp", "seq"), scatter_dimension=1, tiled=True
        ).astype(jnp.float32),
        lax.psum_scatter(
            grad_gate_w.astype(jnp.bfloat16), ("fsdp", "seq"), scatter_dimension=0, tiled=True
        ).astype(jnp.float32),
        lax.psum_scatter(
            grad_up_w.astype(jnp.bfloat16), ("fsdp", "seq"), scatter_dimension=0, tiled=True
        ).astype(jnp.float32),
        lax.psum_scatter(
            grad_down_w.astype(jnp.bfloat16), ("fsdp", "seq"), scatter_dimension=1, tiled=True
        ).astype(jnp.float32),
        lax.psum_scatter(
            gains_total.astype(jnp.bfloat16), ("fsdp", "seq"), scatter_dimension=1, tiled=True
        ).astype(jnp.float32),
    )
    return (
        mixed_out,
        grad_tokens,
        summed[0],
        summed[1],
        summed[2],
        summed[3],
        summed[4],
        summed[5],
        summed[6],
        summed[7],
    )


def to_core(value):
    return lax.ppermute(value, "fsdp", [(i, i ^ 1) for i in range(4)])


def to_x(value):
    return lax.ppermute(value, "fsdp", [(i, i ^ 2) for i in range(4)])


def to_near(value):
    return lax.ppermute(value, "seq", [(i, i ^ 1) for i in range(4)])


def to_far(value):
    return lax.ppermute(value, "seq", [(i, i ^ 2) for i in range(4)])


def to_tp(value):
    return lax.ppermute(value, "tp", [(0, 1), (1, 0)])


def float_of(value):
    return value.astype(jnp.float32)


def low_of(value):
    return value.astype(jnp.bfloat16)


def rows_dot(left, right):
    return lax.dot_general(left, right, (((0,), (0,)), ((), ())), preferred_element_type=jnp.float32)


def cols_dot(left, right):
    return lax.dot_general(left, right, (((1,), (1,)), ((), ())), preferred_element_type=jnp.float32)


def wide_dot(left, pieces):
    depth = pieces[0].shape[0]
    return sum(
        jnp.dot(left[:, i * depth : (i + 1) * depth], piece, preferred_element_type=jnp.float32)
        for i, piece in enumerate(pieces)
    )


def half_plan(
    tokens, doc_lengths, w_query, w_key, w_value, w_out, w_gate, w_up, w_down, norm_gains, cotangent
):
    fsdp_index = lax.axis_index("fsdp")
    seq_index = lax.axis_index("seq")
    tp_index = lax.axis_index("tp")
    near = seq_index % 2
    far = seq_index // 2
    local_rows = tokens.shape[0]
    group_rows = 4 * local_rows
    quarter = D // 4
    block_rows = D // 16
    score_scale = 1.0 / math.sqrt(HEAD_DIM)
    order = (0, 2, 1, 3)

    def columns_in(value):
        return jnp.concatenate(
            [
                lax.dynamic_slice_in_dim(value, (fsdp_index ^ k) * quarter, quarter, 1)
                for k in order
            ],
            axis=1,
        )

    def columns_out(value):
        pieces = []
        for block in range(4):
            k = fsdp_index ^ block
            place = (k // 2) + (k % 2) * 2
            pieces.append(lax.dynamic_slice_in_dim(value, place * quarter, quarter, 1))
        return jnp.concatenate(pieces, axis=1)

    def both_halves(array, axis):
        size = array.shape[axis] // 2
        low_part = lax.slice_in_dim(array, 0, size, axis=axis)
        high_part = lax.slice_in_dim(array, size, 2 * size, axis=axis)
        first = near == 0
        return jnp.where(first, low_part, high_part), jnp.where(first, high_part, low_part)

    def spread(own, other):
        received = to_near(other)
        first = near == 0
        pair = jnp.concatenate(
            [jnp.where(first, own, received), jnp.where(first, received, own)], axis=0
        )
        pair_far = to_far(pair)
        left = far == 0
        plane = jnp.concatenate(
            [jnp.where(left, pair, pair_far), jnp.where(left, pair_far, pair)], axis=0
        )
        mine = jnp.concatenate([plane, to_x(plane)], axis=0)
        return mine, to_core(mine)

    def collect(grad_mine, grad_other):
        from_core = to_core(grad_other)
        send_x = low_of(float_of(grad_mine[quarter:]) + float_of(from_core[quarter:]))
        from_x = to_x(send_x)
        plane = low_of(
            float_of(grad_mine[:quarter]) + float_of(from_core[:quarter]) + float_of(from_x)
        )
        size = 2 * block_rows
        from_far = to_far(lax.dynamic_slice_in_dim(plane, (1 - far) * size, size, 0))
        pair = lax.dynamic_slice_in_dim(plane, far * size, size, 0)
        pair = low_of(float_of(pair) + float_of(from_far))
        received = to_near(lax.dynamic_slice_in_dim(pair, (1 - near) * block_rows, block_rows, 0))
        own = lax.dynamic_slice_in_dim(pair, near * block_rows, block_rows, 0)
        return own, received

    def joined(own, received):
        first = near == 0
        return float_of(
            jnp.concatenate(
                [jnp.where(first, own, received), jnp.where(first, received, own)], axis=1
            )
        )

    def gather_rows(value):
        half = value.shape[1] // 2
        one, two = value[:, :half], value[:, half:]
        one = jnp.concatenate([one, to_near(one)], axis=0)
        two = jnp.concatenate([two, to_tp(two)], axis=0)
        one_far = to_tp(one)
        two_far = to_near(two)
        one = jnp.concatenate(
            [one[:local_rows], one_far[:local_rows], one[local_rows:], one_far[local_rows:]], axis=0
        )
        two = jnp.concatenate([two, two_far], axis=0)
        return jnp.concatenate([one, two], axis=1)

    def scatter_rows(one, two):
        n = local_rows
        send_one = jnp.concatenate([one[n : 2 * n], one[3 * n :]], axis=0)
        got_one = to_tp(send_one)
        got_two = to_near(two[2 * n :])
        next_one = low_of(float_of(one[2 * n : 3 * n]) + float_of(got_one[n:]))
        next_two = low_of(float_of(two[n : 2 * n]) + float_of(got_two[n:]))
        last_one = to_near(next_one)
        last_two = to_tp(next_two)
        sum_one = float_of(one[:n]) + float_of(got_one[:n]) + float_of(last_one)
        sum_two = float_of(two[:n]) + float_of(got_two[:n]) + float_of(last_two)
        return jnp.concatenate([sum_one, sum_two], axis=1)

    query_own, query_other = both_halves(w_query, 1)
    key_own, key_other = both_halves(w_key, 1)
    value_own, value_other = both_halves(w_value, 1)
    heads_weights = spread(
        jnp.concatenate([query_own, key_own, value_own], axis=1),
        jnp.concatenate([query_other, key_other, value_other], axis=1),
    )
    out_weights = spread(*both_halves(w_out.T, 1))
    gate_weights = spread(*both_halves(w_gate, 1))
    up_weights = spread(*both_halves(w_up, 1))
    down_weights = spread(*both_halves(w_down.T, 1))
    gains_low = columns_in(lax.all_gather(norm_gains, ("fsdp", "seq"), axis=1, tiled=True))
    gain_one = float_of(gains_low[0])
    gain_two = float_of(gains_low[1])

    tokens_in = columns_in(tokens)
    cot_in = columns_in(cotangent)
    span_in = gather_rows(tokens_in)
    cot_span = gather_rows(cot_in)

    span_float = float_of(span_in)
    inv_one = rms_scale(span_float)
    normed_one = low_of(span_float * inv_one * gain_one)

    query_width = query_own.shape[1]
    key_width = key_own.shape[1]
    kv_local = key_width // HEAD_DIM
    query_heads = query_width // HEAD_DIM
    row_ids = jnp.arange(local_rows, dtype=jnp.int32)
    own_positions = jnp.concatenate(
        [
            far * (2 * 2 * local_rows)
            + (near ^ i) * (2 * local_rows)
            + (tp_index ^ j) * local_rows
            + row_ids
            for i in range(2)
            for j in range(2)
        ]
    )
    cos_tab, sin_tab = rope_tables(own_positions)
    raw = wide_dot(normed_one, heads_weights)
    query_raw = raw[:, :query_width].reshape(group_rows, query_heads, HEAD_DIM)
    key_raw = raw[:, query_width : query_width + key_width].reshape(group_rows, kv_local, HEAD_DIM)
    query_rot = low_of(rotate(query_raw, cos_tab, sin_tab)).reshape(
        group_rows, kv_local, GROUP, HEAD_DIM
    )
    key_rot = low_of(rotate(key_raw, cos_tab, sin_tab))
    value_low = low_of(raw[:, query_width + key_width :]).reshape(group_rows, kv_local, HEAD_DIM)
    own_kv = jnp.stack([key_rot, value_low])
    early_kv = lax.ppermute(own_kv, "seq", [(0, 2), (1, 3)])
    key_all = jnp.concatenate([early_kv[0], own_kv[0]], axis=0)
    value_all = jnp.concatenate([early_kv[1], own_kv[1]], axis=0)
    key_positions = jnp.concatenate([own_positions - group_rows, own_positions])
    doc_ends = jnp.cumsum(doc_lengths[0])[: DOCS - 1]

    def doc_of(positions):
        return jnp.sum((positions[:, None] >= doc_ends[None, :]).astype(jnp.int32), axis=1)

    allowed = (
        (key_positions[None, :] // BLOCK <= own_positions[:, None] // BLOCK)
        & (key_positions[None, :] >= 0)
        & (doc_of(key_positions)[None, :] == doc_of(own_positions)[:, None])
    )
    scores = (
        jnp.einsum("ckgd,nkd->kgcn", query_rot, key_all, preferred_element_type=jnp.float32)
        * score_scale
    )
    scores = jnp.where(allowed[None, None], scores, mask_fill)
    row_max = jnp.max(scores, axis=-1, keepdims=True)
    log_total = row_max + jnp.log(jnp.sum(jnp.exp(scores - row_max), axis=-1, keepdims=True))
    probs_full = jnp.exp(scores - log_total)
    attn_prob = low_of(probs_full)
    attended = jnp.einsum(
        "kgcn,nkd->ckgd", attn_prob, value_all, preferred_element_type=jnp.float32
    )
    attended_low = low_of(attended.reshape(group_rows, query_width))
    attn_branch = scatter_rows(*[low_of(cols_dot(attended_low, w)) for w in out_weights])
    token_rows = float_of(tokens_in)
    residual = token_rows + attn_branch
    inv_two = rms_scale(residual)
    normed_two = low_of(residual * inv_two * gain_two)
    span_two = gather_rows(normed_two)
    gate_pre = wide_dot(span_two, gate_weights)
    up_pre = wide_dot(span_two, up_weights)
    sig_gate = jax.nn.sigmoid(gate_pre)
    silu_gate = gate_pre * sig_gate
    hidden_low = low_of(silu_gate * up_pre)
    grad_hidden = wide_dot(cot_span, down_weights)
    grad_gate_pre = low_of(grad_hidden * up_pre * (sig_gate * (1.0 + gate_pre * (1.0 - sig_gate))))
    grad_up_pre = low_of(grad_hidden * silu_gate)
    mlp_branch = scatter_rows(*[low_of(cols_dot(hidden_low, w)) for w in down_weights])
    mixed_out = columns_out(low_of(residual + mlp_branch))
    grad_normed_two = scatter_rows(
        *[
            low_of(cols_dot(grad_gate_pre, gate_w) + cols_dot(grad_up_pre, up_w))
            for gate_w, up_w in zip(gate_weights, up_weights)
        ]
    )
    middle = D // 2

    def weight_grad(left, right):
        return collect(
            low_of(rows_dot(left[:, :middle], right)), low_of(rows_dot(left[:, middle:], right))
        )

    down_grad = weight_grad(cot_span, hidden_low)
    gate_grad = weight_grad(span_two, grad_gate_pre)
    up_grad = weight_grad(span_two, grad_up_pre)
    gain_two_term = jnp.sum(grad_normed_two * residual * inv_two, axis=0)
    scaled_two = grad_normed_two * gain_two
    grad_residual = (
        float_of(cot_in)
        + inv_two * scaled_two
        - residual
        * (inv_two * inv_two * inv_two)
        * jnp.mean(scaled_two * residual, axis=-1, keepdims=True)
    )
    grad_span = gather_rows(low_of(grad_residual))
    out_grad = weight_grad(grad_span, attended_low)
    grad_attended = low_of(wide_dot(grad_span, out_weights)).reshape(
        group_rows, kv_local, GROUP, HEAD_DIM
    )
    grad_prob = jnp.einsum(
        "ckgd,nkd->kgcn", grad_attended, value_all, preferred_element_type=jnp.float32
    )
    row_delta = jnp.sum(probs_full * grad_prob, axis=-1, keepdims=True)
    grad_scores = low_of(probs_full * (grad_prob - row_delta))
    query_acc = jnp.einsum(
        "kgcn,nkd->ckgd", grad_scores, key_all, preferred_element_type=jnp.float32
    )
    key_acc = jnp.einsum(
        "kgcn,ckgd->nkd", grad_scores, query_rot, preferred_element_type=jnp.float32
    )
    value_acc = jnp.einsum(
        "kgcn,ckgd->nkd", attn_prob, grad_attended, preferred_element_type=jnp.float32
    )
    kv_grads = jnp.stack([key_acc * score_scale, value_acc])
    late_kv = lax.ppermute(low_of(kv_grads[:, :group_rows]), "seq", [(2, 0), (3, 1)])
    own_grads = kv_grads[:, group_rows:] + float_of(late_kv)
    grad_query_raw = low_of(
        rotate(
            (query_acc * score_scale).reshape(group_rows, query_heads, HEAD_DIM), cos_tab, -sin_tab
        )
    ).reshape(group_rows, query_width)
    grad_key_raw = low_of(rotate(own_grads[0], cos_tab, -sin_tab)).reshape(group_rows, key_width)
    grad_value_raw = low_of(own_grads[1]).reshape(group_rows, key_width)
    grad_raw = jnp.concatenate([grad_query_raw, grad_key_raw, grad_value_raw], axis=1)
    heads_grad = weight_grad(normed_one, grad_raw)
    normed_parts = [cols_dot(grad_raw, w) for w in heads_weights]
    gain_one_term = jnp.sum(
        jnp.concatenate(normed_parts, axis=1) * span_float * inv_one, axis=0
    )
    grad_normed_one = scatter_rows(*[low_of(part) for part in normed_parts])
    inv_rows = inv_one[:local_rows]
    scaled_one = grad_normed_one * gain_one
    grad_tokens = columns_out(
        grad_residual
        + inv_rows * scaled_one
        - token_rows
        * (inv_rows * inv_rows * inv_rows)
        * jnp.mean(scaled_one * token_rows, axis=-1, keepdims=True)
    )
    gain_rows = columns_out(jnp.stack([gain_one_term, gain_two_term]))
    gain_grads = lax.psum_scatter(
        lax.psum(gain_rows, "tp"), ("fsdp", "seq"), scatter_dimension=1, tiled=True
    )
    heads_own, heads_other = heads_grad
    splits = (query_width, query_width + key_width)
    grad_query, grad_key, grad_value = (
        joined(own, other)
        for own, other in zip(
            jnp.split(heads_own, splits, axis=1), jnp.split(heads_other, splits, axis=1)
        )
    )
    return (
        mixed_out,
        grad_tokens,
        grad_query,
        grad_key,
        grad_value,
        joined(*out_grad).T,
        joined(*gate_grad),
        joined(*up_grad),
        joined(*down_grad).T,
        gain_grads,
    )


def solution(mesh):
    halves = mesh.shape["seq"] == 4 and mesh.shape["tp"] == 2 and mesh.shape["fsdp"] == 4
    plan = half_plan if halves else per_device
    in_specs = (
        P(("fsdp", "seq", "tp"), None),
        P("fsdp", None),
        P(("fsdp", "seq"), "tp"),
        P(("fsdp", "seq"), "tp"),
        P(("fsdp", "seq"), "tp"),
        P("tp", ("fsdp", "seq")),
        P(("fsdp", "seq"), "tp"),
        P(("fsdp", "seq"), "tp"),
        P("tp", ("fsdp", "seq")),
        P(None, ("fsdp", "seq")),
        P(("fsdp", "seq", "tp"), None),
    )
    out_specs = (
        P(("fsdp", "seq", "tp"), None),
        P(("fsdp", "seq", "tp"), None),
        P(("fsdp", "seq"), "tp"),
        P(("fsdp", "seq"), "tp"),
        P(("fsdp", "seq"), "tp"),
        P("tp", ("fsdp", "seq")),
        P(("fsdp", "seq"), "tp"),
        P(("fsdp", "seq"), "tp"),
        P("tp", ("fsdp", "seq")),
        P(None, ("fsdp", "seq")),
    )
    return jax.shard_map(
        plan, mesh=mesh, in_specs=in_specs, out_specs=out_specs, check_vma=False
    )
```

```python
import functools
import math

import jax
import jax.numpy as jnp
from jax import lax
from jax.experimental import pallas as pl
from jax.experimental.pallas import tpu as pltpu
from jax.sharding import PartitionSpec as P

D = 2560
HEAD_DIM = 80
BLOCK = 256
DOCS = 3
GROUP = 4


norm_eps = 1e-05
rope_base = 10000.0
mask_fill = -1000000000.0


def rope_tables(positions):
    half_dim = HEAD_DIM // 2
    freq_row = rope_base ** (-jnp.arange(half_dim, dtype=jnp.float32) * 2.0 / HEAD_DIM)
    angles = positions.astype(jnp.float32)[:, None] * freq_row[None, :]
    return (jnp.cos(angles), jnp.sin(angles))


def rotate(values, cos_tab, sin_tab):
    half_dim = HEAD_DIM // 2
    first_half = values[..., :half_dim]
    second_half = values[..., half_dim:]
    cos_wide = cos_tab[:, None, :]
    sin_wide = sin_tab[:, None, :]
    return jnp.concatenate(
        [
            first_half * cos_wide - second_half * sin_wide,
            second_half * cos_wide + first_half * sin_wide,
        ],
        axis=-1,
    )


def document_ids(lengths, positions):
    doc_ends = jnp.cumsum(lengths)
    return jnp.sum((positions[:, None] >= doc_ends[None, : DOCS - 1]).astype(jnp.int32), axis=1)


def rms_scale(row_values):
    return lax.rsqrt(jnp.mean(row_values * row_values, axis=-1, keepdims=True) + norm_eps)


def per_device(
    tokens, doc_lengths, w_query, w_key, w_value, w_out, w_gate, w_up, w_down, norm_gains, cotangent
):
    tp_count = lax.axis_size("tp")
    seq_count = lax.axis_size("seq")
    tp_index = lax.axis_index("tp")
    seq_index = lax.axis_index("seq")
    local_rows = tokens.shape[0]
    span_len = local_rows * tp_count
    seq_length = span_len * seq_count
    score_scale = 1.0 / math.sqrt(HEAD_DIM)
    key_step = math.gcd(512, seq_length)
    gathered = (
        lax.all_gather(w_query, ("fsdp", "seq"), axis=0, tiled=True),
        lax.all_gather(w_key, ("fsdp", "seq"), axis=0, tiled=True),
        lax.all_gather(w_value, ("fsdp", "seq"), axis=0, tiled=True),
        lax.all_gather(w_out, ("fsdp", "seq"), axis=1, tiled=True),
        lax.all_gather(w_gate, ("fsdp", "seq"), axis=0, tiled=True),
        lax.all_gather(w_up, ("fsdp", "seq"), axis=0, tiled=True),
        lax.all_gather(w_down, ("fsdp", "seq"), axis=1, tiled=True),
        lax.all_gather(norm_gains, ("fsdp", "seq"), axis=1, tiled=True),
    )
    query_full, key_full, value_full, out_full, gate_full, up_full, down_full, gains_low = gathered
    gain_one = gains_low[0].astype(jnp.float32)
    gain_two = gains_low[1].astype(jnp.float32)
    query_heads = query_full.shape[1] // HEAD_DIM
    kv_local = key_full.shape[1] // HEAD_DIM
    span_in = lax.all_gather(tokens, "tp", axis=0, tiled=True)
    span_float = span_in.astype(jnp.float32)
    inv_one = rms_scale(span_float)
    normed_one = (span_float * inv_one * gain_one).astype(jnp.bfloat16)
    span_start = seq_index * span_len
    positions = span_start + jnp.arange(span_len, dtype=jnp.int32)
    cos_tab, sin_tab = rope_tables(positions)
    query_raw = jnp.dot(normed_one, query_full, preferred_element_type=jnp.float32).reshape(
        span_len, query_heads, HEAD_DIM
    )
    key_raw = jnp.dot(normed_one, key_full, preferred_element_type=jnp.float32).reshape(
        span_len, kv_local, HEAD_DIM
    )
    value_raw = jnp.dot(normed_one, value_full, preferred_element_type=jnp.float32).reshape(
        span_len, kv_local, HEAD_DIM
    )
    query_rot = rotate(query_raw, cos_tab, sin_tab).astype(jnp.bfloat16)
    key_rot = rotate(key_raw, cos_tab, sin_tab).astype(jnp.bfloat16)
    value_low = value_raw.astype(jnp.bfloat16)
    query_group = query_rot.reshape(span_len, kv_local, GROUP, HEAD_DIM)
    key_all, value_all = (
        lax.all_gather(key_rot, "seq", axis=0, tiled=True),
        lax.all_gather(value_low, "seq", axis=0, tiled=True),
    )
    key_positions = jnp.arange(seq_length, dtype=jnp.int32)
    doc_keys = document_ids(doc_lengths[0], key_positions)
    doc_query = lax.dynamic_slice_in_dim(doc_keys, span_start, span_len, 0)
    key_blocks = key_positions // BLOCK
    query_block = positions // BLOCK
    blocks_used = (span_start + span_len + key_step - 1) // key_step
    stat_shape = (kv_local, GROUP, span_len)
    head_shape = (span_len, kv_local, GROUP, HEAD_DIM)

    def masked_scores(block_index):
        key_start = block_index * key_step
        key_part = lax.dynamic_slice_in_dim(key_all, key_start, key_step, 0)
        scores = (
            jnp.einsum("ckgd,nkd->kgcn", query_group, key_part, preferred_element_type=jnp.float32)
            * score_scale
        )
        block_part = lax.dynamic_slice_in_dim(key_blocks, key_start, key_step, 0)
        doc_part = lax.dynamic_slice_in_dim(doc_keys, key_start, key_step, 0)
        allowed = (block_part[None, :] <= query_block[:, None]) & (
            doc_part[None, :] == doc_query[:, None]
        )
        return (jnp.where(allowed[None, None], scores, mask_fill), key_start, key_part)

    def total_step(block_index, carry):
        row_max, row_sum = carry
        scores = masked_scores(block_index)[0]
        new_max = jnp.maximum(row_max, jnp.max(scores, axis=-1))
        row_sum = row_sum * jnp.exp(row_max - new_max) + jnp.sum(
            jnp.exp(scores - new_max[..., None]), axis=-1
        )
        return (new_max, row_sum)

    row_max, row_sum = lax.fori_loop(
        0,
        blocks_used,
        total_step,
        (jnp.full(stat_shape, mask_fill, jnp.float32), jnp.zeros(stat_shape, jnp.float32)),
    )
    log_total = row_max + jnp.log(row_sum)

    def out_step(block_index, running):
        scores, key_start, key_part = masked_scores(block_index)
        attn_prob = jnp.exp(scores - log_total[..., None]).astype(jnp.bfloat16)
        value_part = lax.dynamic_slice_in_dim(value_all, key_start, key_step, 0)
        return running + jnp.einsum(
            "kgcn,nkd->ckgd", attn_prob, value_part, preferred_element_type=jnp.float32
        )

    attended = lax.fori_loop(0, blocks_used, out_step, jnp.zeros(head_shape, jnp.float32))
    attended_low = attended.reshape(span_len, query_heads * HEAD_DIM).astype(jnp.bfloat16)
    attn_branch = lax.psum_scatter(
        jnp.dot(attended_low, out_full, preferred_element_type=jnp.float32).astype(jnp.bfloat16),
        "tp",
        scatter_dimension=0,
        tiled=True,
    ).astype(jnp.float32)
    token_rows = tokens.astype(jnp.float32)
    residual = token_rows + attn_branch
    inv_two = rms_scale(residual)
    normed_two = (residual * inv_two * gain_two).astype(jnp.bfloat16)
    span_two = lax.all_gather(normed_two, "tp", axis=0, tiled=True)
    gate_pre = jnp.dot(span_two, gate_full, preferred_element_type=jnp.float32)
    up_pre = jnp.dot(span_two, up_full, preferred_element_type=jnp.float32)
    sig_gate = jax.nn.sigmoid(gate_pre)
    silu_gate = gate_pre * sig_gate
    hidden_low = (silu_gate * up_pre).astype(jnp.bfloat16)
    mlp_branch = lax.psum_scatter(
        jnp.dot(hidden_low, down_full, preferred_element_type=jnp.float32).astype(jnp.bfloat16),
        "tp",
        scatter_dimension=0,
        tiled=True,
    ).astype(jnp.float32)
    mixed_out = (residual + mlp_branch).astype(jnp.bfloat16)
    cot_span = lax.all_gather(cotangent, "tp", axis=0, tiled=True)
    grad_down_w = jnp.einsum("cf,cd->fd", hidden_low, cot_span, preferred_element_type=jnp.float32)
    grad_hidden = jnp.einsum("cd,fd->cf", cot_span, down_full, preferred_element_type=jnp.float32)
    grad_gate_pre = (
        grad_hidden * up_pre * (sig_gate * (1.0 + gate_pre * (1.0 - sig_gate)))
    ).astype(jnp.bfloat16)
    grad_up_pre = (grad_hidden * silu_gate).astype(jnp.bfloat16)
    grad_gate_w = jnp.einsum(
        "cd,cf->df", span_two, grad_gate_pre, preferred_element_type=jnp.float32
    )
    grad_up_w = jnp.einsum("cd,cf->df", span_two, grad_up_pre, preferred_element_type=jnp.float32)
    grad_normed_two = lax.psum_scatter(
        (
            jnp.einsum("cf,df->cd", grad_gate_pre, gate_full, preferred_element_type=jnp.float32)
            + jnp.einsum("cf,df->cd", grad_up_pre, up_full, preferred_element_type=jnp.float32)
        ).astype(jnp.bfloat16),
        "tp",
        scatter_dimension=0,
        tiled=True,
    ).astype(jnp.float32)
    gain_two_term = jnp.sum(grad_normed_two * residual * inv_two, axis=0)
    scaled_two = grad_normed_two * gain_two
    grad_residual = (
        cotangent.astype(jnp.float32)
        + inv_two * scaled_two
        - residual
        * (inv_two * inv_two * inv_two)
        * jnp.mean(scaled_two * residual, axis=-1, keepdims=True)
    )
    grad_span = lax.all_gather(grad_residual.astype(jnp.bfloat16), "tp", axis=0, tiled=True)
    grad_out_w = jnp.einsum(
        "ce,cd->ed", attended_low, grad_span, preferred_element_type=jnp.float32
    )
    grad_attended = (
        jnp.einsum("cd,ed->ce", grad_span, out_full, preferred_element_type=jnp.float32)
        .astype(jnp.bfloat16)
        .reshape(head_shape)
    )

    def prob_grads(block_index):
        scores, key_start, key_part = masked_scores(block_index)
        probs_full = jnp.exp(scores - log_total[..., None])
        value_part = lax.dynamic_slice_in_dim(value_all, key_start, key_step, 0)
        grad_prob = jnp.einsum(
            "ckgd,nkd->kgcn", grad_attended, value_part, preferred_element_type=jnp.float32
        )
        return (probs_full, grad_prob, key_start, key_part)

    def delta_step(block_index, running):
        grads_here = prob_grads(block_index)
        return running + jnp.sum(grads_here[0] * grads_here[1], axis=-1)

    row_delta = lax.fori_loop(0, blocks_used, delta_step, jnp.zeros(stat_shape, jnp.float32))

    def grad_step(block_index, carry):
        query_acc, key_acc, value_acc = carry
        probs_full, grad_prob, key_start, key_part = prob_grads(block_index)
        grad_scores = (probs_full * (grad_prob - row_delta[..., None])).astype(jnp.bfloat16)
        query_acc = query_acc + jnp.einsum(
            "kgcn,nkd->ckgd", grad_scores, key_part, preferred_element_type=jnp.float32
        )
        key_term = (
            jnp.einsum(
                "kgcn,ckgd->nkd", grad_scores, query_group, preferred_element_type=jnp.float32
            )
            * score_scale
        )
        value_term = jnp.einsum(
            "kgcn,ckgd->nkd",
            probs_full.astype(jnp.bfloat16),
            grad_attended,
            preferred_element_type=jnp.float32,
        )
        key_old = lax.dynamic_slice_in_dim(key_acc, key_start, key_step, 0)
        value_old = lax.dynamic_slice_in_dim(value_acc, key_start, key_step, 0)
        key_acc = lax.dynamic_update_slice_in_dim(key_acc, key_old + key_term, key_start, 0)
        value_acc = lax.dynamic_update_slice_in_dim(value_acc, value_old + value_term, key_start, 0)
        return (query_acc, key_acc, value_acc)

    kv_zeros = jnp.zeros((seq_length, kv_local, HEAD_DIM), jnp.float32)
    query_acc, key_acc, value_acc = lax.fori_loop(
        0, blocks_used, grad_step, (jnp.zeros(head_shape, jnp.float32), kv_zeros, kv_zeros)
    )
    key_own, value_own = (
        lax.psum_scatter(
            key_acc.astype(jnp.bfloat16), "seq", scatter_dimension=0, tiled=True
        ).astype(jnp.float32),
        lax.psum_scatter(
            value_acc.astype(jnp.bfloat16), "seq", scatter_dimension=0, tiled=True
        ).astype(jnp.float32),
    )
    grad_query_rot = (query_acc * score_scale).reshape(span_len, query_heads, HEAD_DIM)
    grad_query_raw = (
        rotate(grad_query_rot, cos_tab, -sin_tab)
        .reshape(span_len, query_heads * HEAD_DIM)
        .astype(jnp.bfloat16)
    )
    grad_key_raw = (
        rotate(key_own, cos_tab, -sin_tab)
        .reshape(span_len, kv_local * HEAD_DIM)
        .astype(jnp.bfloat16)
    )
    grad_value_raw = value_own.reshape(span_len, kv_local * HEAD_DIM).astype(jnp.bfloat16)
    grad_query_w = jnp.einsum(
        "cd,ce->de", normed_one, grad_query_raw, preferred_element_type=jnp.float32
    )
    grad_key_w = jnp.einsum(
        "cd,ce->de", normed_one, grad_key_raw, preferred_element_type=jnp.float32
    )
    grad_value_w = jnp.einsum(
        "cd,ce->de", normed_one, grad_value_raw, preferred_element_type=jnp.float32
    )
    normed_part = jnp.einsum(
        "ce,de->cd", grad_query_raw, query_full, preferred_element_type=jnp.float32
    )
    normed_part = normed_part + jnp.einsum(
        "ce,de->cd", grad_key_raw, key_full, preferred_element_type=jnp.float32
    )
    normed_part = normed_part + jnp.einsum(
        "ce,de->cd", grad_value_raw, value_full, preferred_element_type=jnp.float32
    )
    gain_one_term = jnp.sum(normed_part * span_float * inv_one, axis=0)
    gain_block = jnp.broadcast_to(jnp.stack([gain_one_term, gain_two_term])[None], (tp_count, 2, D))
    grad_normed_one, gains_summed = (
        lax.psum_scatter(
            normed_part.astype(jnp.bfloat16), "tp", scatter_dimension=0, tiled=True
        ).astype(jnp.float32),
        lax.psum_scatter(
            gain_block.astype(jnp.bfloat16), "tp", scatter_dimension=0, tiled=True
        ).astype(jnp.float32),
    )
    gains_total = gains_summed[0]
    inv_rows = lax.dynamic_slice_in_dim(inv_one, tp_index * local_rows, local_rows, 0)
    scaled_one = grad_normed_one * gain_one
    grad_tokens = (
        grad_residual
        + inv_rows * scaled_one
        - token_rows
        * (inv_rows * inv_rows * inv_rows)
        * jnp.mean(scaled_one * token_rows, axis=-1, keepdims=True)
    )
    summed = (
        lax.psum_scatter(
            grad_query_w.astype(jnp.bfloat16), ("fsdp", "seq"), scatter_dimension=0, tiled=True
        ).astype(jnp.float32),
        lax.psum_scatter(
            grad_key_w.astype(jnp.bfloat16), ("fsdp", "seq"), scatter_dimension=0, tiled=True
        ).astype(jnp.float32),
        lax.psum_scatter(
            grad_value_w.astype(jnp.bfloat16), ("fsdp", "seq"), scatter_dimension=0, tiled=True
        ).astype(jnp.float32),
        lax.psum_scatter(
            grad_out_w.astype(jnp.bfloat16), ("fsdp", "seq"), scatter_dimension=1, tiled=True
        ).astype(jnp.float32),
        lax.psum_scatter(
            grad_gate_w.astype(jnp.bfloat16), ("fsdp", "seq"), scatter_dimension=0, tiled=True
        ).astype(jnp.float32),
        lax.psum_scatter(
            grad_up_w.astype(jnp.bfloat16), ("fsdp", "seq"), scatter_dimension=0, tiled=True
        ).astype(jnp.float32),
        lax.psum_scatter(
            grad_down_w.astype(jnp.bfloat16), ("fsdp", "seq"), scatter_dimension=1, tiled=True
        ).astype(jnp.float32),
        lax.psum_scatter(
            gains_total.astype(jnp.bfloat16), ("fsdp", "seq"), scatter_dimension=1, tiled=True
        ).astype(jnp.float32),
    )
    return (
        mixed_out,
        grad_tokens,
        summed[0],
        summed[1],
        summed[2],
        summed[3],
        summed[4],
        summed[5],
        summed[6],
        summed[7],
    )


def to_core(value):
    return lax.ppermute(value, "fsdp", [(i, i ^ 1) for i in range(4)])


def to_x(value):
    return lax.ppermute(value, "fsdp", [(i, i ^ 2) for i in range(4)])


def to_z(value, step):
    return lax.ppermute(value, "seq", [(i, i ^ step) for i in range(4)])


def to_tp(value):
    return lax.ppermute(value, "tp", [(0, 1), (1, 0)])


def hold(value, *events):
    return lax.optimization_barrier((value, events))[0]


def float_of(value):
    return value.astype(jnp.float32)


def low_of(value):
    return value.astype(jnp.bfloat16)


def rows_dot(left, right):
    return lax.dot_general(left, right, (((0,), (0,)), ((), ())), preferred_element_type=jnp.float32)


def cols_dot(left, right):
    return lax.dot_general(left, right, (((1,), (1,)), ((), ())), preferred_element_type=jnp.float32)


def wide_dot(left, pieces):
    depth = pieces[0].shape[0]
    return sum(
        jnp.dot(left[:, i * depth : (i + 1) * depth], piece, preferred_element_type=jnp.float32)
        for i, piece in enumerate(pieces)
    )


def place_kernel(rows, place, one, two, three, four, plane, mine, held, read_sems, sems):
    reads = [
        pltpu.make_async_copy(piece, held.at[k], read_sems.at[k])
        for k, piece in enumerate((one, two, three, four))
    ]
    for copy in reads:
        copy.start()
    writes = []
    for k, read in enumerate(reads):
        read.wait()
        start = pl.multiple_of((place[0] ^ k) * rows, 16)
        for i, target in enumerate((plane, mine)):
            write = pltpu.make_async_copy(
                held.at[k], target.at[pl.ds(start, rows), :], sems.at[2 * k + i]
            )
            write.start()
            writes.append(write)
    for write in writes:
        write.wait()


def place_rows(pieces, place):
    rows, columns = pieces[0].shape
    anywhere = pl.BlockSpec(memory_space=pl.ANY)
    return pl.pallas_call(
        lambda *refs: place_kernel(rows, *refs),
        out_shape=(
            jax.ShapeDtypeStruct((4 * rows, columns), jnp.bfloat16),
            jax.ShapeDtypeStruct((8 * rows, columns), jnp.bfloat16),
        ),
        in_specs=[pl.BlockSpec(memory_space=pltpu.SMEM)] + [anywhere] * 4,
        out_specs=(anywhere, anywhere),
        scratch_shapes=[
            pltpu.VMEM((4, rows, columns), jnp.bfloat16),
            pltpu.SemaphoreType.DMA((4,)),
            pltpu.SemaphoreType.DMA((8,)),
        ],
        cost_estimate=pl.CostEstimate(
            flops=0, bytes_accessed=24 * rows * columns, transcendentals=0
        ),
        name="place_rows",
    )(place.reshape(1), *pieces)


def fill_kernel(rows, across, first, mine, held, read_sems, sems):
    part = rows // 4
    reads = [
        pltpu.make_async_copy(across.at[pl.ds(k * part, part), :], held.at[k], read_sems.at[k])
        for k in range(4)
    ]
    for copy in reads:
        copy.start()
    writes = []
    for k, read in enumerate(reads):
        read.wait()
        write = pltpu.make_async_copy(
            held.at[k], mine.at[pl.ds(rows + k * part, part), :], sems.at[k]
        )
        write.start()
        writes.append(write)
    for write in writes:
        write.wait()


def fill_rows(mine, across):
    rows, columns = across.shape
    anywhere = pl.BlockSpec(memory_space=pl.ANY)
    return pl.pallas_call(
        lambda *refs: fill_kernel(rows, *refs),
        out_shape=jax.ShapeDtypeStruct(mine.shape, mine.dtype),
        in_specs=[anywhere] * 2,
        out_specs=anywhere,
        scratch_shapes=[
            pltpu.VMEM((4, rows // 4, columns), jnp.bfloat16),
            pltpu.SemaphoreType.DMA((4,)),
            pltpu.SemaphoreType.DMA((4,)),
        ],
        input_output_aliases={1: 0},
        cost_estimate=pl.CostEstimate(flops=0, bytes_accessed=4 * rows * columns, transcendentals=0),
        name="fill_rows",
    )(across, mine)


VMEM_BYTES = 40 * 1024 * 1024


def take_rows_kernel(own, one_near, one_far, two_tp, two_far, out, sems):
    n = own.shape[0]
    half = own.shape[1] // 2
    left, right = pl.ds(0, half), pl.ds(half, half)
    moves = [
        (own, pl.ds(0, n), pl.ds(0, 2 * half)),
        (one_near, pl.ds(2 * n, n), left),
        (one_far.at[pl.ds(0, n), :], pl.ds(n, n), left),
        (one_far.at[pl.ds(n, n), :], pl.ds(3 * n, n), left),
        (two_tp, pl.ds(n, n), right),
        (two_far, pl.ds(2 * n, 2 * n), right),
    ]
    copies = [
        pltpu.make_async_copy(source, out.at[rows, columns], sems.at[k])
        for k, (source, rows, columns) in enumerate(moves)
    ]
    for copy in copies:
        copy.start()
    for copy in copies:
        copy.wait()


def take_rows(own, *received):
    shape = (4 * own.shape[0], own.shape[1])
    return pl.pallas_call(
        take_rows_kernel,
        out_shape=jax.ShapeDtypeStruct(shape, own.dtype),
        in_specs=[pl.BlockSpec(memory_space=pl.ANY)] * 5,
        out_specs=pl.BlockSpec(memory_space=pltpu.VMEM),
        scratch_shapes=[pltpu.SemaphoreType.DMA((6,))],
        compiler_params=pltpu.CompilerParams(vmem_limit_bytes=VMEM_BYTES),
        cost_estimate=pl.CostEstimate(flops=0, bytes_accessed=4096, transcendentals=0),
        name="take_rows",
    )(own, *received)


def dense_call(kernel, name, outs, scratch, args):
    whole = pl.BlockSpec(memory_space=pltpu.VMEM)
    return pl.pallas_call(
        kernel,
        out_shape=[jax.ShapeDtypeStruct(shape, kind) for shape, kind in outs],
        in_specs=[whole] * len(args),
        out_specs=[whole] * len(outs),
        scratch_shapes=scratch,
        compiler_params=pltpu.CompilerParams(vmem_limit_bytes=VMEM_BYTES),
        cost_estimate=pl.CostEstimate(flops=1024, bytes_accessed=4096, transcendentals=0),
        name=name,
    )(*args)


def turned(value, cos_wide, sin_wide):
    half = HEAD_DIM // 2
    swapped = jnp.concatenate([value[:, half:], value[:, :half]], axis=1)
    return value * cos_wide + swapped * sin_wide


def rope_kernel(raw, cos_wide, sin_wide, query, kv):
    cos, sin = cos_wide[...], sin_wide[...]
    query_width, kv_width = query.shape[1], kv.shape[1] // 2
    for start in range(0, query_width, HEAD_DIM):
        columns = slice(start, start + HEAD_DIM)
        query[:, columns] = turned(raw[:, columns], cos, sin).astype(jnp.bfloat16)
    for start in range(0, kv_width, HEAD_DIM):
        columns = slice(query_width + start, query_width + start + HEAD_DIM)
        kv[:, start : start + HEAD_DIM] = turned(raw[:, columns], cos, sin).astype(jnp.bfloat16)
    values = raw[:, query_width + kv_width : query_width + 2 * kv_width]
    kv[:, kv_width:] = values.astype(jnp.bfloat16)


def pair_of(early, own, index):
    columns = slice(index * HEAD_DIM, (index + 1) * HEAD_DIM)
    return jnp.concatenate([early[:, columns], own[:, columns]], axis=0)


def attend_kernel(scale, query, early, own, query_ids, key_ids, attended, log_total, fill):
    kv_local = own.shape[1] // HEAD_DIM // 2
    rows_total = query.shape[0]
    half_rows = rows_total // 2
    for part in range(2):
        rows = slice(part * half_rows, (part + 1) * half_rows)
        allowed = (key_ids[:, 0:1] == query_ids[0:1, rows]) & (
            key_ids[:, 1:2] <= query_ids[1:2, rows]
        )
        fill[...] = jnp.where(allowed, 0.0, mask_fill)
        for kv in range(kv_local):
            keys = pair_of(early, own, kv)
            values = pair_of(early, own, kv_local + kv)
            for member in range(GROUP):
                head = kv * GROUP + member
                columns = slice(head * HEAD_DIM, (head + 1) * HEAD_DIM)
                scores = cols_dot(keys, query[rows, columns]) + fill[...]
                top = jnp.max(scores, axis=0, keepdims=True)
                weights = jnp.exp((scores - top) * scale)
                total = jnp.sum(weights, axis=0, keepdims=True)
                probs = (weights * (1.0 / total)).astype(jnp.bfloat16)
                attended[rows, columns] = rows_dot(values, probs).T.astype(jnp.bfloat16)
                log_total[head : head + 1, rows] = top * scale + jnp.log(total)


def attend_back_kernel(
    scale,
    query,
    early,
    own,
    query_ids,
    key_ids,
    log_total,
    grad_attended,
    cos_wide,
    sin_wide,
    grad_query,
    grad_early,
    grad_own,
    fill,
    all_probs,
    all_grads,
):
    kv_local = own.shape[1] // HEAD_DIM // 2
    rows_total = query.shape[0]
    half_rows = rows_total // 2
    for part in range(2):
        rows = slice(part * half_rows, (part + 1) * half_rows)
        allowed = (key_ids[:, 0:1] == query_ids[0:1, rows]) & (
            key_ids[:, 1:2] <= query_ids[1:2, rows]
        )
        fill[:, rows] = jnp.where(allowed, 0.0, mask_fill)
    for kv in range(kv_local):
        keys = pair_of(early, own, kv)
        values = pair_of(early, own, kv_local + kv)
        queries, outs = [], []
        for part in range(2):
            rows = slice(part * half_rows, (part + 1) * half_rows)
            cos, sin = cos_wide[rows, :], -sin_wide[rows, :]
            for member in range(GROUP):
                head = kv * GROUP + member
                columns = slice(head * HEAD_DIM, (head + 1) * HEAD_DIM)
                place = (part * GROUP + member) * half_rows
                where = slice(place, place + half_rows)
                one_query, one_out = query[rows, columns], grad_attended[rows, columns]
                queries.append(one_query)
                outs.append(one_out)
                scores = cols_dot(keys, one_query) + fill[:, rows]
                probs = jnp.exp(scores * scale - log_total[head : head + 1, rows])
                grad_probs = cols_dot(values, one_out)
                delta = jnp.sum(probs * grad_probs, axis=0, keepdims=True)
                grads = (probs * (grad_probs - delta)).astype(jnp.bfloat16)
                all_probs[:, where] = probs.astype(jnp.bfloat16)
                all_grads[:, where] = grads
                turned_grad = rows_dot(keys, grads).T * scale
                grad_query[rows, columns] = turned(turned_grad, cos, sin).astype(jnp.bfloat16)
        grad_keys = (
            jnp.dot(
                all_grads[...], jnp.concatenate(queries, axis=0), preferred_element_type=jnp.float32
            )
            * scale
        )
        grad_values = jnp.dot(
            all_probs[...], jnp.concatenate(outs, axis=0), preferred_element_type=jnp.float32
        )
        for start, grad in ((kv, grad_keys), (kv_local + kv, grad_values)):
            columns = slice(start * HEAD_DIM, (start + 1) * HEAD_DIM)
            grad_early[:, columns] = grad[:rows_total].astype(jnp.bfloat16)
            grad_own[:, columns] = grad[rows_total:]


def join_kernel(grad_query, grad_own, late, cos_wide, sin_wide, grad_raw):
    cos, sin = cos_wide[...], -sin_wide[...]
    query_width, kv_width = grad_query.shape[1], grad_own.shape[1] // 2
    grad_raw[:, :query_width] = grad_query[...]
    for start in range(0, kv_width, HEAD_DIM):
        columns = slice(start, start + HEAD_DIM)
        grad = grad_own[:, columns] + late[:, columns].astype(jnp.float32)
        grad_raw[:, query_width + start : query_width + start + HEAD_DIM] = turned(
            grad, cos, sin
        ).astype(jnp.bfloat16)
    values = grad_own[:, kv_width:] + late[:, kv_width:].astype(jnp.float32)
    used = query_width + 2 * kv_width
    grad_raw[:, query_width + kv_width : used] = values.astype(jnp.bfloat16)
    spare = grad_raw.shape[1] - used
    grad_raw[:, used:] = jnp.zeros((grad_raw.shape[0], spare), jnp.bfloat16)


def half_plan(
    tokens, doc_lengths, w_query, w_key, w_value, w_out, w_gate, w_up, w_down, norm_gains, cotangent
):
    fsdp_index = lax.axis_index("fsdp")
    seq_index = lax.axis_index("seq")
    tp_index = lax.axis_index("tp")
    near = seq_index % 2
    far = seq_index // 2
    local_rows = tokens.shape[0]
    group_rows = 4 * local_rows
    middle = D // 2
    quarter = D // 4
    block_rows = D // 16
    score_scale = 1.0 / math.sqrt(HEAD_DIM)

    def columns_in(value):
        return jnp.concatenate(
            [
                lax.dynamic_slice_in_dim(value, (fsdp_index ^ k) * quarter, quarter, 1)
                for k in (0, 2, 1, 3)
            ],
            axis=1,
        )

    def columns_out(value):
        pieces = []
        for block in range(4):
            k = fsdp_index ^ block
            place = (k // 2) + (k % 2) * 2
            pieces.append(lax.dynamic_slice_in_dim(value, place * quarter, quarter, 1))
        return jnp.concatenate(pieces, axis=1)

    def both_halves(array, size):
        low_part = array[:, :size]
        high_part = array[:, size:]
        high_part = jnp.pad(high_part, ((0, 0), (0, size - high_part.shape[1])))
        first = near == 0
        return jnp.where(first, low_part, high_part), jnp.where(first, high_part, low_part)

    def z_stage(halves):
        own, other = halves
        return own, to_z(other, 1), to_z(own, 2), to_z(other, 3)

    def joined(own, received, width):
        first = near == 0
        size = own.shape[1]
        low_part = jnp.where(first, own, received)
        high_part = jnp.where(first, received, own)[:, : width - size]
        return jnp.concatenate([low_part, high_part], axis=1)

    def gather_rows(value):
        half = value.shape[1] // 2
        one, two = value[:, :half], value[:, half:]
        one_near, two_tp = to_z(one, 1), to_tp(two)
        one_far = to_tp(jnp.concatenate([one, one_near], axis=0))
        two_far = to_z(jnp.concatenate([two, two_tp], axis=0), 1)
        return value, one_near, one_far, two_tp, two_far

    def scatter_start(one, two):
        n = local_rows
        send_one = jnp.concatenate([one[n : 2 * n], one[3 * n :]], axis=0)
        return one, two, to_tp(send_one), to_z(two[2 * n :], 1)

    def scatter_end(one, two, got_one, got_two):
        n = local_rows
        next_one = low_of(float_of(one[2 * n : 3 * n]) + float_of(got_one[n:]))
        next_two = low_of(float_of(two[n : 2 * n]) + float_of(got_two[n:]))
        last_one = to_z(next_one, 1)
        last_two = to_tp(next_two)
        sum_one = float_of(one[:n]) + float_of(got_one[:n]) + float_of(last_one)
        sum_two = float_of(two[:n]) + float_of(got_two[:n]) + float_of(last_two)
        return jnp.concatenate([sum_one, sum_two], axis=1)

    def grad_pair(left, right):
        other = low_of(rows_dot(left[:, middle:], right))
        from_core = to_core(other)
        return low_of(rows_dot(left[:, :middle], right)), from_core

    def x_send(mine, from_core):
        return low_of(float_of(mine[quarter:]) + float_of(from_core[quarter:]))

    def z_pieces(mine, from_core, from_x):
        total = low_of(
            float_of(mine[:quarter]) + float_of(from_core[:quarter]) + float_of(from_x)
        )
        return [
            lax.dynamic_slice_in_dim(total, (seq_index ^ k) * block_rows, block_rows, 0)
            for k in range(4)
        ]

    def z_send(pieces):
        return pieces[0], to_z(pieces[1], 1), to_z(pieces[2], 2), to_z(pieces[3], 3)

    def z_sum(own, from_near, from_far, from_last, width):
        return joined(
            float_of(own) + float_of(from_far), float_of(from_near) + float_of(from_last), width
        )

    query_width = w_query.shape[1] // 2
    key_width = w_key.shape[1] // 2
    kv_local = key_width // HEAD_DIM
    query_heads = query_width // HEAD_DIM
    heads_width = -(-(query_width + 2 * key_width) // 128) * 128
    hidden_width = -(-(w_gate.shape[1] // 2) // 128) * 128
    heads_parts = [
        both_halves(w_query, query_width),
        both_halves(w_key, key_width),
        both_halves(w_value, key_width),
    ]
    spare = heads_width - query_width - 2 * key_width
    heads_halves = [
        jnp.pad(jnp.concatenate([part[i] for part in heads_parts], axis=1), ((0, 0), (0, spare)))
        for i in range(2)
    ]
    gain_stack = norm_gains[None]
    for step in (1, 2):
        gain_stack = jnp.concatenate([gain_stack, to_z(gain_stack, step)], axis=0)
    gain_plane = jnp.concatenate(
        [
            lax.dynamic_index_in_dim(gain_stack, seq_index ^ k, 0, keepdims=False)
            for k in range(4)
        ],
        axis=1,
    )
    gain_mine = jnp.concatenate([gain_plane, to_x(gain_plane)], axis=1)
    gains = float_of(jnp.concatenate([gain_mine, to_core(gain_mine)], axis=1))
    gain_one = gains[0]
    gain_two = gains[1]
    heads_z = z_stage(heads_halves)
    tokens_in = columns_in(tokens)
    token_rows = float_of(tokens_in)
    inv_one = rms_scale(token_rows)
    heads_plane, heads_mine = place_rows(hold(heads_z, gain_stack), seq_index)
    heads_x = to_x(heads_plane)
    normed_rows = low_of(token_rows * inv_one * gain_one)
    normed_wait = gather_rows(hold(normed_rows, heads_plane))
    out_z = z_stage(hold(both_halves(w_out.T, query_width), heads_z[1]))
    gate_z = z_stage(hold(both_halves(w_gate, hidden_width), heads_z[2:]))
    up_z = z_stage(hold(both_halves(w_up, hidden_width), out_z[2:]))
    down_z = z_stage(hold(both_halves(w_down.T, hidden_width), gate_z[2:]))
    out_plane, out_mine = place_rows(hold(out_z, normed_rows), seq_index)

    row_ids = jnp.arange(local_rows, dtype=jnp.int32)
    own_positions = jnp.concatenate(
        [
            far * (2 * 2 * local_rows)
            + (near ^ i) * (2 * local_rows)
            + (tp_index ^ j) * local_rows
            + row_ids
            for i in range(2)
            for j in range(2)
        ]
    )
    cos_tab, sin_tab = rope_tables(own_positions)
    cos_wide = jnp.concatenate([cos_tab, cos_tab], axis=1)
    sin_wide = jnp.concatenate([-sin_tab, sin_tab], axis=1)
    key_positions = jnp.concatenate([own_positions - group_rows, own_positions])
    doc_ends = jnp.cumsum(doc_lengths[0])[: DOCS - 1]

    def doc_of(positions):
        return jnp.sum((positions[:, None] >= doc_ends[None, :]).astype(jnp.int32), axis=1)

    key_docs = jnp.where(key_positions >= 0, doc_of(key_positions), -1)
    query_ids = jnp.stack([doc_of(own_positions), own_positions // BLOCK])
    key_ids = jnp.stack([key_docs, key_positions // BLOCK], axis=1)

    heads_mine = fill_rows(*hold((heads_mine, heads_x), out_plane))
    heads_weights = heads_mine, to_core(heads_mine)
    out_x = to_x(out_plane)
    normed_one = take_rows(*hold(normed_wait, heads_mine))
    cot_in = columns_in(cotangent)
    cot_wait = gather_rows(hold(cot_in, normed_one))
    gate_plane, gate_mine = place_rows(hold(gate_z, heads_mine), seq_index)
    gate_x = to_x(gate_plane)
    raw = wide_dot(hold(normed_one, gate_plane), heads_weights)
    query_rot, own_kv = dense_call(
        rope_kernel,
        "rope",
        [
            ((group_rows, query_width), jnp.bfloat16),
            ((group_rows, 2 * key_width), jnp.bfloat16),
        ],
        [],
        (raw, cos_wide, sin_wide),
    )
    early_kv = lax.ppermute(own_kv, "seq", [(0, 2), (1, 3)])
    out_mine = fill_rows(*hold((out_mine, out_x), own_kv))
    out_weights = out_mine, to_core(out_mine)
    cot_span = take_rows(*hold(cot_wait, out_mine))
    query_rot = hold(query_rot, cot_span)
    attended_low, log_total = dense_call(
        functools.partial(attend_kernel, score_scale),
        "attend",
        [
            ((group_rows, query_width), jnp.bfloat16),
            ((query_heads, group_rows), jnp.float32),
        ],
        [pltpu.VMEM((2 * group_rows, group_rows // 2), jnp.float32)],
        (query_rot, early_kv, own_kv, query_ids, key_ids),
    )
    up_plane, up_mine = place_rows(hold(up_z, log_total), seq_index)
    up_x = to_x(up_plane)
    branch = scatter_start(
        *[low_of(cols_dot(hold(attended_low, up_plane), w)) for w in out_weights]
    )
    gate_mine = fill_rows(*hold((gate_mine, gate_x), branch[:2]))
    gate_weights = gate_mine, to_core(gate_mine)
    attn_branch = scatter_end(*hold(branch, gate_mine))
    residual = token_rows + attn_branch
    inv_two = rms_scale(residual)
    normed_two = low_of(residual * inv_two * gain_two)
    two_wait = gather_rows(normed_two)
    down_plane, down_mine = place_rows(hold(down_z, normed_two), seq_index)
    down_x = to_x(down_plane)
    up_mine = fill_rows(*hold((up_mine, up_x), down_plane))
    up_weights = up_mine, to_core(up_mine)
    span_two = take_rows(*hold(two_wait, up_mine))
    gate_pre = wide_dot(span_two, gate_weights)
    up_pre = wide_dot(span_two, up_weights)
    sig_gate = jax.nn.sigmoid(gate_pre)
    silu_gate = gate_pre * sig_gate
    hidden_low = low_of(silu_gate * up_pre)
    down_pair = grad_pair(cot_span, hidden_low)
    down_send = x_send(*down_pair)
    down_back = to_x(down_send)
    down_mine = fill_rows(*hold((down_mine, down_x), down_send))
    down_weights = down_mine, to_core(down_mine)
    grad_hidden = wide_dot(cot_span, down_weights)
    grad_gate_pre = low_of(grad_hidden * up_pre * (sig_gate * (1.0 + gate_pre * (1.0 - sig_gate))))
    grad_up_pre = low_of(grad_hidden * silu_gate)
    normed_back = scatter_start(
        *[
            low_of(cols_dot(grad_gate_pre, gate_w) + cols_dot(grad_up_pre, up_w))
            for gate_w, up_w in zip(gate_weights, up_weights)
        ]
    )
    gate_pair = grad_pair(hold(span_two, normed_back[:2]), grad_gate_pre)
    up_pair = grad_pair(hold(span_two, gate_pair[0]), grad_up_pre)
    gate_send = x_send(*hold(gate_pair, up_pair[0]))
    gate_back = to_x(gate_send)
    down_pieces = z_pieces(*hold((*down_pair, down_back), gate_send))
    down_done = z_send(down_pieces)
    grad_normed_two = scatter_end(*hold(normed_back, down_pieces))
    gain_two_term = jnp.sum(grad_normed_two * residual * inv_two, axis=0)
    scaled_two = grad_normed_two * gain_two
    grad_residual = (
        float_of(cot_in)
        + inv_two * scaled_two
        - residual
        * (inv_two * inv_two * inv_two)
        * jnp.mean(scaled_two * residual, axis=-1, keepdims=True)
    )
    grad_residual_low = low_of(grad_residual)
    grad_wait = gather_rows(grad_residual_low)
    up_send = x_send(*hold(up_pair, grad_residual_low))
    up_back = to_x(up_send)
    mlp_parts = [low_of(cols_dot(hold(hidden_low, up_send), w)) for w in down_weights]
    gate_pieces = z_pieces(*hold((*gate_pair, gate_back), mlp_parts))
    gate_done = z_send(gate_pieces)
    hidden_units = w_gate.shape[1]
    grad_down = z_sum(*hold(down_done, gate_pieces), hidden_units).T
    grad_span = take_rows(*hold(grad_wait, gate_pieces))
    grad_attended = low_of(wide_dot(grad_span, out_weights))
    branch_mlp = scatter_start(*hold(mlp_parts, grad_span))
    grad_query, grad_early, grad_own = dense_call(
        functools.partial(attend_back_kernel, score_scale),
        "attend_back",
        [
            ((group_rows, query_width), jnp.bfloat16),
            ((group_rows, 2 * key_width), jnp.bfloat16),
            ((group_rows, 2 * key_width), jnp.float32),
        ],
        [
            pltpu.VMEM((2 * group_rows, group_rows), jnp.float32),
            pltpu.VMEM((2 * group_rows, GROUP * group_rows), jnp.bfloat16),
            pltpu.VMEM((2 * group_rows, GROUP * group_rows), jnp.bfloat16),
        ],
        (
            query_rot,
            early_kv,
            own_kv,
            query_ids,
            key_ids,
            log_total,
            hold(grad_attended, grad_down),
            cos_wide,
            sin_wide,
        ),
    )
    late_kv = lax.ppermute(grad_early, "seq", [(2, 0), (3, 1)])
    out_pair = grad_pair(hold(grad_span, grad_early), attended_low)
    mlp_branch = scatter_end(*hold(branch_mlp, out_pair[0]))
    mixed_out = columns_out(low_of(residual + mlp_branch))
    out_send = x_send(*out_pair)
    out_back = to_x(out_send)
    up_pieces = z_pieces(*hold((*up_pair, up_back), out_send))
    up_done = z_send(up_pieces)
    (grad_raw,) = dense_call(
        join_kernel,
        "join",
        [((group_rows, heads_width), jnp.bfloat16)],
        [],
        (grad_query, grad_own, hold(late_kv, up_pieces), cos_wide, sin_wide),
    )
    heads_pair = grad_pair(normed_one, grad_raw)
    first_back = scatter_start(
        *[low_of(cols_dot(hold(grad_raw, heads_pair[0]), w)) for w in heads_weights]
    )
    heads_send = x_send(*hold(heads_pair, first_back[:2]))
    heads_back = to_x(heads_send)
    grad_gate = z_sum(*hold(gate_done, heads_send), hidden_units)
    out_pieces = z_pieces(*hold((*out_pair, out_back), heads_send))
    out_done = z_send(out_pieces)
    grad_normed_one = scatter_end(*hold(first_back, out_pieces, grad_gate))
    scaled_one = grad_normed_one * gain_one
    grad_tokens = columns_out(
        grad_residual
        + inv_one * scaled_one
        - token_rows
        * (inv_one * inv_one * inv_one)
        * jnp.mean(scaled_one * token_rows, axis=-1, keepdims=True)
    )
    gain_one_term = jnp.sum(grad_normed_one * token_rows * inv_one, axis=0)
    gain_rows = jnp.stack([gain_one_term, gain_two_term])
    heads_pieces = z_pieces(*hold((*heads_pair, heads_back), gain_rows))
    heads_done = z_send(heads_pieces)
    gain_rows = gain_rows[:, :middle] + to_core(gain_rows[:, middle:])
    gain_rows = gain_rows[:, :quarter] + to_x(gain_rows[:, quarter:])
    gain_rows = gain_rows + to_tp(gain_rows)
    gain_blocks = gain_rows.reshape(2, 4, block_rows)
    gain_grads = sum(
        to_z(piece, k) if k else piece
        for k, piece in (
            (k, lax.dynamic_index_in_dim(gain_blocks, seq_index ^ k, 1, keepdims=False))
            for k in range(4)
        )
    )
    grad_up = z_sum(*hold(up_done, heads_pieces), hidden_units)
    grad_out = z_sum(*hold(out_done, grad_up), w_out.shape[0]).T
    heads_own, heads_near, heads_far, heads_last = hold(heads_done, grad_out)
    heads_first = float_of(heads_own) + float_of(heads_far)
    heads_second = float_of(heads_near) + float_of(heads_last)
    splits = (query_width, query_width + key_width, query_width + 2 * key_width)
    grad_query_w, grad_key_w, grad_value_w = (
        joined(own, other, 2 * own.shape[1])
        for own, other in list(
            zip(jnp.split(heads_first, splits, axis=1), jnp.split(heads_second, splits, axis=1))
        )[:3]
    )
    return (
        mixed_out,
        grad_tokens,
        grad_query_w,
        grad_key_w,
        grad_value_w,
        grad_out,
        grad_gate,
        grad_up,
        grad_down,
        gain_grads,
    )


def solution(mesh):
    halves = mesh.shape["seq"] == 4 and mesh.shape["tp"] == 2 and mesh.shape["fsdp"] == 4
    plan = half_plan if halves else per_device
    in_specs = (
        P(("fsdp", "seq", "tp"), None),
        P("fsdp", None),
        P(("fsdp", "seq"), "tp"),
        P(("fsdp", "seq"), "tp"),
        P(("fsdp", "seq"), "tp"),
        P("tp", ("fsdp", "seq")),
        P(("fsdp", "seq"), "tp"),
        P(("fsdp", "seq"), "tp"),
        P("tp", ("fsdp", "seq")),
        P(None, ("fsdp", "seq")),
        P(("fsdp", "seq", "tp"), None),
    )
    out_specs = (
        P(("fsdp", "seq", "tp"), None),
        P(("fsdp", "seq", "tp"), None),
        P(("fsdp", "seq"), "tp"),
        P(("fsdp", "seq"), "tp"),
        P(("fsdp", "seq"), "tp"),
        P("tp", ("fsdp", "seq")),
        P(("fsdp", "seq"), "tp"),
        P(("fsdp", "seq"), "tp"),
        P("tp", ("fsdp", "seq")),
        P(None, ("fsdp", "seq")),
    )
    return jax.shard_map(
        plan, mesh=mesh, in_specs=in_specs, out_specs=out_specs, check_vma=False
    )
```

```python
import functools
import math

import jax
import jax.numpy as jnp
from jax import lax
from jax.experimental import pallas as pl
from jax.experimental.pallas import tpu as pltpu
from jax.sharding import PartitionSpec as P

D = 2560
HEAD_DIM = 80
BLOCK = 256
DOCS = 3
GROUP = 4


norm_eps = 1e-05
rope_base = 10000.0
mask_fill = -1000000000.0


def rope_tables(positions):
    half_dim = HEAD_DIM // 2
    freq_row = rope_base ** (-jnp.arange(half_dim, dtype=jnp.float32) * 2.0 / HEAD_DIM)
    angles = positions.astype(jnp.float32)[:, None] * freq_row[None, :]
    return (jnp.cos(angles), jnp.sin(angles))


def rotate(values, cos_tab, sin_tab):
    half_dim = HEAD_DIM // 2
    first_half = values[..., :half_dim]
    second_half = values[..., half_dim:]
    cos_wide = cos_tab[:, None, :]
    sin_wide = sin_tab[:, None, :]
    return jnp.concatenate(
        [
            first_half * cos_wide - second_half * sin_wide,
            second_half * cos_wide + first_half * sin_wide,
        ],
        axis=-1,
    )


def document_ids(lengths, positions):
    doc_ends = jnp.cumsum(lengths)
    return jnp.sum((positions[:, None] >= doc_ends[None, : DOCS - 1]).astype(jnp.int32), axis=1)


def rms_scale(row_values):
    return lax.rsqrt(jnp.mean(row_values * row_values, axis=-1, keepdims=True) + norm_eps)


def per_device(
    tokens, doc_lengths, w_query, w_key, w_value, w_out, w_gate, w_up, w_down, norm_gains, cotangent
):
    tp_count = lax.axis_size("tp")
    seq_count = lax.axis_size("seq")
    tp_index = lax.axis_index("tp")
    seq_index = lax.axis_index("seq")
    local_rows = tokens.shape[0]
    span_len = local_rows * tp_count
    seq_length = span_len * seq_count
    score_scale = 1.0 / math.sqrt(HEAD_DIM)
    key_step = math.gcd(512, seq_length)
    gathered = (
        lax.all_gather(w_query, ("fsdp", "seq"), axis=0, tiled=True),
        lax.all_gather(w_key, ("fsdp", "seq"), axis=0, tiled=True),
        lax.all_gather(w_value, ("fsdp", "seq"), axis=0, tiled=True),
        lax.all_gather(w_out, ("fsdp", "seq"), axis=1, tiled=True),
        lax.all_gather(w_gate, ("fsdp", "seq"), axis=0, tiled=True),
        lax.all_gather(w_up, ("fsdp", "seq"), axis=0, tiled=True),
        lax.all_gather(w_down, ("fsdp", "seq"), axis=1, tiled=True),
        lax.all_gather(norm_gains, ("fsdp", "seq"), axis=1, tiled=True),
    )
    query_full, key_full, value_full, out_full, gate_full, up_full, down_full, gains_low = gathered
    gain_one = gains_low[0].astype(jnp.float32)
    gain_two = gains_low[1].astype(jnp.float32)
    query_heads = query_full.shape[1] // HEAD_DIM
    kv_local = key_full.shape[1] // HEAD_DIM
    span_in = lax.all_gather(tokens, "tp", axis=0, tiled=True)
    span_float = span_in.astype(jnp.float32)
    inv_one = rms_scale(span_float)
    normed_one = (span_float * inv_one * gain_one).astype(jnp.bfloat16)
    span_start = seq_index * span_len
    positions = span_start + jnp.arange(span_len, dtype=jnp.int32)
    cos_tab, sin_tab = rope_tables(positions)
    query_raw = jnp.dot(normed_one, query_full, preferred_element_type=jnp.float32).reshape(
        span_len, query_heads, HEAD_DIM
    )
    key_raw = jnp.dot(normed_one, key_full, preferred_element_type=jnp.float32).reshape(
        span_len, kv_local, HEAD_DIM
    )
    value_raw = jnp.dot(normed_one, value_full, preferred_element_type=jnp.float32).reshape(
        span_len, kv_local, HEAD_DIM
    )
    query_rot = rotate(query_raw, cos_tab, sin_tab).astype(jnp.bfloat16)
    key_rot = rotate(key_raw, cos_tab, sin_tab).astype(jnp.bfloat16)
    value_low = value_raw.astype(jnp.bfloat16)
    query_group = query_rot.reshape(span_len, kv_local, GROUP, HEAD_DIM)
    key_all, value_all = (
        lax.all_gather(key_rot, "seq", axis=0, tiled=True),
        lax.all_gather(value_low, "seq", axis=0, tiled=True),
    )
    key_positions = jnp.arange(seq_length, dtype=jnp.int32)
    doc_keys = document_ids(doc_lengths[0], key_positions)
    doc_query = lax.dynamic_slice_in_dim(doc_keys, span_start, span_len, 0)
    key_blocks = key_positions // BLOCK
    query_block = positions // BLOCK
    blocks_used = (span_start + span_len + key_step - 1) // key_step
    stat_shape = (kv_local, GROUP, span_len)
    head_shape = (span_len, kv_local, GROUP, HEAD_DIM)

    def masked_scores(block_index):
        key_start = block_index * key_step
        key_part = lax.dynamic_slice_in_dim(key_all, key_start, key_step, 0)
        scores = (
            jnp.einsum("ckgd,nkd->kgcn", query_group, key_part, preferred_element_type=jnp.float32)
            * score_scale
        )
        block_part = lax.dynamic_slice_in_dim(key_blocks, key_start, key_step, 0)
        doc_part = lax.dynamic_slice_in_dim(doc_keys, key_start, key_step, 0)
        allowed = (block_part[None, :] <= query_block[:, None]) & (
            doc_part[None, :] == doc_query[:, None]
        )
        return (jnp.where(allowed[None, None], scores, mask_fill), key_start, key_part)

    def total_step(block_index, carry):
        row_max, row_sum = carry
        scores = masked_scores(block_index)[0]
        new_max = jnp.maximum(row_max, jnp.max(scores, axis=-1))
        row_sum = row_sum * jnp.exp(row_max - new_max) + jnp.sum(
            jnp.exp(scores - new_max[..., None]), axis=-1
        )
        return (new_max, row_sum)

    row_max, row_sum = lax.fori_loop(
        0,
        blocks_used,
        total_step,
        (jnp.full(stat_shape, mask_fill, jnp.float32), jnp.zeros(stat_shape, jnp.float32)),
    )
    log_total = row_max + jnp.log(row_sum)

    def out_step(block_index, running):
        scores, key_start, key_part = masked_scores(block_index)
        attn_prob = jnp.exp(scores - log_total[..., None]).astype(jnp.bfloat16)
        value_part = lax.dynamic_slice_in_dim(value_all, key_start, key_step, 0)
        return running + jnp.einsum(
            "kgcn,nkd->ckgd", attn_prob, value_part, preferred_element_type=jnp.float32
        )

    attended = lax.fori_loop(0, blocks_used, out_step, jnp.zeros(head_shape, jnp.float32))
    attended_low = attended.reshape(span_len, query_heads * HEAD_DIM).astype(jnp.bfloat16)
    attn_branch = lax.psum_scatter(
        jnp.dot(attended_low, out_full, preferred_element_type=jnp.float32).astype(jnp.bfloat16),
        "tp",
        scatter_dimension=0,
        tiled=True,
    ).astype(jnp.float32)
    token_rows = tokens.astype(jnp.float32)
    residual = token_rows + attn_branch
    inv_two = rms_scale(residual)
    normed_two = (residual * inv_two * gain_two).astype(jnp.bfloat16)
    span_two = lax.all_gather(normed_two, "tp", axis=0, tiled=True)
    gate_pre = jnp.dot(span_two, gate_full, preferred_element_type=jnp.float32)
    up_pre = jnp.dot(span_two, up_full, preferred_element_type=jnp.float32)
    sig_gate = jax.nn.sigmoid(gate_pre)
    silu_gate = gate_pre * sig_gate
    hidden_low = (silu_gate * up_pre).astype(jnp.bfloat16)
    mlp_branch = lax.psum_scatter(
        jnp.dot(hidden_low, down_full, preferred_element_type=jnp.float32).astype(jnp.bfloat16),
        "tp",
        scatter_dimension=0,
        tiled=True,
    ).astype(jnp.float32)
    mixed_out = (residual + mlp_branch).astype(jnp.bfloat16)
    cot_span = lax.all_gather(cotangent, "tp", axis=0, tiled=True)
    grad_down_w = jnp.einsum("cf,cd->fd", hidden_low, cot_span, preferred_element_type=jnp.float32)
    grad_hidden = jnp.einsum("cd,fd->cf", cot_span, down_full, preferred_element_type=jnp.float32)
    grad_gate_pre = (
        grad_hidden * up_pre * (sig_gate * (1.0 + gate_pre * (1.0 - sig_gate)))
    ).astype(jnp.bfloat16)
    grad_up_pre = (grad_hidden * silu_gate).astype(jnp.bfloat16)
    grad_gate_w = jnp.einsum(
        "cd,cf->df", span_two, grad_gate_pre, preferred_element_type=jnp.float32
    )
    grad_up_w = jnp.einsum("cd,cf->df", span_two, grad_up_pre, preferred_element_type=jnp.float32)
    grad_normed_two = lax.psum_scatter(
        (
            jnp.einsum("cf,df->cd", grad_gate_pre, gate_full, preferred_element_type=jnp.float32)
            + jnp.einsum("cf,df->cd", grad_up_pre, up_full, preferred_element_type=jnp.float32)
        ).astype(jnp.bfloat16),
        "tp",
        scatter_dimension=0,
        tiled=True,
    ).astype(jnp.float32)
    gain_two_term = jnp.sum(grad_normed_two * residual * inv_two, axis=0)
    scaled_two = grad_normed_two * gain_two
    grad_residual = (
        cotangent.astype(jnp.float32)
        + inv_two * scaled_two
        - residual
        * (inv_two * inv_two * inv_two)
        * jnp.mean(scaled_two * residual, axis=-1, keepdims=True)
    )
    grad_span = lax.all_gather(grad_residual.astype(jnp.bfloat16), "tp", axis=0, tiled=True)
    grad_out_w = jnp.einsum(
        "ce,cd->ed", attended_low, grad_span, preferred_element_type=jnp.float32
    )
    grad_attended = (
        jnp.einsum("cd,ed->ce", grad_span, out_full, preferred_element_type=jnp.float32)
        .astype(jnp.bfloat16)
        .reshape(head_shape)
    )

    def prob_grads(block_index):
        scores, key_start, key_part = masked_scores(block_index)
        probs_full = jnp.exp(scores - log_total[..., None])
        value_part = lax.dynamic_slice_in_dim(value_all, key_start, key_step, 0)
        grad_prob = jnp.einsum(
            "ckgd,nkd->kgcn", grad_attended, value_part, preferred_element_type=jnp.float32
        )
        return (probs_full, grad_prob, key_start, key_part)

    def delta_step(block_index, running):
        grads_here = prob_grads(block_index)
        return running + jnp.sum(grads_here[0] * grads_here[1], axis=-1)

    row_delta = lax.fori_loop(0, blocks_used, delta_step, jnp.zeros(stat_shape, jnp.float32))

    def grad_step(block_index, carry):
        query_acc, key_acc, value_acc = carry
        probs_full, grad_prob, key_start, key_part = prob_grads(block_index)
        grad_scores = (probs_full * (grad_prob - row_delta[..., None])).astype(jnp.bfloat16)
        query_acc = query_acc + jnp.einsum(
            "kgcn,nkd->ckgd", grad_scores, key_part, preferred_element_type=jnp.float32
        )
        key_term = (
            jnp.einsum(
                "kgcn,ckgd->nkd", grad_scores, query_group, preferred_element_type=jnp.float32
            )
            * score_scale
        )
        value_term = jnp.einsum(
            "kgcn,ckgd->nkd",
            probs_full.astype(jnp.bfloat16),
            grad_attended,
            preferred_element_type=jnp.float32,
        )
        key_old = lax.dynamic_slice_in_dim(key_acc, key_start, key_step, 0)
        value_old = lax.dynamic_slice_in_dim(value_acc, key_start, key_step, 0)
        key_acc = lax.dynamic_update_slice_in_dim(key_acc, key_old + key_term, key_start, 0)
        value_acc = lax.dynamic_update_slice_in_dim(value_acc, value_old + value_term, key_start, 0)
        return (query_acc, key_acc, value_acc)

    kv_zeros = jnp.zeros((seq_length, kv_local, HEAD_DIM), jnp.float32)
    query_acc, key_acc, value_acc = lax.fori_loop(
        0, blocks_used, grad_step, (jnp.zeros(head_shape, jnp.float32), kv_zeros, kv_zeros)
    )
    key_own, value_own = (
        lax.psum_scatter(
            key_acc.astype(jnp.bfloat16), "seq", scatter_dimension=0, tiled=True
        ).astype(jnp.float32),
        lax.psum_scatter(
            value_acc.astype(jnp.bfloat16), "seq", scatter_dimension=0, tiled=True
        ).astype(jnp.float32),
    )
    grad_query_rot = (query_acc * score_scale).reshape(span_len, query_heads, HEAD_DIM)
    grad_query_raw = (
        rotate(grad_query_rot, cos_tab, -sin_tab)
        .reshape(span_len, query_heads * HEAD_DIM)
        .astype(jnp.bfloat16)
    )
    grad_key_raw = (
        rotate(key_own, cos_tab, -sin_tab)
        .reshape(span_len, kv_local * HEAD_DIM)
        .astype(jnp.bfloat16)
    )
    grad_value_raw = value_own.reshape(span_len, kv_local * HEAD_DIM).astype(jnp.bfloat16)
    grad_query_w = jnp.einsum(
        "cd,ce->de", normed_one, grad_query_raw, preferred_element_type=jnp.float32
    )
    grad_key_w = jnp.einsum(
        "cd,ce->de", normed_one, grad_key_raw, preferred_element_type=jnp.float32
    )
    grad_value_w = jnp.einsum(
        "cd,ce->de", normed_one, grad_value_raw, preferred_element_type=jnp.float32
    )
    normed_part = jnp.einsum(
        "ce,de->cd", grad_query_raw, query_full, preferred_element_type=jnp.float32
    )
    normed_part = normed_part + jnp.einsum(
        "ce,de->cd", grad_key_raw, key_full, preferred_element_type=jnp.float32
    )
    normed_part = normed_part + jnp.einsum(
        "ce,de->cd", grad_value_raw, value_full, preferred_element_type=jnp.float32
    )
    gain_one_term = jnp.sum(normed_part * span_float * inv_one, axis=0)
    gain_block = jnp.broadcast_to(jnp.stack([gain_one_term, gain_two_term])[None], (tp_count, 2, D))
    grad_normed_one, gains_summed = (
        lax.psum_scatter(
            normed_part.astype(jnp.bfloat16), "tp", scatter_dimension=0, tiled=True
        ).astype(jnp.float32),
        lax.psum_scatter(
            gain_block.astype(jnp.bfloat16), "tp", scatter_dimension=0, tiled=True
        ).astype(jnp.float32),
    )
    gains_total = gains_summed[0]
    inv_rows = lax.dynamic_slice_in_dim(inv_one, tp_index * local_rows, local_rows, 0)
    scaled_one = grad_normed_one * gain_one
    grad_tokens = (
        grad_residual
        + inv_rows * scaled_one
        - token_rows
        * (inv_rows * inv_rows * inv_rows)
        * jnp.mean(scaled_one * token_rows, axis=-1, keepdims=True)
    )
    summed = (
        lax.psum_scatter(
            grad_query_w.astype(jnp.bfloat16), ("fsdp", "seq"), scatter_dimension=0, tiled=True
        ).astype(jnp.float32),
        lax.psum_scatter(
            grad_key_w.astype(jnp.bfloat16), ("fsdp", "seq"), scatter_dimension=0, tiled=True
        ).astype(jnp.float32),
        lax.psum_scatter(
            grad_value_w.astype(jnp.bfloat16), ("fsdp", "seq"), scatter_dimension=0, tiled=True
        ).astype(jnp.float32),
        lax.psum_scatter(
            grad_out_w.astype(jnp.bfloat16), ("fsdp", "seq"), scatter_dimension=1, tiled=True
        ).astype(jnp.float32),
        lax.psum_scatter(
            grad_gate_w.astype(jnp.bfloat16), ("fsdp", "seq"), scatter_dimension=0, tiled=True
        ).astype(jnp.float32),
        lax.psum_scatter(
            grad_up_w.astype(jnp.bfloat16), ("fsdp", "seq"), scatter_dimension=0, tiled=True
        ).astype(jnp.float32),
        lax.psum_scatter(
            grad_down_w.astype(jnp.bfloat16), ("fsdp", "seq"), scatter_dimension=1, tiled=True
        ).astype(jnp.float32),
        lax.psum_scatter(
            gains_total.astype(jnp.bfloat16), ("fsdp", "seq"), scatter_dimension=1, tiled=True
        ).astype(jnp.float32),
    )
    return (
        mixed_out,
        grad_tokens,
        summed[0],
        summed[1],
        summed[2],
        summed[3],
        summed[4],
        summed[5],
        summed[6],
        summed[7],
    )


VMEM_BYTES = 48 * 1024 * 1024
SMALL_COST = pl.CostEstimate(flops=1024, bytes_accessed=4096, transcendentals=0)


def to_core(value):
    return lax.ppermute(value, "fsdp", [(i, i ^ 1) for i in range(4)])


def to_x(value):
    return lax.ppermute(value, "fsdp", [(i, i ^ 2) for i in range(4)])


def to_z(value, step):
    return lax.ppermute(value, "seq", [(i, i ^ step) for i in range(4)])


def to_tp(value):
    return lax.ppermute(value, "tp", [(0, 1), (1, 0)])


def hold(value, *events):
    return lax.optimization_barrier((value, events))[0]


def float_of(value):
    return value.astype(jnp.float32)


def low_of(value):
    return value.astype(jnp.bfloat16)


def rows_dot(left, right):
    return lax.dot_general(left, right, (((0,), (0,)), ((), ())), preferred_element_type=jnp.float32)


def cols_dot(left, right):
    return lax.dot_general(left, right, (((1,), (1,)), ((), ())), preferred_element_type=jnp.float32)


def place_kernel(rows, place, pair, pair_far, plane, mine, held, read_sems, sems):
    reads = [
        pltpu.make_async_copy(
            (pair, pair_far)[k // 2].at[pl.ds((k % 2) * rows, rows), :], held.at[k], read_sems.at[k]
        )
        for k in range(4)
    ]
    for copy in reads:
        copy.start()
    writes = []
    for k, read in enumerate(reads):
        read.wait()
        start = pl.multiple_of((place[0] ^ k) * rows, 16)
        for i, target in enumerate((plane, mine)):
            write = pltpu.make_async_copy(
                held.at[k], target.at[pl.ds(start, rows), :], sems.at[2 * k + i]
            )
            write.start()
            writes.append(write)
    for write in writes:
        write.wait()


def place_rows(pair, pair_far, place):
    rows, columns = pair.shape[0] // 2, pair.shape[1]
    anywhere = pl.BlockSpec(memory_space=pl.ANY)
    return pl.pallas_call(
        lambda *refs: place_kernel(rows, *refs),
        out_shape=(
            jax.ShapeDtypeStruct((4 * rows, columns), jnp.bfloat16),
            jax.ShapeDtypeStruct((8 * rows, columns), jnp.bfloat16),
        ),
        in_specs=[pl.BlockSpec(memory_space=pltpu.SMEM)] + [anywhere] * 2,
        out_specs=(anywhere, anywhere),
        scratch_shapes=[
            pltpu.VMEM((4, rows, columns), jnp.bfloat16),
            pltpu.SemaphoreType.DMA((4,)),
            pltpu.SemaphoreType.DMA((8,)),
        ],
        cost_estimate=SMALL_COST,
        name="place_rows",
    )(place.reshape(1), pair, pair_far)


def fill_kernel(rows, part, start, across, first, mine, held, read_sems, sems):
    columns = pl.ds(start, mine.shape[1])
    reads = [
        pltpu.make_async_copy(
            across.at[pl.ds(k * part, part), columns], held.at[k], read_sems.at[k]
        )
        for k in range(rows // part)
    ]
    for copy in reads:
        copy.start()
    writes = []
    for k, read in enumerate(reads):
        read.wait()
        write = pltpu.make_async_copy(
            held.at[k], mine.at[pl.ds(rows + k * part, part), :], sems.at[k]
        )
        write.start()
        writes.append(write)
    for write in writes:
        write.wait()


def fill_rows(mine, across, start=0):
    rows, columns = across.shape[0], mine.shape[1]
    part = 128 if rows % 128 == 0 else 32
    anywhere = pl.BlockSpec(memory_space=pl.ANY)
    return pl.pallas_call(
        lambda *refs: fill_kernel(rows, part, start, *refs),
        out_shape=jax.ShapeDtypeStruct(mine.shape, mine.dtype),
        in_specs=[anywhere] * 2,
        out_specs=anywhere,
        scratch_shapes=[
            pltpu.VMEM((rows // part, part, columns), jnp.bfloat16),
            pltpu.SemaphoreType.DMA((rows // part,)),
            pltpu.SemaphoreType.DMA((rows // part,)),
        ],
        input_output_aliases={1: 0},
        cost_estimate=SMALL_COST,
        name="fill_rows",
    )(across, mine)


def take_rows_kernel(one, two, one_near, one_far, two_tp, two_far, out, sems):
    n, half = one.shape
    left, right = pl.ds(0, half), pl.ds(half, half)
    moves = [
        (one, pl.ds(0, n), left),
        (two, pl.ds(0, n), right),
        (one_near, pl.ds(2 * n, n), left),
        (one_far.at[pl.ds(0, n), :], pl.ds(n, n), left),
        (one_far.at[pl.ds(n, n), :], pl.ds(3 * n, n), left),
        (two_tp, pl.ds(n, n), right),
        (two_far, pl.ds(2 * n, 2 * n), right),
    ]
    copies = [
        pltpu.make_async_copy(source, out.at[rows, columns], sems.at[k])
        for k, (source, rows, columns) in enumerate(moves)
    ]
    for copy in copies:
        copy.start()
    for copy in copies:
        copy.wait()


def take_rows(*pieces):
    rows, half = pieces[0].shape
    return pl.pallas_call(
        take_rows_kernel,
        out_shape=jax.ShapeDtypeStruct((4 * rows, 2 * half), pieces[0].dtype),
        in_specs=[pl.BlockSpec(memory_space=pl.ANY)] * 6,
        out_specs=pl.BlockSpec(memory_space=pltpu.VMEM),
        scratch_shapes=[pltpu.SemaphoreType.DMA((7,))],
        compiler_params=pltpu.CompilerParams(vmem_limit_bytes=VMEM_BYTES),
        cost_estimate=SMALL_COST,
        name="take_rows",
    )(*pieces)


def dense_call(kernel, name, outs, scratch, args):
    whole = pl.BlockSpec(memory_space=pltpu.VMEM)
    return pl.pallas_call(
        kernel,
        out_shape=[jax.ShapeDtypeStruct(shape, kind) for shape, kind in outs],
        in_specs=[whole] * len(args),
        out_specs=[whole] * len(outs),
        scratch_shapes=scratch,
        compiler_params=pltpu.CompilerParams(vmem_limit_bytes=VMEM_BYTES),
        cost_estimate=SMALL_COST,
        name=name,
    )(*args)


def turned(value, cos_wide, sin_wide):
    half = HEAD_DIM // 2
    swapped = jnp.concatenate([value[:, half:], value[:, :half]], axis=1)
    return value * cos_wide + swapped * sin_wide


def rope_kernel(raw, cos_wide, sin_wide, query, kv):
    cos, sin = cos_wide[...], sin_wide[...]
    query_width, kv_width = query.shape[1], kv.shape[1] // 2
    for start in range(0, query_width, HEAD_DIM):
        columns = slice(start, start + HEAD_DIM)
        query[:, columns] = turned(raw[:, columns], cos, sin).astype(jnp.bfloat16)
    for start in range(0, kv_width, HEAD_DIM):
        columns = slice(query_width + start, query_width + start + HEAD_DIM)
        kv[:, start : start + HEAD_DIM] = turned(raw[:, columns], cos, sin).astype(jnp.bfloat16)
    values = raw[:, query_width + kv_width : query_width + 2 * kv_width]
    kv[:, kv_width:] = values.astype(jnp.bfloat16)


def pair_of(early, own, index):
    columns = slice(index * HEAD_DIM, (index + 1) * HEAD_DIM)
    return jnp.concatenate([early[:, columns], own[:, columns]], axis=0)


def attend_kernel(scale, query, early, own, query_ids, key_ids, attended, log_total, fill):
    kv_local = own.shape[1] // HEAD_DIM // 2
    rows_total = query.shape[0]
    half_rows = rows_total // 2
    for part in range(2):
        rows = slice(part * half_rows, (part + 1) * half_rows)
        allowed = (key_ids[:, 0:1] == query_ids[0:1, rows]) & (
            key_ids[:, 1:2] <= query_ids[1:2, rows]
        )
        fill[...] = jnp.where(allowed, 0.0, mask_fill)
        for kv in range(kv_local):
            keys = pair_of(early, own, kv)
            values = pair_of(early, own, kv_local + kv)
            for member in range(GROUP):
                head = kv * GROUP + member
                columns = slice(head * HEAD_DIM, (head + 1) * HEAD_DIM)
                scores = cols_dot(keys, query[rows, columns]) + fill[...]
                top = jnp.max(scores, axis=0, keepdims=True)
                weights = jnp.exp((scores - top) * scale)
                total = jnp.sum(weights, axis=0, keepdims=True)
                probs = (weights * (1.0 / total)).astype(jnp.bfloat16)
                attended[rows, columns] = rows_dot(values, probs).T.astype(jnp.bfloat16)
                log_total[head : head + 1, rows] = top * scale + jnp.log(total)


def attend_back_kernel(
    scale,
    query,
    early,
    own,
    query_ids,
    key_ids,
    log_total,
    grad_attended,
    cos_wide,
    sin_wide,
    grad_query,
    grad_early,
    grad_own,
    fill,
    all_probs,
    all_grads,
):
    kv_local = own.shape[1] // HEAD_DIM // 2
    rows_total = query.shape[0]
    half_rows = rows_total // 2
    for part in range(2):
        rows = slice(part * half_rows, (part + 1) * half_rows)
        allowed = (key_ids[:, 0:1] == query_ids[0:1, rows]) & (
            key_ids[:, 1:2] <= query_ids[1:2, rows]
        )
        fill[:, rows] = jnp.where(allowed, 0.0, mask_fill)
    for kv in range(kv_local):
        keys = pair_of(early, own, kv)
        values = pair_of(early, own, kv_local + kv)
        queries, outs = [], []
        for part in range(2):
            rows = slice(part * half_rows, (part + 1) * half_rows)
            cos, sin = cos_wide[rows, :], -sin_wide[rows, :]
            for member in range(GROUP):
                head = kv * GROUP + member
                columns = slice(head * HEAD_DIM, (head + 1) * HEAD_DIM)
                place = (part * GROUP + member) * half_rows
                where = slice(place, place + half_rows)
                one_query, one_out = query[rows, columns], grad_attended[rows, columns]
                queries.append(one_query)
                outs.append(one_out)
                scores = cols_dot(keys, one_query) + fill[:, rows]
                probs = jnp.exp(scores * scale - log_total[head : head + 1, rows])
                grad_probs = cols_dot(values, one_out)
                delta = jnp.sum(probs * grad_probs, axis=0, keepdims=True)
                grads = (probs * (grad_probs - delta)).astype(jnp.bfloat16)
                all_probs[:, where] = probs.astype(jnp.bfloat16)
                all_grads[:, where] = grads
                turned_grad = rows_dot(keys, grads).T * scale
                grad_query[rows, columns] = turned(turned_grad, cos, sin).astype(jnp.bfloat16)
        grad_keys = (
            jnp.dot(
                all_grads[...], jnp.concatenate(queries, axis=0), preferred_element_type=jnp.float32
            )
            * scale
        )
        grad_values = jnp.dot(
            all_probs[...], jnp.concatenate(outs, axis=0), preferred_element_type=jnp.float32
        )
        for start, grad in ((kv, grad_keys), (kv_local + kv, grad_values)):
            columns = slice(start * HEAD_DIM, (start + 1) * HEAD_DIM)
            grad_early[:, columns] = grad[:rows_total].astype(jnp.bfloat16)
            grad_own[:, columns] = grad[rows_total:]


def join_kernel(grad_query, grad_own, late, cos_wide, sin_wide, grad_raw):
    cos, sin = cos_wide[...], -sin_wide[...]
    query_width, kv_width = grad_query.shape[1], grad_own.shape[1] // 2
    grad_raw[:, :query_width] = grad_query[...]
    for start in range(0, kv_width, HEAD_DIM):
        columns = slice(start, start + HEAD_DIM)
        grad = grad_own[:, columns] + late[:, columns].astype(jnp.float32)
        grad_raw[:, query_width + start : query_width + start + HEAD_DIM] = turned(
            grad, cos, sin
        ).astype(jnp.bfloat16)
    values = grad_own[:, kv_width:] + late[:, kv_width:].astype(jnp.float32)
    used = query_width + 2 * kv_width
    grad_raw[:, query_width + kv_width : used] = values.astype(jnp.bfloat16)
    spare = grad_raw.shape[1] - used
    grad_raw[:, used:] = jnp.zeros((grad_raw.shape[0], spare), jnp.bfloat16)


def tiled_call(kernel, name, steps, in_specs, outs, args):
    return pl.pallas_call(
        kernel,
        grid=(steps,),
        out_shape=[jax.ShapeDtypeStruct(shape, kind) for shape, kind, _, _ in outs],
        in_specs=[pl.BlockSpec(block, index) for block, index in in_specs],
        out_specs=[pl.BlockSpec(block, index) for _, _, block, index in outs],
        compiler_params=pltpu.CompilerParams(vmem_limit_bytes=VMEM_BYTES),
        cost_estimate=SMALL_COST,
        name=name,
    )(*args)


def fixed(step):
    return (0, 0)


def by_row(step):
    return (step, 0)


def by_column(step):
    return (0, step)


def split_dot(left, mine, other):
    depth = mine.shape[0]
    first = jnp.dot(left[:, :depth], mine[...], preferred_element_type=jnp.float32)
    return first + jnp.dot(left[:, depth:], other[...], preferred_element_type=jnp.float32)


def project_kernel(start, left, mine, other, out):
    columns = slice(start, start + out.shape[1])
    depth = mine.shape[0]
    first = jnp.dot(left[:, :depth], mine[:, columns], preferred_element_type=jnp.float32)
    second = jnp.dot(left[:, depth:], other[:, columns], preferred_element_type=jnp.float32)
    out[...] = (first + second).astype(out.dtype)


def project(left, weights, start, columns, kind):
    mine, other = weights
    rows, depth = left.shape[0], mine.shape[0]
    tiled = start == 0 and columns % 512 == 0
    tile = 512 if tiled else columns
    block = (depth, tile) if tiled else mine.shape
    (out,) = tiled_call(
        functools.partial(project_kernel, start),
        "project",
        columns // tile,
        [(left.shape, fixed), (block, by_column), (block, by_column)],
        [((rows, columns), kind, (rows, tile), by_column)],
        (left, mine, other),
    )
    return out


def hidden_kernel(normed, gate_m, gate_o, up_m, up_o, hidden, gate_slope, up_slope):
    gate_pre = split_dot(normed, gate_m, gate_o)
    up_pre = split_dot(normed, up_m, up_o)
    sig_gate = 1.0 / (1.0 + jnp.exp(-gate_pre))
    silu_gate = gate_pre * sig_gate
    hidden[...] = (silu_gate * up_pre).astype(jnp.bfloat16)
    gate_slope[...] = up_pre * (sig_gate * (1.0 + gate_pre * (1.0 - sig_gate)))
    up_slope[...] = silu_gate


def hidden_units(normed, gate_weights, up_weights):
    rows = normed.shape[0]
    depth, columns = gate_weights[0].shape
    tile = 256
    outs = [
        ((rows, columns), kind, (rows, tile), by_column)
        for kind in (jnp.bfloat16, jnp.float32, jnp.float32)
    ]
    return tiled_call(
        hidden_kernel,
        "hidden_units",
        columns // tile,
        [(normed.shape, fixed)] + [((depth, tile), by_column)] * 4,
        outs,
        (normed, *gate_weights, *up_weights),
    )


def hidden_grad_kernel(cot, down_m, down_o, gate_slope, up_slope, gate_grad, up_grad):
    grad_hidden = split_dot(cot, down_m, down_o)
    gate_grad[...] = (grad_hidden * gate_slope[...]).astype(jnp.bfloat16)
    up_grad[...] = (grad_hidden * up_slope[...]).astype(jnp.bfloat16)


def hidden_grads(cot, down_weights, gate_slope, up_slope):
    rows = cot.shape[0]
    depth, columns = down_weights[0].shape
    tile = 256
    out = ((rows, columns), jnp.bfloat16, (rows, tile), by_column)
    return tiled_call(
        hidden_grad_kernel,
        "hidden_grads",
        columns // tile,
        [(cot.shape, fixed)]
        + [((depth, tile), by_column)] * 2
        + [((rows, tile), by_column)] * 2,
        [out] * 2,
        (cot, *down_weights, gate_slope, up_slope),
    )


def back_kernel(count, start, *refs):
    lefts, weights, outs = refs[:count], refs[count : 3 * count], refs[3 * count :]
    columns = slice(start, start + lefts[0].shape[1])
    sums = []
    for half in range(2):
        terms = [
            cols_dot(left[...], weights[2 * i + half][:, columns]) for i, left in enumerate(lefts)
        ]
        sums.append(sum(terms).astype(jnp.bfloat16))
    one, two = sums
    one_keep, one_send, two_keep, two_send = outs
    n = one.shape[0] // 4
    one_keep[:n, :], one_send[:n, :] = one[:n], one[n : 2 * n]
    one_keep[n:, :], one_send[n:, :] = one[2 * n : 3 * n], one[3 * n :]
    two_keep[...], two_send[...] = two[: 2 * n], two[2 * n :]


def project_back(lefts, weights, start=0):
    rows, width = lefts[0].shape
    depth = weights[0][0].shape[0]
    tile = 256
    flat = [half for pair in weights for half in pair]
    return tiled_call(
        functools.partial(back_kernel, len(lefts), start),
        "project_back",
        depth // tile,
        [((rows, width), fixed)] * len(lefts) + [((tile, flat[0].shape[1]), by_row)] * len(flat),
        [((rows // 2, depth), jnp.bfloat16, (rows // 2, tile), by_column)] * 4,
        (*lefts, *flat),
    )


def outer_kernel(left, left_other, right, right_other, out):
    first = rows_dot(left[...], right[...])
    out[...] = (first + rows_dot(left_other[...], right_other[...])).astype(jnp.bfloat16)


def outer(left, left_other, right, right_other, index):
    rows, width = left.shape[0], right.shape[1]
    depth = left_other.shape[1] // 2
    tile = 256 if width % 256 == 0 else width
    (out,) = tiled_call(
        outer_kernel,
        "outer",
        width // tile,
        [((rows, depth), lambda step: (0, index))] * 2 + [((rows, tile), by_column)] * 2,
        [((depth, width), jnp.bfloat16, (depth, tile), by_column)],
        (left, left_other, right, right_other),
    )
    return out


def norm_kernel(rows, gain, out):
    value = rows[...].astype(jnp.float32)
    scale = lax.rsqrt(jnp.mean(value * value, axis=1, keepdims=True) + norm_eps)
    out[...] = (value * scale * gain[...]).astype(jnp.bfloat16)


def norm_rows(rows, gain):
    count, width = rows.shape
    tile = count // 4
    (out,) = tiled_call(
        norm_kernel,
        "norm_rows",
        4,
        [((tile, width), by_row), ((1, width), fixed)],
        [((count, width), jnp.bfloat16, (tile, width), by_row)],
        (rows, gain.reshape(1, width)),
    )
    return out


def take_wide_kernel(own, from_near, from_tp, out, sems):
    n = own.shape[0]
    moves = [
        (own, pl.ds(0, n)),
        (from_tp.at[pl.ds(0, n), :], pl.ds(n, n)),
        (from_near, pl.ds(2 * n, n)),
        (from_tp.at[pl.ds(n, n), :], pl.ds(3 * n, n)),
    ]
    copies = [
        pltpu.make_async_copy(source, out.at[rows, :], sems.at[k])
        for k, (source, rows) in enumerate(moves)
    ]
    for copy in copies:
        copy.start()
    for copy in copies:
        copy.wait()


def take_wide(own, from_near, from_tp):
    return pl.pallas_call(
        take_wide_kernel,
        out_shape=jax.ShapeDtypeStruct((4 * own.shape[0], own.shape[1]), own.dtype),
        in_specs=[pl.BlockSpec(memory_space=pl.ANY)] * 3,
        out_specs=pl.BlockSpec(memory_space=pltpu.VMEM),
        scratch_shapes=[pltpu.SemaphoreType.DMA((4,))],
        compiler_params=pltpu.CompilerParams(vmem_limit_bytes=VMEM_BYTES),
        cost_estimate=SMALL_COST,
        name="take_wide",
    )(own, from_near, from_tp)


def rows_call(fn, name, where, steps, ins, outs):
    def kernel(where_ref, *refs):
        values = [ref[...].astype(jnp.float32) for ref in refs[: len(ins)]]
        for ref, value in zip(refs[len(ins) :], fn(*values)):
            ref[...] = value.astype(ref.dtype)

    def spec(rows, columns, place):
        return pl.BlockSpec((rows, columns), lambda step, ref: (place(step, ref), 0))

    return pl.pallas_call(
        kernel,
        grid_spec=pltpu.PrefetchScalarGridSpec(
            num_scalar_prefetch=1,
            grid=(steps,),
            in_specs=[spec(rows, array.shape[1], place) for array, rows, place in ins],
            out_specs=[spec(rows, shape[1], place) for shape, _, rows, place in outs],
        ),
        out_shape=[jax.ShapeDtypeStruct(shape, kind) for shape, kind, _, _ in outs],
        compiler_params=pltpu.CompilerParams(vmem_limit_bytes=VMEM_BYTES),
        cost_estimate=SMALL_COST,
        name=name,
    )(where, *[array for array, _, _ in ins])


def far_halves(where, own, from_x):
    rows, columns = own.shape[0] // 4, own.shape[1]
    keep, give = (lambda step, ref: 2 * ref[0] + step), (lambda step, ref: 2 - 2 * ref[0] + step)
    out = ((2 * rows, columns), jnp.bfloat16, rows, lambda step, ref: step)
    return rows_call(
        lambda a, b, c, d: (a + b, c + d),
        "far_halves",
        where,
        2,
        [(array, rows, place) for place in (keep, give) for array in (own, from_x)],
        [out, out],
    )


def near_halves(where, pair, from_far):
    rows, columns = pair.shape[0] // 2, pair.shape[1]
    keep, give = (lambda step, ref: ref[1]), (lambda step, ref: 1 - ref[1])
    out = ((rows, columns), jnp.bfloat16, rows, lambda step, ref: 0)
    return rows_call(
        lambda a, b, c, d: (a + b, c + d),
        "near_halves",
        where,
        1,
        [(array, rows, place) for place in (keep, give) for array in (pair, from_far)],
        [out, out],
    )


def join_halves_kernel(turn, where, own, received, *outs):
    first = where[1] == 0
    low_part = jnp.where(first, own[...], received[...]).astype(jnp.float32)
    high_part = jnp.where(first, received[...], own[...]).astype(jnp.float32)
    start = 0
    for out in outs:
        width = out.shape[0] if turn else out.shape[1]
        if len(outs) == 1:
            size = own.shape[1]
            rest = width - size
        else:
            size = rest = width // 2
        left, right = low_part[:, start : start + size], high_part[:, start : start + rest]
        if turn:
            out[:size, :] = left.T
            out[size:, :] = right.T
        else:
            out[:, :size] = left
            out[:, size:] = right
        start += size


def join_halves(where, own, received, widths, turn=False):
    rows = own.shape[0]
    shapes = [(width, rows) if turn else (rows, width) for width in widths]
    whole = pl.BlockSpec(memory_space=pltpu.VMEM)
    return pl.pallas_call(
        functools.partial(join_halves_kernel, turn),
        out_shape=[jax.ShapeDtypeStruct(shape, jnp.float32) for shape in shapes],
        in_specs=[pl.BlockSpec(memory_space=pltpu.SMEM), whole, whole],
        out_specs=[whole] * len(shapes),
        compiler_params=pltpu.CompilerParams(vmem_limit_bytes=VMEM_BYTES),
        cost_estimate=SMALL_COST,
        name="join_halves",
    )(where, own, received)


def split_halves_kernel(plan, where, *refs):
    arrays, pairs, other = refs[: len(plan)], refs[len(plan) : -1], refs[-1]
    rows = other.shape[0]
    first = where[1] == 0
    offset = 0
    filled = [0] * len(pairs)
    for index, (array, (target, size, turn)) in enumerate(zip(arrays, plan)):
        value = array[...]
        if turn:
            value = value.astype(jnp.float32).T.astype(jnp.bfloat16)
        low_part, high_part = value[:, :size], value[:, size:]
        missing = size - high_part.shape[1]
        if missing:
            high_part = jnp.concatenate(
                [high_part, jnp.zeros((rows, missing), jnp.bfloat16)], axis=1
            )
        start = filled[target]
        pair = pairs[target]
        pair[:rows, start : start + size] = jnp.where(first, low_part, high_part)
        other[:, offset + start : offset + start + size] = jnp.where(first, high_part, low_part)
        filled[target] = start + size
        if index + 1 == len(plan) or plan[index + 1][0] != target:
            spare = pair.shape[1] - filled[target]
            if spare:
                pair[:rows, filled[target] :] = jnp.zeros((rows, spare), jnp.bfloat16)
                end = offset + pair.shape[1]
                other[:, end - spare : end] = jnp.zeros((rows, spare), jnp.bfloat16)
            offset += pair.shape[1]


def split_halves(where, arrays, plan, widths):
    rows = D // 16
    whole = pl.BlockSpec(memory_space=pltpu.VMEM)
    return pl.pallas_call(
        functools.partial(split_halves_kernel, plan),
        out_shape=[jax.ShapeDtypeStruct((2 * rows, width), jnp.bfloat16) for width in widths]
        + [jax.ShapeDtypeStruct((rows, sum(widths)), jnp.bfloat16)],
        in_specs=[pl.BlockSpec(memory_space=pltpu.SMEM)] + [whole] * len(arrays),
        out_specs=[whole] * (len(widths) + 1),
        compiler_params=pltpu.CompilerParams(vmem_limit_bytes=VMEM_BYTES),
        cost_estimate=SMALL_COST,
        name="split_halves",
    )(where, *arrays)


def pair_kernel(first, second, out):
    n = first.shape[0]
    out[:n, :] = first[...]
    out[n:, :] = second[...]


def pair_rows(first, second):
    rows, columns = first.shape
    (out,) = dense_call(
        pair_kernel, "pair_rows", [((2 * rows, columns), first.dtype)], [], (first, second)
    )
    return out


def middle_kernel(one, got_one, two, got_two, next_one, next_two, sum_one, sum_two):
    n = sum_one.shape[0]
    for keep, got, later, total in (
        (one, got_one, next_one, sum_one),
        (two, got_two, next_two, sum_two),
    ):
        both = keep[...].astype(jnp.float32) + got[...].astype(jnp.float32)
        total[...] = both[:n]
        later[...] = both[n:].astype(jnp.bfloat16)


def scatter_middle(one, got_one, two, got_two):
    rows, columns = one.shape[0] // 2, one.shape[1]
    return dense_call(
        middle_kernel,
        "scatter_middle",
        [((rows, columns), jnp.bfloat16)] * 2 + [((rows, columns), jnp.float32)] * 2,
        [],
        (one, got_one, two, got_two),
    )


def summed(sum_one, sum_two, last_one, last_two):
    one = sum_one[...] + last_one[...].astype(jnp.float32)
    two = sum_two[...] + last_two[...].astype(jnp.float32)
    return jnp.concatenate([one, two], axis=1)


def store_halves(value, one, two):
    half = one.shape[1]
    one[...] = value[:, :half].astype(one.dtype)
    two[...] = value[:, half:].astype(two.dtype)


def residual_kernel(sum_one, sum_two, last_one, last_two, rows, gain, residual, one, two):
    value = rows[...].astype(jnp.float32) + summed(sum_one, sum_two, last_one, last_two)
    residual[...] = value
    scale = lax.rsqrt(jnp.mean(value * value, axis=1, keepdims=True) + norm_eps)
    store_halves(value * scale * gain[...], one, two)


def norm_grad(grad, value, gain):
    scale = lax.rsqrt(jnp.mean(value * value, axis=1, keepdims=True) + norm_eps)
    scaled = grad * gain
    inner = jnp.mean(scaled * value, axis=1, keepdims=True)
    gain_term = jnp.sum(grad * value * scale, axis=0, keepdims=True)
    return scale * scaled - value * (scale * scale * scale) * inner, gain_term


def residual_grad_kernel(
    sum_one, sum_two, last_one, last_two, residual, gain, cot, grad, gain_term, one, two
):
    back, term = norm_grad(summed(sum_one, sum_two, last_one, last_two), residual[...], gain[...])
    value = cot[...].astype(jnp.float32) + back
    grad[...] = value
    gain_term[...] = term
    store_halves(value, one, two)


def token_grad_kernel(
    sum_one, sum_two, last_one, last_two, rows, gain, grad_residual, grad, gain_term
):
    value = rows[...].astype(jnp.float32)
    back, term = norm_grad(summed(sum_one, sum_two, last_one, last_two), value, gain[...])
    grad[...] = grad_residual[...] + back
    gain_term[...] = term


def mixed_kernel(sum_one, sum_two, last_one, last_two, residual, mixed):
    total = residual[...] + summed(sum_one, sum_two, last_one, last_two)
    mixed[...] = total.astype(jnp.bfloat16)


def half_plan(
    tokens, doc_lengths, w_query, w_key, w_value, w_out, w_gate, w_up, w_down, norm_gains, cotangent
):
    fsdp_index = lax.axis_index("fsdp")
    seq_index = lax.axis_index("seq")
    tp_index = lax.axis_index("tp")
    near = seq_index % 2
    far = seq_index // 2
    local_rows = tokens.shape[0]
    group_rows = 4 * local_rows
    middle = D // 2
    quarter = D // 4
    block_rows = D // 16
    score_scale = 1.0 / math.sqrt(HEAD_DIM)

    def columns_in(value):
        return jnp.concatenate(
            [
                lax.dynamic_slice_in_dim(value, (fsdp_index ^ k) * quarter, quarter, 1)
                for k in (0, 2, 1, 3)
            ],
            axis=1,
        )

    def columns_out(value):
        pieces = []
        for block in range(4):
            k = fsdp_index ^ block
            place = (k // 2) + (k % 2) * 2
            pieces.append(lax.dynamic_slice_in_dim(value, place * quarter, quarter, 1))
        return jnp.concatenate(pieces, axis=1)

    def gather_first(one, two):
        return one, two, to_z(one, 1), to_tp(two)

    def gather_second(one, two, one_near, two_tp):
        one_far = to_tp(pair_rows(one, one_near))
        two_far = to_z(pair_rows(two, two_tp), 1)
        return one, two, one_near, one_far, two_tp, two_far

    def scatter_first(one_keep, one_send, two_keep, two_send):
        return one_keep, to_tp(one_send), two_keep, to_z(two_send, 1)

    def scatter_second(next_one, next_two, sum_one, sum_two):
        return sum_one, sum_two, to_z(next_one, 1), to_tp(next_two)

    where = jnp.stack([far, near]).astype(jnp.int32)
    query_width = w_query.shape[1] // 2
    key_width = w_key.shape[1] // 2
    query_heads = query_width // HEAD_DIM
    heads_width = -(-(query_width + 2 * key_width) // 128) * 128
    hidden_width = -(-(w_gate.shape[1] // 2) // 128) * 128
    row_shape = (local_rows, D)
    half_shape = (local_rows, middle)

    tokens_in = columns_in(tokens)
    cot_in = columns_in(cotangent)
    first_width = heads_width + query_width
    plan = ((0, query_width, False), (0, key_width, False), (0, key_width, False))
    spare = heads_width - query_width - 2 * key_width
    first_pair, first_other = split_halves(
        where,
        (w_query, w_key, w_value, jnp.zeros((block_rows, 2 * spare), jnp.bfloat16), w_out),
        (*plan, (0, spare, False), (0, query_width, True)),
        (first_width,),
    )
    gain_stack = norm_gains[None]
    gain_stack = jnp.concatenate([gain_stack, to_z(gain_stack, 1)], axis=0)
    first_near = to_z(first_other, 1)
    token_wait = gather_first(tokens_in[:, :middle], tokens_in[:, middle:])
    gain_far = to_z(hold(gain_stack, token_wait[2:]), 2)
    gain_stack = jnp.concatenate([gain_stack, gain_far], axis=0)
    first_pair = fill_rows(*hold((first_pair, first_near), gain_stack))
    first_far = to_z(first_pair, 2)
    token_wait = gather_second(*hold(token_wait, first_pair))
    gate_pair, gate_other = split_halves(
        where, (w_gate,), ((0, hidden_width, False),), (hidden_width,)
    )
    up_pair, up_other = split_halves(where, (w_up,), ((0, hidden_width, False),), (hidden_width,))
    down_pair, down_other = split_halves(
        where, (w_down,), ((0, hidden_width, True),), (hidden_width,)
    )
    gate_near = to_z(hold(gate_other, first_pair), 1)
    token_wait = hold(token_wait, gate_other, up_other, down_other)
    gain_plane = jnp.concatenate(
        [
            lax.dynamic_index_in_dim(gain_stack, seq_index ^ k, 0, keepdims=False)
            for k in range(4)
        ],
        axis=1,
    )
    gain_mine = jnp.concatenate([gain_plane, to_x(gain_plane)], axis=1)
    gains = float_of(jnp.concatenate([gain_mine, to_core(gain_mine)], axis=1))
    gain_one = gains[0:1]
    gain_two = gains[1:2]
    token_span = take_rows(*hold(token_wait, gains))

    row_ids = jnp.arange(local_rows, dtype=jnp.int32)
    own_positions = jnp.concatenate(
        [
            far * (2 * 2 * local_rows)
            + (near ^ i) * (2 * local_rows)
            + (tp_index ^ j) * local_rows
            + row_ids
            for i in range(2)
            for j in range(2)
        ]
    )
    cos_tab, sin_tab = rope_tables(own_positions)
    cos_wide = jnp.concatenate([cos_tab, cos_tab], axis=1)
    sin_wide = jnp.concatenate([-sin_tab, sin_tab], axis=1)
    key_positions = jnp.concatenate([own_positions - group_rows, own_positions])
    doc_ends = jnp.cumsum(doc_lengths[0])[: DOCS - 1]

    def doc_of(positions):
        return jnp.sum((positions[:, None] >= doc_ends[None, :]).astype(jnp.int32), axis=1)

    key_docs = jnp.where(key_positions >= 0, doc_of(key_positions), -1)
    query_ids = jnp.stack([doc_of(own_positions), own_positions // BLOCK])
    key_ids = jnp.stack([key_docs, key_positions // BLOCK], axis=1)

    gate_pair = fill_rows(*hold((gate_pair, gate_near), token_span))
    first_plane, first_mine = place_rows(*hold((first_pair, first_far), gate_pair), seq_index)
    first_x = to_x(first_plane)
    gate_far = to_z(hold(gate_pair, first_plane), 2)
    normed_one = norm_rows(hold(token_span, first_plane), gain_one)
    normed_other = to_core(normed_one[:, middle:])
    up_pair = fill_rows(up_pair, to_z(hold(up_other, first_plane), 1))
    down_pair = fill_rows(down_pair, to_z(hold(down_other, first_plane), 1))
    cot_first = gather_first(*hold((cot_in[:, :middle], cot_in[:, middle:]), up_pair))
    gate_plane, gate_mine = place_rows(
        *hold((gate_pair, gate_far), cot_first[2:], down_pair, normed_one), seq_index
    )
    first_mine = fill_rows(*hold((first_mine, first_x), gate_plane))
    first_weights = first_mine, to_core(first_mine)
    gate_x = to_x(hold(gate_plane, first_mine))
    up_far = to_z(hold(up_pair, gate_plane), 2)
    cot_wait = gather_second(*hold(cot_first, first_mine))
    raw = project(normed_one, first_weights, 0, heads_width, jnp.float32)
    query_rot, own_kv = dense_call(
        rope_kernel,
        "rope",
        [
            ((group_rows, query_width), jnp.bfloat16),
            ((group_rows, 2 * key_width), jnp.bfloat16),
        ],
        [],
        (raw, cos_wide, sin_wide),
    )
    cot_span = take_rows(*hold(cot_wait, own_kv))
    up_plane, up_mine = place_rows(*hold((up_pair, up_far), cot_span), seq_index)
    early_kv = lax.ppermute(hold(own_kv, up_plane), "seq", [(0, 2), (1, 3)])
    gate_mine = fill_rows(*hold((gate_mine, gate_x), up_plane))
    gate_weights = gate_mine, to_core(gate_mine)
    up_x = to_x(hold(up_plane, gate_mine))
    attended_low, log_total = dense_call(
        functools.partial(attend_kernel, score_scale),
        "attend",
        [
            ((group_rows, query_width), jnp.bfloat16),
            ((query_heads, group_rows), jnp.float32),
        ],
        [pltpu.VMEM((2 * group_rows, group_rows // 2), jnp.float32)],
        (query_rot, early_kv, own_kv, query_ids, key_ids),
    )
    attended_other = to_core(attended_low)
    down_far = to_z(hold(down_pair, log_total), 2)
    branch = scatter_first(
        *project_back([attended_low], [first_weights], heads_width)
    )
    branch = scatter_middle(*branch)
    branch = scatter_second(*branch)
    down_plane, down_mine = place_rows(*hold((down_pair, down_far), branch[:2]), seq_index)
    up_mine = fill_rows(*hold((up_mine, up_x), down_plane))
    up_weights = up_mine, to_core(up_mine)
    down_x = to_x(hold(down_plane, up_mine))
    residual, two_one, two_two = dense_call(
        residual_kernel,
        "residual",
        [(row_shape, jnp.float32)] + [(half_shape, jnp.bfloat16)] * 2,
        [],
        (*hold(branch, up_mine), tokens_in, gain_two),
    )
    two_wait = gather_second(*gather_first(two_one, two_two))
    span_two = take_rows(*two_wait)
    span_other = to_core(span_two[:, middle:])
    cot_other = to_core(hold(cot_span[:, middle:], log_total))
    hidden_low, gate_slope, up_slope = hidden_units(span_two, gate_weights, up_weights)
    hidden_other = to_core(hidden_low)
    down_mine = fill_rows(*hold((down_mine, down_x), hidden_low))
    down_weights = down_mine, to_core(down_mine)

    down_parts = hold((cot_span, cot_other, hidden_low, hidden_other), down_mine)
    down_give = outer(*down_parts, 1)
    down_back = to_x(down_give)
    mlp_parts = project_back([hold(hidden_low, down_give)], [down_weights])
    grad_gate_pre, grad_up_pre = hidden_grads(
        hold(cot_span, mlp_parts), down_weights, gate_slope, up_slope
    )
    gate_other = to_core(grad_gate_pre)
    up_other = to_core(grad_up_pre)
    branch_mlp = scatter_first(*mlp_parts)
    back_parts = project_back(
        [grad_gate_pre, grad_up_pre], [gate_weights, up_weights]
    )
    branch_mlp = scatter_middle(*hold(branch_mlp, back_parts))
    normed_back = scatter_first(*hold(back_parts, branch_mlp))
    down_keep = outer(*hold(down_parts, branch_mlp), 0)
    gate_parts = hold((span_two, span_other, grad_gate_pre, gate_other), down_keep)
    gate_give = outer(*gate_parts, 1)
    down_keep, down_give = far_halves(where, *hold((down_keep, down_back), gate_give))
    down_far = to_z(down_give, 2)
    gate_back = to_x(hold(gate_give, down_give))
    normed_back = scatter_second(*scatter_middle(*hold(normed_back, down_give)))
    gate_keep = outer(*hold(gate_parts, normed_back[:2]), 0)
    up_parts = hold((span_two, span_other, grad_up_pre, up_other), gate_keep)
    up_give = outer(*up_parts, 1)
    up_keep = outer(*hold(up_parts, up_give), 0)
    grad_residual, gain_two_term, grad_one, grad_two = dense_call(
        residual_grad_kernel,
        "residual_grad",
        [(row_shape, jnp.float32), ((1, D), jnp.float32)] + [(half_shape, jnp.bfloat16)] * 2,
        [],
        (*hold(normed_back, up_keep), residual, gain_two, cot_in),
    )
    grad_wait = gather_first(grad_one, grad_two)
    down_own, down_other = near_halves(where, *hold((down_keep, down_far), grad_one))
    gate_keep, gate_give = far_halves(where, *hold((gate_keep, gate_back), down_other))
    gate_far = to_z(gate_give, 2)
    up_back = to_x(hold(up_give, gate_give))
    grad_wait = gather_second(*hold(grad_wait, gate_give))
    gate_own, gate_other = near_halves(where, *hold((gate_keep, gate_far), grad_wait[2::2]))
    up_keep, up_give = far_halves(where, *hold((up_keep, up_back), gate_other))
    up_far = to_z(up_give, 2)
    grad_span = take_rows(*hold(grad_wait, up_give))
    down_near = to_z(hold(down_other, grad_span), 1)
    gate_near = to_z(hold(gate_other, grad_span), 1)
    span_grad_other = to_core(grad_span[:, middle:])
    grad_attended = project(grad_span, first_weights, heads_width, query_width, jnp.bfloat16)
    grad_query, grad_early, grad_own = dense_call(
        functools.partial(attend_back_kernel, score_scale),
        "attend_back",
        [
            ((group_rows, query_width), jnp.bfloat16),
            ((group_rows, 2 * key_width), jnp.bfloat16),
            ((group_rows, 2 * key_width), jnp.float32),
        ],
        [
            pltpu.VMEM((2 * group_rows, group_rows), jnp.float32),
            pltpu.VMEM((2 * group_rows, GROUP * group_rows), jnp.bfloat16),
            pltpu.VMEM((2 * group_rows, GROUP * group_rows), jnp.bfloat16),
        ],
        (
            query_rot,
            early_kv,
            own_kv,
            query_ids,
            key_ids,
            log_total,
            grad_attended,
            cos_wide,
            sin_wide,
        ),
    )
    up_own, up_other = near_halves(where, *hold((up_keep, up_far), grad_early))
    late_kv = lax.ppermute(hold(grad_early, up_other), "seq", [(2, 0), (3, 1)])
    out_parts = hold((grad_span, span_grad_other, attended_low, attended_other), up_other)
    up_near = to_z(hold(up_other, late_kv), 1)
    out_give = outer(*out_parts, 1)
    out_back = to_x(out_give)
    out_keep = outer(*out_parts, 0)
    (grad_raw,) = dense_call(
        join_kernel,
        "join",
        [((group_rows, heads_width), jnp.bfloat16)],
        [],
        (grad_query, grad_own, hold(late_kv, out_give, out_keep, down_near, gate_near), cos_wide, sin_wide),
    )
    raw_other = to_core(grad_raw)
    first_parts = project_back([grad_raw], [first_weights])
    first_back = scatter_first(*first_parts)
    heads_parts = hold((normed_one, normed_other, grad_raw, raw_other), first_parts, up_near)
    heads_give = outer(*heads_parts, 1)
    heads_back = to_x(heads_give)
    out_keep, out_give = far_halves(where, *hold((out_keep, out_back), heads_give))
    out_far = to_z(out_give, 2)
    heads_keep = outer(*hold(heads_parts, out_give), 0)
    units = w_gate.shape[1]
    first_back = scatter_middle(*hold(first_back, heads_keep, heads_give))
    heads_keep, heads_give = far_halves(where, *hold((heads_keep, heads_back), first_back))
    heads_far = to_z(heads_give, 2)
    first_back = scatter_second(*hold(first_back, heads_give))
    out_own, out_other = near_halves(where, *hold((out_keep, out_far), first_back[:2]))
    out_near = to_z(out_other, 1)
    grad_rows, gain_one_term = dense_call(
        token_grad_kernel,
        "token_grad",
        [(row_shape, jnp.float32), ((1, D), jnp.float32)],
        [],
        (*hold(first_back, out_other), tokens_in, gain_one, grad_residual),
    )
    gain_rows = jnp.concatenate([gain_one_term, gain_two_term], axis=0)
    (grad_down,) = join_halves(where, *hold((down_own, down_near), grad_rows), (units,), True)
    (grad_gate,) = join_halves(where, *hold((gate_own, gate_near), grad_down), (units,))
    (grad_up,) = join_halves(where, *hold((up_own, up_near), grad_gate), (units,))
    heads_own, heads_other = near_halves(where, *hold((heads_keep, heads_far), grad_up))
    heads_near = to_z(heads_other, 1)
    gain_rows = hold(gain_rows, heads_other)
    gain_rows = gain_rows[:, :middle] + to_core(gain_rows[:, middle:])
    gain_rows = gain_rows[:, :quarter] + to_x(gain_rows[:, quarter:])
    gain_rows = gain_rows + to_tp(gain_rows)
    branch_mlp = scatter_second(*hold(branch_mlp, heads_other))
    (grad_out,) = join_halves(
        where, *hold((out_own, out_near), gain_rows), (w_out.shape[0],), True
    )
    (mixed,) = dense_call(
        mixed_kernel,
        "mixed",
        [(row_shape, jnp.bfloat16)],
        [],
        (*hold(branch_mlp, grad_out), residual),
    )
    mixed_out = columns_out(mixed)
    grad_tokens = columns_out(grad_rows)
    gain_blocks = gain_rows.reshape(2, 4, block_rows)
    gain_pair = [
        lax.dynamic_index_in_dim(gain_blocks, seq_index ^ k, 1, keepdims=False) for k in range(4)
    ]
    gain_half = jnp.stack(gain_pair[:2]) + to_z(jnp.stack(gain_pair[2:]), 2)
    gain_grads = gain_half[0] + to_z(gain_half[1], 1)
    grad_query_w, grad_key_w, grad_value_w = join_halves(
        where,
        *(heads_own, heads_near),
        (2 * query_width, 2 * key_width, 2 * key_width),
    )
    return (
        mixed_out,
        grad_tokens,
        grad_query_w,
        grad_key_w,
        grad_value_w,
        grad_out,
        grad_gate,
        grad_up,
        grad_down,
        gain_grads,
    )


def solution(mesh):
    halves = mesh.shape["seq"] == 4 and mesh.shape["tp"] == 2 and mesh.shape["fsdp"] == 4
    plan = half_plan if halves else per_device
    in_specs = (
        P(("fsdp", "seq", "tp"), None),
        P("fsdp", None),
        P(("fsdp", "seq"), "tp"),
        P(("fsdp", "seq"), "tp"),
        P(("fsdp", "seq"), "tp"),
        P("tp", ("fsdp", "seq")),
        P(("fsdp", "seq"), "tp"),
        P(("fsdp", "seq"), "tp"),
        P("tp", ("fsdp", "seq")),
        P(None, ("fsdp", "seq")),
        P(("fsdp", "seq", "tp"), None),
    )
    out_specs = (
        P(("fsdp", "seq", "tp"), None),
        P(("fsdp", "seq", "tp"), None),
        P(("fsdp", "seq"), "tp"),
        P(("fsdp", "seq"), "tp"),
        P(("fsdp", "seq"), "tp"),
        P("tp", ("fsdp", "seq")),
        P(("fsdp", "seq"), "tp"),
        P(("fsdp", "seq"), "tp"),
        P("tp", ("fsdp", "seq")),
        P(None, ("fsdp", "seq")),
    )
    return jax.shard_map(
        plan, mesh=mesh, in_specs=in_specs, out_specs=out_specs, check_vma=False
    )
```

```python
import functools
import math

import jax
import jax.numpy as jnp
from jax import lax
from jax.experimental import pallas as pl
from jax.experimental.pallas import tpu as pltpu
from jax.sharding import PartitionSpec as P

D = 2560
HEAD_DIM = 80
BLOCK = 256
DOCS = 3
GROUP = 4


norm_eps = 1e-05
rope_base = 10000.0
mask_fill = -1000000000.0


def rope_tables(positions):
    half_dim = HEAD_DIM // 2
    freq_row = rope_base ** (-jnp.arange(half_dim, dtype=jnp.float32) * 2.0 / HEAD_DIM)
    angles = positions.astype(jnp.float32)[:, None] * freq_row[None, :]
    return (jnp.cos(angles), jnp.sin(angles))


def rotate(values, cos_tab, sin_tab):
    half_dim = HEAD_DIM // 2
    first_half = values[..., :half_dim]
    second_half = values[..., half_dim:]
    cos_wide = cos_tab[:, None, :]
    sin_wide = sin_tab[:, None, :]
    return jnp.concatenate(
        [
            first_half * cos_wide - second_half * sin_wide,
            second_half * cos_wide + first_half * sin_wide,
        ],
        axis=-1,
    )


def document_ids(lengths, positions):
    doc_ends = jnp.cumsum(lengths)
    return jnp.sum((positions[:, None] >= doc_ends[None, : DOCS - 1]).astype(jnp.int32), axis=1)


def rms_scale(row_values):
    return lax.rsqrt(jnp.mean(row_values * row_values, axis=-1, keepdims=True) + norm_eps)


def per_device(
    tokens, doc_lengths, w_query, w_key, w_value, w_out, w_gate, w_up, w_down, norm_gains, cotangent
):
    tp_count = lax.axis_size("tp")
    seq_count = lax.axis_size("seq")
    tp_index = lax.axis_index("tp")
    seq_index = lax.axis_index("seq")
    local_rows = tokens.shape[0]
    span_len = local_rows * tp_count
    seq_length = span_len * seq_count
    score_scale = 1.0 / math.sqrt(HEAD_DIM)
    key_step = math.gcd(512, seq_length)
    gathered = (
        lax.all_gather(w_query, ("fsdp", "seq"), axis=0, tiled=True),
        lax.all_gather(w_key, ("fsdp", "seq"), axis=0, tiled=True),
        lax.all_gather(w_value, ("fsdp", "seq"), axis=0, tiled=True),
        lax.all_gather(w_out, ("fsdp", "seq"), axis=1, tiled=True),
        lax.all_gather(w_gate, ("fsdp", "seq"), axis=0, tiled=True),
        lax.all_gather(w_up, ("fsdp", "seq"), axis=0, tiled=True),
        lax.all_gather(w_down, ("fsdp", "seq"), axis=1, tiled=True),
        lax.all_gather(norm_gains, ("fsdp", "seq"), axis=1, tiled=True),
    )
    query_full, key_full, value_full, out_full, gate_full, up_full, down_full, gains_low = gathered
    gain_one = gains_low[0].astype(jnp.float32)
    gain_two = gains_low[1].astype(jnp.float32)
    query_heads = query_full.shape[1] // HEAD_DIM
    kv_local = key_full.shape[1] // HEAD_DIM
    span_in = lax.all_gather(tokens, "tp", axis=0, tiled=True)
    span_float = span_in.astype(jnp.float32)
    inv_one = rms_scale(span_float)
    normed_one = (span_float * inv_one * gain_one).astype(jnp.bfloat16)
    span_start = seq_index * span_len
    positions = span_start + jnp.arange(span_len, dtype=jnp.int32)
    cos_tab, sin_tab = rope_tables(positions)
    query_raw = jnp.dot(normed_one, query_full, preferred_element_type=jnp.float32).reshape(
        span_len, query_heads, HEAD_DIM
    )
    key_raw = jnp.dot(normed_one, key_full, preferred_element_type=jnp.float32).reshape(
        span_len, kv_local, HEAD_DIM
    )
    value_raw = jnp.dot(normed_one, value_full, preferred_element_type=jnp.float32).reshape(
        span_len, kv_local, HEAD_DIM
    )
    query_rot = rotate(query_raw, cos_tab, sin_tab).astype(jnp.bfloat16)
    key_rot = rotate(key_raw, cos_tab, sin_tab).astype(jnp.bfloat16)
    value_low = value_raw.astype(jnp.bfloat16)
    query_group = query_rot.reshape(span_len, kv_local, GROUP, HEAD_DIM)
    key_all, value_all = (
        lax.all_gather(key_rot, "seq", axis=0, tiled=True),
        lax.all_gather(value_low, "seq", axis=0, tiled=True),
    )
    key_positions = jnp.arange(seq_length, dtype=jnp.int32)
    doc_keys = document_ids(doc_lengths[0], key_positions)
    doc_query = lax.dynamic_slice_in_dim(doc_keys, span_start, span_len, 0)
    key_blocks = key_positions // BLOCK
    query_block = positions // BLOCK
    blocks_used = (span_start + span_len + key_step - 1) // key_step
    stat_shape = (kv_local, GROUP, span_len)
    head_shape = (span_len, kv_local, GROUP, HEAD_DIM)

    def masked_scores(block_index):
        key_start = block_index * key_step
        key_part = lax.dynamic_slice_in_dim(key_all, key_start, key_step, 0)
        scores = (
            jnp.einsum("ckgd,nkd->kgcn", query_group, key_part, preferred_element_type=jnp.float32)
            * score_scale
        )
        block_part = lax.dynamic_slice_in_dim(key_blocks, key_start, key_step, 0)
        doc_part = lax.dynamic_slice_in_dim(doc_keys, key_start, key_step, 0)
        allowed = (block_part[None, :] <= query_block[:, None]) & (
            doc_part[None, :] == doc_query[:, None]
        )
        return (jnp.where(allowed[None, None], scores, mask_fill), key_start, key_part)

    def total_step(block_index, carry):
        row_max, row_sum = carry
        scores = masked_scores(block_index)[0]
        new_max = jnp.maximum(row_max, jnp.max(scores, axis=-1))
        row_sum = row_sum * jnp.exp(row_max - new_max) + jnp.sum(
            jnp.exp(scores - new_max[..., None]), axis=-1
        )
        return (new_max, row_sum)

    row_max, row_sum = lax.fori_loop(
        0,
        blocks_used,
        total_step,
        (jnp.full(stat_shape, mask_fill, jnp.float32), jnp.zeros(stat_shape, jnp.float32)),
    )
    log_total = row_max + jnp.log(row_sum)

    def out_step(block_index, running):
        scores, key_start, key_part = masked_scores(block_index)
        attn_prob = jnp.exp(scores - log_total[..., None]).astype(jnp.bfloat16)
        value_part = lax.dynamic_slice_in_dim(value_all, key_start, key_step, 0)
        return running + jnp.einsum(
            "kgcn,nkd->ckgd", attn_prob, value_part, preferred_element_type=jnp.float32
        )

    attended = lax.fori_loop(0, blocks_used, out_step, jnp.zeros(head_shape, jnp.float32))
    attended_low = attended.reshape(span_len, query_heads * HEAD_DIM).astype(jnp.bfloat16)
    attn_branch = lax.psum_scatter(
        jnp.dot(attended_low, out_full, preferred_element_type=jnp.float32).astype(jnp.bfloat16),
        "tp",
        scatter_dimension=0,
        tiled=True,
    ).astype(jnp.float32)
    token_rows = tokens.astype(jnp.float32)
    residual = token_rows + attn_branch
    inv_two = rms_scale(residual)
    normed_two = (residual * inv_two * gain_two).astype(jnp.bfloat16)
    span_two = lax.all_gather(normed_two, "tp", axis=0, tiled=True)
    gate_pre = jnp.dot(span_two, gate_full, preferred_element_type=jnp.float32)
    up_pre = jnp.dot(span_two, up_full, preferred_element_type=jnp.float32)
    sig_gate = jax.nn.sigmoid(gate_pre)
    silu_gate = gate_pre * sig_gate
    hidden_low = (silu_gate * up_pre).astype(jnp.bfloat16)
    mlp_branch = lax.psum_scatter(
        jnp.dot(hidden_low, down_full, preferred_element_type=jnp.float32).astype(jnp.bfloat16),
        "tp",
        scatter_dimension=0,
        tiled=True,
    ).astype(jnp.float32)
    mixed_out = (residual + mlp_branch).astype(jnp.bfloat16)
    cot_span = lax.all_gather(cotangent, "tp", axis=0, tiled=True)
    grad_down_w = jnp.einsum("cf,cd->fd", hidden_low, cot_span, preferred_element_type=jnp.float32)
    grad_hidden = jnp.einsum("cd,fd->cf", cot_span, down_full, preferred_element_type=jnp.float32)
    grad_gate_pre = (
        grad_hidden * up_pre * (sig_gate * (1.0 + gate_pre * (1.0 - sig_gate)))
    ).astype(jnp.bfloat16)
    grad_up_pre = (grad_hidden * silu_gate).astype(jnp.bfloat16)
    grad_gate_w = jnp.einsum(
        "cd,cf->df", span_two, grad_gate_pre, preferred_element_type=jnp.float32
    )
    grad_up_w = jnp.einsum("cd,cf->df", span_two, grad_up_pre, preferred_element_type=jnp.float32)
    grad_normed_two = lax.psum_scatter(
        (
            jnp.einsum("cf,df->cd", grad_gate_pre, gate_full, preferred_element_type=jnp.float32)
            + jnp.einsum("cf,df->cd", grad_up_pre, up_full, preferred_element_type=jnp.float32)
        ).astype(jnp.bfloat16),
        "tp",
        scatter_dimension=0,
        tiled=True,
    ).astype(jnp.float32)
    gain_two_term = jnp.sum(grad_normed_two * residual * inv_two, axis=0)
    scaled_two = grad_normed_two * gain_two
    grad_residual = (
        cotangent.astype(jnp.float32)
        + inv_two * scaled_two
        - residual
        * (inv_two * inv_two * inv_two)
        * jnp.mean(scaled_two * residual, axis=-1, keepdims=True)
    )
    grad_span = lax.all_gather(grad_residual.astype(jnp.bfloat16), "tp", axis=0, tiled=True)
    grad_out_w = jnp.einsum(
        "ce,cd->ed", attended_low, grad_span, preferred_element_type=jnp.float32
    )
    grad_attended = (
        jnp.einsum("cd,ed->ce", grad_span, out_full, preferred_element_type=jnp.float32)
        .astype(jnp.bfloat16)
        .reshape(head_shape)
    )

    def prob_grads(block_index):
        scores, key_start, key_part = masked_scores(block_index)
        probs_full = jnp.exp(scores - log_total[..., None])
        value_part = lax.dynamic_slice_in_dim(value_all, key_start, key_step, 0)
        grad_prob = jnp.einsum(
            "ckgd,nkd->kgcn", grad_attended, value_part, preferred_element_type=jnp.float32
        )
        return (probs_full, grad_prob, key_start, key_part)

    def delta_step(block_index, running):
        grads_here = prob_grads(block_index)
        return running + jnp.sum(grads_here[0] * grads_here[1], axis=-1)

    row_delta = lax.fori_loop(0, blocks_used, delta_step, jnp.zeros(stat_shape, jnp.float32))

    def grad_step(block_index, carry):
        query_acc, key_acc, value_acc = carry
        probs_full, grad_prob, key_start, key_part = prob_grads(block_index)
        grad_scores = (probs_full * (grad_prob - row_delta[..., None])).astype(jnp.bfloat16)
        query_acc = query_acc + jnp.einsum(
            "kgcn,nkd->ckgd", grad_scores, key_part, preferred_element_type=jnp.float32
        )
        key_term = (
            jnp.einsum(
                "kgcn,ckgd->nkd", grad_scores, query_group, preferred_element_type=jnp.float32
            )
            * score_scale
        )
        value_term = jnp.einsum(
            "kgcn,ckgd->nkd",
            probs_full.astype(jnp.bfloat16),
            grad_attended,
            preferred_element_type=jnp.float32,
        )
        key_old = lax.dynamic_slice_in_dim(key_acc, key_start, key_step, 0)
        value_old = lax.dynamic_slice_in_dim(value_acc, key_start, key_step, 0)
        key_acc = lax.dynamic_update_slice_in_dim(key_acc, key_old + key_term, key_start, 0)
        value_acc = lax.dynamic_update_slice_in_dim(value_acc, value_old + value_term, key_start, 0)
        return (query_acc, key_acc, value_acc)

    kv_zeros = jnp.zeros((seq_length, kv_local, HEAD_DIM), jnp.float32)
    query_acc, key_acc, value_acc = lax.fori_loop(
        0, blocks_used, grad_step, (jnp.zeros(head_shape, jnp.float32), kv_zeros, kv_zeros)
    )
    key_own, value_own = (
        lax.psum_scatter(
            key_acc.astype(jnp.bfloat16), "seq", scatter_dimension=0, tiled=True
        ).astype(jnp.float32),
        lax.psum_scatter(
            value_acc.astype(jnp.bfloat16), "seq", scatter_dimension=0, tiled=True
        ).astype(jnp.float32),
    )
    grad_query_rot = (query_acc * score_scale).reshape(span_len, query_heads, HEAD_DIM)
    grad_query_raw = (
        rotate(grad_query_rot, cos_tab, -sin_tab)
        .reshape(span_len, query_heads * HEAD_DIM)
        .astype(jnp.bfloat16)
    )
    grad_key_raw = (
        rotate(key_own, cos_tab, -sin_tab)
        .reshape(span_len, kv_local * HEAD_DIM)
        .astype(jnp.bfloat16)
    )
    grad_value_raw = value_own.reshape(span_len, kv_local * HEAD_DIM).astype(jnp.bfloat16)
    grad_query_w = jnp.einsum(
        "cd,ce->de", normed_one, grad_query_raw, preferred_element_type=jnp.float32
    )
    grad_key_w = jnp.einsum(
        "cd,ce->de", normed_one, grad_key_raw, preferred_element_type=jnp.float32
    )
    grad_value_w = jnp.einsum(
        "cd,ce->de", normed_one, grad_value_raw, preferred_element_type=jnp.float32
    )
    normed_part = jnp.einsum(
        "ce,de->cd", grad_query_raw, query_full, preferred_element_type=jnp.float32
    )
    normed_part = normed_part + jnp.einsum(
        "ce,de->cd", grad_key_raw, key_full, preferred_element_type=jnp.float32
    )
    normed_part = normed_part + jnp.einsum(
        "ce,de->cd", grad_value_raw, value_full, preferred_element_type=jnp.float32
    )
    gain_one_term = jnp.sum(normed_part * span_float * inv_one, axis=0)
    gain_block = jnp.broadcast_to(jnp.stack([gain_one_term, gain_two_term])[None], (tp_count, 2, D))
    grad_normed_one, gains_summed = (
        lax.psum_scatter(
            normed_part.astype(jnp.bfloat16), "tp", scatter_dimension=0, tiled=True
        ).astype(jnp.float32),
        lax.psum_scatter(
            gain_block.astype(jnp.bfloat16), "tp", scatter_dimension=0, tiled=True
        ).astype(jnp.float32),
    )
    gains_total = gains_summed[0]
    inv_rows = lax.dynamic_slice_in_dim(inv_one, tp_index * local_rows, local_rows, 0)
    scaled_one = grad_normed_one * gain_one
    grad_tokens = (
        grad_residual
        + inv_rows * scaled_one
        - token_rows
        * (inv_rows * inv_rows * inv_rows)
        * jnp.mean(scaled_one * token_rows, axis=-1, keepdims=True)
    )
    summed = (
        lax.psum_scatter(
            grad_query_w.astype(jnp.bfloat16), ("fsdp", "seq"), scatter_dimension=0, tiled=True
        ).astype(jnp.float32),
        lax.psum_scatter(
            grad_key_w.astype(jnp.bfloat16), ("fsdp", "seq"), scatter_dimension=0, tiled=True
        ).astype(jnp.float32),
        lax.psum_scatter(
            grad_value_w.astype(jnp.bfloat16), ("fsdp", "seq"), scatter_dimension=0, tiled=True
        ).astype(jnp.float32),
        lax.psum_scatter(
            grad_out_w.astype(jnp.bfloat16), ("fsdp", "seq"), scatter_dimension=1, tiled=True
        ).astype(jnp.float32),
        lax.psum_scatter(
            grad_gate_w.astype(jnp.bfloat16), ("fsdp", "seq"), scatter_dimension=0, tiled=True
        ).astype(jnp.float32),
        lax.psum_scatter(
            grad_up_w.astype(jnp.bfloat16), ("fsdp", "seq"), scatter_dimension=0, tiled=True
        ).astype(jnp.float32),
        lax.psum_scatter(
            grad_down_w.astype(jnp.bfloat16), ("fsdp", "seq"), scatter_dimension=1, tiled=True
        ).astype(jnp.float32),
        lax.psum_scatter(
            gains_total.astype(jnp.bfloat16), ("fsdp", "seq"), scatter_dimension=1, tiled=True
        ).astype(jnp.float32),
    )
    return (
        mixed_out,
        grad_tokens,
        summed[0],
        summed[1],
        summed[2],
        summed[3],
        summed[4],
        summed[5],
        summed[6],
        summed[7],
    )


VMEM_BYTES = 48 * 1024 * 1024
SMALL_COST = pl.CostEstimate(flops=1024, bytes_accessed=4096, transcendentals=0)


def to_core(value):
    return lax.ppermute(value, "fsdp", [(i, i ^ 1) for i in range(4)])


def to_x(value):
    return lax.ppermute(value, "fsdp", [(i, i ^ 2) for i in range(4)])


def to_z(value, step):
    return lax.ppermute(value, "seq", [(i, i ^ step) for i in range(4)])


def to_tp(value):
    return lax.ppermute(value, "tp", [(0, 1), (1, 0)])


def hold(value, *events):
    return lax.optimization_barrier((value, events))[0]


def float_of(value):
    return value.astype(jnp.float32)


def low_of(value):
    return value.astype(jnp.bfloat16)


def rows_dot(left, right):
    return lax.dot_general(left, right, (((0,), (0,)), ((), ())), preferred_element_type=jnp.float32)


def cols_dot(left, right):
    return lax.dot_general(left, right, (((1,), (1,)), ((), ())), preferred_element_type=jnp.float32)


def place_kernel(rows, place, pair, pair_far, plane, mine, held, read_sems, sems):
    reads = [
        pltpu.make_async_copy(
            (pair, pair_far)[k // 2].at[pl.ds((k % 2) * rows, rows), :], held.at[k], read_sems.at[k]
        )
        for k in range(4)
    ]
    for copy in reads:
        copy.start()
    writes = []
    for k, read in enumerate(reads):
        read.wait()
        start = pl.multiple_of((place[0] ^ k) * rows, 16)
        for i, target in enumerate((plane, mine)):
            write = pltpu.make_async_copy(
                held.at[k], target.at[pl.ds(start, rows), :], sems.at[2 * k + i]
            )
            write.start()
            writes.append(write)
    for write in writes:
        write.wait()


def place_rows(pair, pair_far, place):
    rows, columns = pair.shape[0] // 2, pair.shape[1]
    anywhere = pl.BlockSpec(memory_space=pl.ANY)
    return pl.pallas_call(
        lambda *refs: place_kernel(rows, *refs),
        out_shape=(
            jax.ShapeDtypeStruct((4 * rows, columns), jnp.bfloat16),
            jax.ShapeDtypeStruct((8 * rows, columns), jnp.bfloat16),
        ),
        in_specs=[pl.BlockSpec(memory_space=pltpu.SMEM)] + [anywhere] * 2,
        out_specs=(anywhere, anywhere),
        scratch_shapes=[
            pltpu.VMEM((4, rows, columns), jnp.bfloat16),
            pltpu.SemaphoreType.DMA((4,)),
            pltpu.SemaphoreType.DMA((8,)),
        ],
        cost_estimate=SMALL_COST,
        name="place_rows",
    )(place.reshape(1), pair, pair_far)


def fill_kernel(rows, part, start, across, first, mine, held, read_sems, sems):
    columns = pl.ds(start, mine.shape[1])
    reads = [
        pltpu.make_async_copy(
            across.at[pl.ds(k * part, part), columns], held.at[k], read_sems.at[k]
        )
        for k in range(rows // part)
    ]
    for copy in reads:
        copy.start()
    writes = []
    for k, read in enumerate(reads):
        read.wait()
        write = pltpu.make_async_copy(
            held.at[k], mine.at[pl.ds(rows + k * part, part), :], sems.at[k]
        )
        write.start()
        writes.append(write)
    for write in writes:
        write.wait()


def fill_rows(mine, across, start=0):
    rows, columns = across.shape[0], mine.shape[1]
    part = 128 if rows % 128 == 0 else 32
    anywhere = pl.BlockSpec(memory_space=pl.ANY)
    return pl.pallas_call(
        lambda *refs: fill_kernel(rows, part, start, *refs),
        out_shape=jax.ShapeDtypeStruct(mine.shape, mine.dtype),
        in_specs=[anywhere] * 2,
        out_specs=anywhere,
        scratch_shapes=[
            pltpu.VMEM((rows // part, part, columns), jnp.bfloat16),
            pltpu.SemaphoreType.DMA((rows // part,)),
            pltpu.SemaphoreType.DMA((rows // part,)),
        ],
        input_output_aliases={1: 0},
        cost_estimate=SMALL_COST,
        name="fill_rows",
    )(across, mine)


def take_rows_kernel(one, two, one_near, one_far, two_tp, two_far, out, sems):
    n, half = one.shape
    left, right = pl.ds(0, half), pl.ds(half, half)
    moves = [
        (one, pl.ds(0, n), left),
        (two, pl.ds(0, n), right),
        (one_near, pl.ds(2 * n, n), left),
        (one_far.at[pl.ds(0, n), :], pl.ds(n, n), left),
        (one_far.at[pl.ds(n, n), :], pl.ds(3 * n, n), left),
        (two_tp, pl.ds(n, n), right),
        (two_far, pl.ds(2 * n, 2 * n), right),
    ]
    copies = [
        pltpu.make_async_copy(source, out.at[rows, columns], sems.at[k])
        for k, (source, rows, columns) in enumerate(moves)
    ]
    for copy in copies:
        copy.start()
    for copy in copies:
        copy.wait()


def take_rows(*pieces):
    rows, half = pieces[0].shape
    return pl.pallas_call(
        take_rows_kernel,
        out_shape=jax.ShapeDtypeStruct((4 * rows, 2 * half), pieces[0].dtype),
        in_specs=[pl.BlockSpec(memory_space=pl.ANY)] * 6,
        out_specs=pl.BlockSpec(memory_space=pltpu.VMEM),
        scratch_shapes=[pltpu.SemaphoreType.DMA((7,))],
        compiler_params=pltpu.CompilerParams(vmem_limit_bytes=VMEM_BYTES),
        cost_estimate=SMALL_COST,
        name="take_rows",
    )(*pieces)


def dense_call(kernel, name, outs, scratch, args):
    whole = pl.BlockSpec(memory_space=pltpu.VMEM)
    return pl.pallas_call(
        kernel,
        out_shape=[jax.ShapeDtypeStruct(shape, kind) for shape, kind in outs],
        in_specs=[whole] * len(args),
        out_specs=[whole] * len(outs),
        scratch_shapes=scratch,
        compiler_params=pltpu.CompilerParams(vmem_limit_bytes=VMEM_BYTES),
        cost_estimate=SMALL_COST,
        name=name,
    )(*args)


def turned(value, cos_wide, sin_wide):
    half = HEAD_DIM // 2
    swapped = jnp.concatenate([value[:, half:], value[:, :half]], axis=1)
    return value * cos_wide + swapped * sin_wide


def rope_kernel(raw, cos_wide, sin_wide, query, kv):
    cos, sin = cos_wide[...], sin_wide[...]
    query_width, kv_width = query.shape[1], kv.shape[1] // 2
    for start in range(0, query_width, HEAD_DIM):
        columns = slice(start, start + HEAD_DIM)
        query[:, columns] = turned(raw[:, columns], cos, sin).astype(jnp.bfloat16)
    for start in range(0, kv_width, HEAD_DIM):
        columns = slice(query_width + start, query_width + start + HEAD_DIM)
        kv[:, start : start + HEAD_DIM] = turned(raw[:, columns], cos, sin).astype(jnp.bfloat16)
    values = raw[:, query_width + kv_width : query_width + 2 * kv_width]
    kv[:, kv_width:] = values.astype(jnp.bfloat16)


def pair_of(early, own, index):
    columns = slice(index * HEAD_DIM, (index + 1) * HEAD_DIM)
    return jnp.concatenate([early[:, columns], own[:, columns]], axis=0)


def attend_kernel(scale, query, early, own, query_ids, key_ids, attended, log_total, fill):
    kv_local = own.shape[1] // HEAD_DIM // 2
    rows_total = query.shape[0]
    half_rows = rows_total // 2
    for part in range(2):
        rows = slice(part * half_rows, (part + 1) * half_rows)
        allowed = (key_ids[:, 0:1] == query_ids[0:1, rows]) & (
            key_ids[:, 1:2] <= query_ids[1:2, rows]
        )
        fill[...] = jnp.where(allowed, 0.0, mask_fill)
        for kv in range(kv_local):
            keys = pair_of(early, own, kv)
            values = pair_of(early, own, kv_local + kv)
            for member in range(GROUP):
                head = kv * GROUP + member
                columns = slice(head * HEAD_DIM, (head + 1) * HEAD_DIM)
                scores = cols_dot(keys, query[rows, columns]) + fill[...]
                top = jnp.max(scores, axis=0, keepdims=True)
                weights = jnp.exp((scores - top) * scale)
                total = jnp.sum(weights, axis=0, keepdims=True)
                probs = (weights * (1.0 / total)).astype(jnp.bfloat16)
                attended[rows, columns] = rows_dot(values, probs).T.astype(jnp.bfloat16)
                log_total[head : head + 1, rows] = top * scale + jnp.log(total)


def attend_back_kernel(
    scale,
    query,
    early,
    own,
    query_ids,
    key_ids,
    log_total,
    grad_attended,
    cos_wide,
    sin_wide,
    grad_query,
    grad_early,
    grad_own,
    fill,
    all_probs,
    all_grads,
):
    kv_local = own.shape[1] // HEAD_DIM // 2
    rows_total = query.shape[0]
    half_rows = rows_total // 2
    for part in range(2):
        rows = slice(part * half_rows, (part + 1) * half_rows)
        allowed = (key_ids[:, 0:1] == query_ids[0:1, rows]) & (
            key_ids[:, 1:2] <= query_ids[1:2, rows]
        )
        fill[:, rows] = jnp.where(allowed, 0.0, mask_fill)
    for kv in range(kv_local):
        keys = pair_of(early, own, kv)
        values = pair_of(early, own, kv_local + kv)
        queries, outs = [], []
        for part in range(2):
            rows = slice(part * half_rows, (part + 1) * half_rows)
            cos, sin = cos_wide[rows, :], -sin_wide[rows, :]
            for member in range(GROUP):
                head = kv * GROUP + member
                columns = slice(head * HEAD_DIM, (head + 1) * HEAD_DIM)
                place = (part * GROUP + member) * half_rows
                where = slice(place, place + half_rows)
                one_query, one_out = query[rows, columns], grad_attended[rows, columns]
                queries.append(one_query)
                outs.append(one_out)
                scores = cols_dot(keys, one_query) + fill[:, rows]
                probs = jnp.exp(scores * scale - log_total[head : head + 1, rows])
                grad_probs = cols_dot(values, one_out)
                delta = jnp.sum(probs * grad_probs, axis=0, keepdims=True)
                grads = (probs * (grad_probs - delta)).astype(jnp.bfloat16)
                all_probs[:, where] = probs.astype(jnp.bfloat16)
                all_grads[:, where] = grads
                turned_grad = rows_dot(keys, grads).T * scale
                grad_query[rows, columns] = turned(turned_grad, cos, sin).astype(jnp.bfloat16)
        grad_keys = (
            jnp.dot(
                all_grads[...], jnp.concatenate(queries, axis=0), preferred_element_type=jnp.float32
            )
            * scale
        )
        grad_values = jnp.dot(
            all_probs[...], jnp.concatenate(outs, axis=0), preferred_element_type=jnp.float32
        )
        for start, grad in ((kv, grad_keys), (kv_local + kv, grad_values)):
            columns = slice(start * HEAD_DIM, (start + 1) * HEAD_DIM)
            grad_early[:, columns] = grad[:rows_total].astype(jnp.bfloat16)
            grad_own[:, columns] = grad[rows_total:]


def join_kernel(grad_query, grad_own, late, cos_wide, sin_wide, grad_raw):
    cos, sin = cos_wide[...], -sin_wide[...]
    query_width, kv_width = grad_query.shape[1], grad_own.shape[1] // 2
    grad_raw[:, :query_width] = grad_query[...]
    for start in range(0, kv_width, HEAD_DIM):
        columns = slice(start, start + HEAD_DIM)
        grad = grad_own[:, columns] + late[:, columns].astype(jnp.float32)
        grad_raw[:, query_width + start : query_width + start + HEAD_DIM] = turned(
            grad, cos, sin
        ).astype(jnp.bfloat16)
    values = grad_own[:, kv_width:] + late[:, kv_width:].astype(jnp.float32)
    used = query_width + 2 * kv_width
    grad_raw[:, query_width + kv_width : used] = values.astype(jnp.bfloat16)
    spare = grad_raw.shape[1] - used
    grad_raw[:, used:] = jnp.zeros((grad_raw.shape[0], spare), jnp.bfloat16)


def tiled_call(kernel, name, steps, in_specs, outs, args):
    return pl.pallas_call(
        kernel,
        grid=(steps,),
        out_shape=[jax.ShapeDtypeStruct(shape, kind) for shape, kind, _, _ in outs],
        in_specs=[pl.BlockSpec(block, index) for block, index in in_specs],
        out_specs=[pl.BlockSpec(block, index) for _, _, block, index in outs],
        compiler_params=pltpu.CompilerParams(vmem_limit_bytes=VMEM_BYTES),
        cost_estimate=SMALL_COST,
        name=name,
    )(*args)


def fixed(step):
    return (0, 0)


def by_row(step):
    return (step, 0)


def by_column(step):
    return (0, step)


def split_dot(left, mine, other):
    depth = mine.shape[0]
    first = jnp.dot(left[:, :depth], mine[...], preferred_element_type=jnp.float32)
    return first + jnp.dot(left[:, depth:], other[...], preferred_element_type=jnp.float32)


def project_kernel(start, left, mine, other, out):
    columns = slice(start, start + out.shape[1])
    depth = mine.shape[0]
    first = jnp.dot(left[:, :depth], mine[:, columns], preferred_element_type=jnp.float32)
    second = jnp.dot(left[:, depth:], other[:, columns], preferred_element_type=jnp.float32)
    out[...] = (first + second).astype(out.dtype)


def project(left, weights, start, columns, kind):
    mine, other = weights
    rows, depth = left.shape[0], mine.shape[0]
    tiled = start == 0 and columns % 512 == 0
    tile = 512 if tiled else columns
    block = (depth, tile) if tiled else mine.shape
    (out,) = tiled_call(
        functools.partial(project_kernel, start),
        "project",
        columns // tile,
        [(left.shape, fixed), (block, by_column), (block, by_column)],
        [((rows, columns), kind, (rows, tile), by_column)],
        (left, mine, other),
    )
    return out


def hidden_kernel(normed, gate_m, gate_o, up_m, up_o, hidden, gate_slope, up_slope):
    gate_pre = split_dot(normed, gate_m, gate_o)
    up_pre = split_dot(normed, up_m, up_o)
    sig_gate = 1.0 / (1.0 + jnp.exp(-gate_pre))
    silu_gate = gate_pre * sig_gate
    hidden[...] = (silu_gate * up_pre).astype(jnp.bfloat16)
    gate_slope[...] = up_pre * (sig_gate * (1.0 + gate_pre * (1.0 - sig_gate)))
    up_slope[...] = silu_gate


def hidden_units(normed, gate_weights, up_weights):
    rows = normed.shape[0]
    depth, columns = gate_weights[0].shape
    tile = 256
    outs = [
        ((rows, columns), kind, (rows, tile), by_column)
        for kind in (jnp.bfloat16, jnp.float32, jnp.float32)
    ]
    return tiled_call(
        hidden_kernel,
        "hidden_units",
        columns // tile,
        [(normed.shape, fixed)] + [((depth, tile), by_column)] * 4,
        outs,
        (normed, *gate_weights, *up_weights),
    )


def hidden_grad_kernel(cot, down_m, down_o, gate_slope, up_slope, gate_grad, up_grad):
    grad_hidden = split_dot(cot, down_m, down_o)
    gate_grad[...] = (grad_hidden * gate_slope[...]).astype(jnp.bfloat16)
    up_grad[...] = (grad_hidden * up_slope[...]).astype(jnp.bfloat16)


def hidden_grads(cot, down_weights, gate_slope, up_slope):
    rows = cot.shape[0]
    depth, columns = down_weights[0].shape
    tile = 256
    out = ((rows, columns), jnp.bfloat16, (rows, tile), by_column)
    return tiled_call(
        hidden_grad_kernel,
        "hidden_grads",
        columns // tile,
        [(cot.shape, fixed)]
        + [((depth, tile), by_column)] * 2
        + [((rows, tile), by_column)] * 2,
        [out] * 2,
        (cot, *down_weights, gate_slope, up_slope),
    )


def back_kernel(count, start, *refs):
    lefts, weights, outs = refs[:count], refs[count : 3 * count], refs[3 * count :]
    columns = slice(start, start + lefts[0].shape[1])
    sums = []
    for half in range(2):
        terms = [
            cols_dot(left[...], weights[2 * i + half][:, columns]) for i, left in enumerate(lefts)
        ]
        sums.append(sum(terms).astype(jnp.bfloat16))
    one, two = sums
    one_keep, one_send, two_keep, two_send = outs
    n = one.shape[0] // 4
    one_keep[:n, :], one_send[:n, :] = one[:n], one[n : 2 * n]
    one_keep[n:, :], one_send[n:, :] = one[2 * n : 3 * n], one[3 * n :]
    two_keep[...], two_send[...] = two[: 2 * n], two[2 * n :]


def project_back(lefts, weights, start=0):
    rows, width = lefts[0].shape
    depth = weights[0][0].shape[0]
    tile = 256
    flat = [half for pair in weights for half in pair]
    return tiled_call(
        functools.partial(back_kernel, len(lefts), start),
        "project_back",
        depth // tile,
        [((rows, width), fixed)] * len(lefts) + [((tile, flat[0].shape[1]), by_row)] * len(flat),
        [((rows // 2, depth), jnp.bfloat16, (rows // 2, tile), by_column)] * 4,
        (*lefts, *flat),
    )


def outer_kernel(left, left_other, right, *refs):
    others, out = refs[:-1], refs[-1]
    total = rows_dot(left[...], right[...])
    rows = left.shape[0] // len(others)
    for i, other in enumerate(others):
        total = total + rows_dot(left_other[i * rows : (i + 1) * rows, :], other[...])
    out[...] = total.astype(jnp.bfloat16)


def outer(left, left_others, right, right_others, index):
    rows, width = left.shape[0], right.shape[1]
    left_other = left_others[index]
    depth = left_other.shape[1]
    tile = 256 if width % 256 == 0 else width
    (out,) = tiled_call(
        outer_kernel,
        "outer",
        width // tile,
        [((rows, depth), lambda step: (0, index)), ((rows, depth), fixed)]
        + [((rows, tile), by_column)]
        + [((other.shape[0], tile), by_column) for other in right_others],
        [((depth, width), jnp.bfloat16, (depth, tile), by_column)],
        (left, left_other, right, *right_others),
    )
    return out


def norm_kernel(rows, gain, out):
    value = rows[...].astype(jnp.float32)
    scale = lax.rsqrt(jnp.mean(value * value, axis=1, keepdims=True) + norm_eps)
    out[...] = (value * scale * gain[...]).astype(jnp.bfloat16)


def norm_rows(rows, gain):
    count, width = rows.shape
    tile = count // 4
    (out,) = tiled_call(
        norm_kernel,
        "norm_rows",
        4,
        [((tile, width), by_row), ((1, width), fixed)],
        [((count, width), jnp.bfloat16, (tile, width), by_row)],
        (rows, gain.reshape(1, width)),
    )
    return out


def take_wide_kernel(own, from_near, from_tp, out, sems):
    n = own.shape[0]
    moves = [
        (own, pl.ds(0, n)),
        (from_tp.at[pl.ds(0, n), :], pl.ds(n, n)),
        (from_near, pl.ds(2 * n, n)),
        (from_tp.at[pl.ds(n, n), :], pl.ds(3 * n, n)),
    ]
    copies = [
        pltpu.make_async_copy(source, out.at[rows, :], sems.at[k])
        for k, (source, rows) in enumerate(moves)
    ]
    for copy in copies:
        copy.start()
    for copy in copies:
        copy.wait()


def take_wide(own, from_near, from_tp):
    return pl.pallas_call(
        take_wide_kernel,
        out_shape=jax.ShapeDtypeStruct((4 * own.shape[0], own.shape[1]), own.dtype),
        in_specs=[pl.BlockSpec(memory_space=pl.ANY)] * 3,
        out_specs=pl.BlockSpec(memory_space=pltpu.VMEM),
        scratch_shapes=[pltpu.SemaphoreType.DMA((4,))],
        compiler_params=pltpu.CompilerParams(vmem_limit_bytes=VMEM_BYTES),
        cost_estimate=SMALL_COST,
        name="take_wide",
    )(own, from_near, from_tp)


def rows_call(fn, name, where, steps, ins, outs):
    def kernel(where_ref, *refs):
        values = [ref[...].astype(jnp.float32) for ref in refs[: len(ins)]]
        for ref, value in zip(refs[len(ins) :], fn(*values)):
            ref[...] = value.astype(ref.dtype)

    def spec(rows, columns, place):
        return pl.BlockSpec((rows, columns), lambda step, ref: (place(step, ref), 0))

    return pl.pallas_call(
        kernel,
        grid_spec=pltpu.PrefetchScalarGridSpec(
            num_scalar_prefetch=1,
            grid=(steps,),
            in_specs=[spec(rows, array.shape[1], place) for array, rows, place in ins],
            out_specs=[spec(rows, shape[1], place) for shape, _, rows, place in outs],
        ),
        out_shape=[jax.ShapeDtypeStruct(shape, kind) for shape, kind, _, _ in outs],
        compiler_params=pltpu.CompilerParams(vmem_limit_bytes=VMEM_BYTES),
        cost_estimate=SMALL_COST,
        name=name,
    )(where, *[array for array, _, _ in ins])


def far_halves(where, *terms):
    rows = terms[0][0].shape[0] // 4
    columns = sum(own.shape[1] for own, _ in terms)
    keep, give = (lambda step, ref: 2 * ref[0] + step), (lambda step, ref: 2 - 2 * ref[0] + step)
    out = ((2 * rows, columns), jnp.bfloat16, rows, lambda step, ref: step)
    count = len(terms)

    def sums(*values):
        pairs = [values[2 * i] + values[2 * i + 1] for i in range(2 * count)]
        if count == 1:
            return pairs
        return jnp.concatenate(pairs[:count], axis=1), jnp.concatenate(pairs[count:], axis=1)

    return rows_call(
        sums,
        "far_halves",
        where,
        2,
        [(array, rows, place) for place in (keep, give) for pair in terms for array in pair],
        [out, out],
    )


def near_halves(where, pair, from_far):
    rows, columns = pair.shape[0] // 2, pair.shape[1]
    keep, give = (lambda step, ref: ref[1]), (lambda step, ref: 1 - ref[1])
    out = ((rows, columns), jnp.bfloat16, rows, lambda step, ref: 0)
    return rows_call(
        lambda a, b, c, d: (a + b, c + d),
        "near_halves",
        where,
        1,
        [(array, rows, place) for place in (keep, give) for array in (pair, from_far)],
        [out, out],
    )


def join_halves_kernel(turn, where, own, received, *outs):
    first = where[1] == 0
    low_part = jnp.where(first, own[...], received[...]).astype(jnp.float32)
    high_part = jnp.where(first, received[...], own[...]).astype(jnp.float32)
    start = 0
    for out in outs:
        width = out.shape[0] if turn else out.shape[1]
        if len(outs) == 1:
            size = own.shape[1]
            rest = width - size
        else:
            size = rest = width // 2
        left, right = low_part[:, start : start + size], high_part[:, start : start + rest]
        if turn:
            out[:size, :] = left.T
            out[size:, :] = right.T
        else:
            out[:, :size] = left
            out[:, size:] = right
        start += size


def join_halves(where, own, received, widths, turn=False):
    rows = own.shape[0]
    shapes = [(width, rows) if turn else (rows, width) for width in widths]
    whole = pl.BlockSpec(memory_space=pltpu.VMEM)
    return pl.pallas_call(
        functools.partial(join_halves_kernel, turn),
        out_shape=[jax.ShapeDtypeStruct(shape, jnp.float32) for shape in shapes],
        in_specs=[pl.BlockSpec(memory_space=pltpu.SMEM), whole, whole],
        out_specs=[whole] * len(shapes),
        compiler_params=pltpu.CompilerParams(vmem_limit_bytes=VMEM_BYTES),
        cost_estimate=SMALL_COST,
        name="join_halves",
    )(where, own, received)


def split_halves_kernel(plan, where, *refs):
    arrays, pairs, other = refs[: len(plan)], refs[len(plan) : -1], refs[-1]
    rows = other.shape[0]
    first = where[1] == 0
    offset = 0
    filled = [0] * len(pairs)
    for index, (array, (target, size, turn)) in enumerate(zip(arrays, plan)):
        value = array[...]
        if turn:
            value = value.astype(jnp.float32).T.astype(jnp.bfloat16)
        low_part, high_part = value[:, :size], value[:, size:]
        missing = size - high_part.shape[1]
        if missing:
            high_part = jnp.concatenate(
                [high_part, jnp.zeros((rows, missing), jnp.bfloat16)], axis=1
            )
        start = filled[target]
        pair = pairs[target]
        pair[:rows, start : start + size] = jnp.where(first, low_part, high_part)
        other[:, offset + start : offset + start + size] = jnp.where(first, high_part, low_part)
        filled[target] = start + size
        if index + 1 == len(plan) or plan[index + 1][0] != target:
            spare = pair.shape[1] - filled[target]
            if spare:
                pair[:rows, filled[target] :] = jnp.zeros((rows, spare), jnp.bfloat16)
                end = offset + pair.shape[1]
                other[:, end - spare : end] = jnp.zeros((rows, spare), jnp.bfloat16)
            offset += pair.shape[1]


def split_halves(where, arrays, plan, widths):
    rows = D // 16
    whole = pl.BlockSpec(memory_space=pltpu.VMEM)
    return pl.pallas_call(
        functools.partial(split_halves_kernel, plan),
        out_shape=[jax.ShapeDtypeStruct((2 * rows, width), jnp.bfloat16) for width in widths]
        + [jax.ShapeDtypeStruct((rows, sum(widths)), jnp.bfloat16)],
        in_specs=[pl.BlockSpec(memory_space=pltpu.SMEM)] + [whole] * len(arrays),
        out_specs=[whole] * (len(widths) + 1),
        compiler_params=pltpu.CompilerParams(vmem_limit_bytes=VMEM_BYTES),
        cost_estimate=SMALL_COST,
        name="split_halves",
    )(where, *arrays)


def pair_kernel(first, second, out):
    n = first.shape[0]
    out[:n, :] = first[...]
    out[n:, :] = second[...]


def pair_rows(first, second):
    rows, columns = first.shape
    (out,) = dense_call(
        pair_kernel, "pair_rows", [((2 * rows, columns), first.dtype)], [], (first, second)
    )
    return out


def middle_kernel(one, got_one, two, got_two, next_one, next_two, sum_one, sum_two):
    n = sum_one.shape[0]
    for keep, got, later, total in (
        (one, got_one, next_one, sum_one),
        (two, got_two, next_two, sum_two),
    ):
        both = keep[...].astype(jnp.float32) + got[...].astype(jnp.float32)
        total[...] = both[:n]
        later[...] = both[n:].astype(jnp.bfloat16)


def scatter_middle(one, got_one, two, got_two):
    rows, columns = one.shape[0] // 2, one.shape[1]
    return dense_call(
        middle_kernel,
        "scatter_middle",
        [((rows, columns), jnp.bfloat16)] * 2 + [((rows, columns), jnp.float32)] * 2,
        [],
        (one, got_one, two, got_two),
    )


def summed(sum_one, sum_two, last_one, last_two):
    one = sum_one[...] + last_one[...].astype(jnp.float32)
    two = sum_two[...] + last_two[...].astype(jnp.float32)
    return jnp.concatenate([one, two], axis=1)


def store_halves(value, one, two):
    half = one.shape[1]
    one[...] = value[:, :half].astype(one.dtype)
    two[...] = value[:, half:].astype(two.dtype)


def residual_kernel(sum_one, sum_two, last_one, last_two, rows, gain, residual, one, two):
    value = rows[...].astype(jnp.float32) + summed(sum_one, sum_two, last_one, last_two)
    residual[...] = value
    scale = lax.rsqrt(jnp.mean(value * value, axis=1, keepdims=True) + norm_eps)
    store_halves(value * scale * gain[...], one, two)


def norm_grad(grad, value, gain):
    scale = lax.rsqrt(jnp.mean(value * value, axis=1, keepdims=True) + norm_eps)
    scaled = grad * gain
    inner = jnp.mean(scaled * value, axis=1, keepdims=True)
    gain_term = jnp.sum(grad * value * scale, axis=0, keepdims=True)
    return scale * scaled - value * (scale * scale * scale) * inner, gain_term


def residual_grad_kernel(
    sum_one, sum_two, last_one, last_two, residual, gain, cot, grad, gain_term, one, two
):
    back, term = norm_grad(summed(sum_one, sum_two, last_one, last_two), residual[...], gain[...])
    value = cot[...].astype(jnp.float32) + back
    grad[...] = value
    gain_term[...] = term
    store_halves(value, one, two)


def token_grad_kernel(
    sum_one, sum_two, last_one, last_two, rows, gain, grad_residual, grad
):
    value = rows[...].astype(jnp.float32)
    back, _ = norm_grad(summed(sum_one, sum_two, last_one, last_two), value, gain[...])
    grad[...] = grad_residual[...] + back


def gain_kernel(one_keep, one_send, two_keep, two_send, rows, out):
    n, half = one_keep.shape[0] // 2, one_keep.shape[1]
    low_half, high_half = slice(0, n), slice(n, 2 * n)
    ones = (one_keep, low_half), (one_send, low_half), (one_keep, high_half), (one_send, high_half)
    twos = (two_keep, low_half), (two_keep, high_half), (two_send, low_half), (two_send, high_half)
    left = right = 0.0
    for k in range(4):
        value = rows[k * n : (k + 1) * n, :].astype(jnp.float32)
        scale = lax.rsqrt(jnp.mean(value * value, axis=1, keepdims=True) + norm_eps)
        value = value * scale
        one = ones[k][0][ones[k][1], :].astype(jnp.float32)
        two = twos[k][0][twos[k][1], :].astype(jnp.float32)
        left = left + jnp.sum(one * value[:, :half], axis=0, keepdims=True)
        right = right + jnp.sum(two * value[:, half:], axis=0, keepdims=True)
    out[:, :half] = left
    out[:, half:] = right


def mixed_kernel(sum_one, sum_two, last_one, last_two, residual, mixed):
    total = residual[...] + summed(sum_one, sum_two, last_one, last_two)
    mixed[...] = total.astype(jnp.bfloat16)


def half_plan(
    tokens, doc_lengths, w_query, w_key, w_value, w_out, w_gate, w_up, w_down, norm_gains, cotangent
):
    fsdp_index = lax.axis_index("fsdp")
    seq_index = lax.axis_index("seq")
    tp_index = lax.axis_index("tp")
    near = seq_index % 2
    far = seq_index // 2
    local_rows = tokens.shape[0]
    group_rows = 4 * local_rows
    middle = D // 2
    quarter = D // 4
    block_rows = D // 16
    score_scale = 1.0 / math.sqrt(HEAD_DIM)

    def columns_in(value):
        return jnp.concatenate(
            [
                lax.dynamic_slice_in_dim(value, (fsdp_index ^ k) * quarter, quarter, 1)
                for k in (0, 2, 1, 3)
            ],
            axis=1,
        )

    def columns_out(value):
        pieces = []
        for block in range(4):
            k = fsdp_index ^ block
            place = (k // 2) + (k % 2) * 2
            pieces.append(lax.dynamic_slice_in_dim(value, place * quarter, quarter, 1))
        return jnp.concatenate(pieces, axis=1)

    def gather_first(one, two):
        return one, two, to_z(one, 1), to_tp(two)

    def gather_second(one, two, one_near, two_tp):
        one_far = to_tp(pair_rows(one, one_near))
        two_far = to_z(pair_rows(two, two_tp), 1)
        return one, two, one_near, one_far, two_tp, two_far

    def scatter_first(one_keep, one_send, two_keep, two_send):
        return one_keep, to_tp(one_send), two_keep, to_z(two_send, 1)

    def scatter_second(next_one, next_two, sum_one, sum_two):
        return sum_one, sum_two, to_z(next_one, 1), to_tp(next_two)

    where = jnp.stack([far, near]).astype(jnp.int32)
    query_width = w_query.shape[1] // 2
    key_width = w_key.shape[1] // 2
    query_heads = query_width // HEAD_DIM
    heads_width = -(-(query_width + 2 * key_width) // 128) * 128
    hidden_width = -(-(w_gate.shape[1] // 2) // 128) * 128
    row_shape = (local_rows, D)
    half_shape = (local_rows, middle)

    def cross_left(value, *events):
        first, second = value[:, middle : middle + quarter], value[:, middle + quarter :]
        return to_core(hold(first, events)), to_core(hold(second, events))

    def cross_right(value, count):
        rows = value.shape[0] // count
        return tuple(to_core(value[i * rows : (i + 1) * rows]) for i in range(count))

    tokens_in = columns_in(tokens)
    cot_in = columns_in(cotangent)
    first_width = heads_width + query_width
    plan = ((0, query_width, False), (0, key_width, False), (0, key_width, False))
    spare = heads_width - query_width - 2 * key_width
    first_pair, first_other = split_halves(
        where,
        (w_query, w_key, w_value, jnp.zeros((block_rows, 2 * spare), jnp.bfloat16), w_out),
        (*plan, (0, spare, False), (0, query_width, True)),
        (first_width,),
    )
    gain_stack = norm_gains[None]
    gain_stack = jnp.concatenate([gain_stack, to_z(gain_stack, 1)], axis=0)
    first_near = to_z(first_other, 1)
    token_wait = gather_first(tokens_in[:, :middle], tokens_in[:, middle:])
    gain_far = to_z(hold(gain_stack, token_wait[2:]), 2)
    gain_stack = jnp.concatenate([gain_stack, gain_far], axis=0)
    first_pair = fill_rows(*hold((first_pair, first_near), gain_stack))
    first_far = to_z(first_pair, 2)
    token_wait = gather_second(*hold(token_wait, first_pair))
    gate_pair, gate_other = split_halves(
        where, (w_gate,), ((0, hidden_width, False),), (hidden_width,)
    )
    up_pair, up_other = split_halves(where, (w_up,), ((0, hidden_width, False),), (hidden_width,))
    down_pair, down_other = split_halves(
        where, (w_down,), ((0, hidden_width, True),), (hidden_width,)
    )
    gate_near = to_z(hold(gate_other, first_pair), 1)
    token_wait = hold(token_wait, gate_other, up_other, down_other)
    gain_plane = jnp.concatenate(
        [
            lax.dynamic_index_in_dim(gain_stack, seq_index ^ k, 0, keepdims=False)
            for k in range(4)
        ],
        axis=1,
    )
    gain_mine = jnp.concatenate([gain_plane, to_x(gain_plane)], axis=1)
    gains = float_of(jnp.concatenate([gain_mine, to_core(gain_mine)], axis=1))
    gain_one = gains[0:1]
    gain_two = gains[1:2]
    token_span = take_rows(*hold(token_wait, gains))

    row_ids = jnp.arange(local_rows, dtype=jnp.int32)
    own_positions = jnp.concatenate(
        [
            far * (2 * 2 * local_rows)
            + (near ^ i) * (2 * local_rows)
            + (tp_index ^ j) * local_rows
            + row_ids
            for i in range(2)
            for j in range(2)
        ]
    )
    cos_tab, sin_tab = rope_tables(own_positions)
    cos_wide = jnp.concatenate([cos_tab, cos_tab], axis=1)
    sin_wide = jnp.concatenate([-sin_tab, sin_tab], axis=1)
    key_positions = jnp.concatenate([own_positions - group_rows, own_positions])
    doc_ends = jnp.cumsum(doc_lengths[0])[: DOCS - 1]

    def doc_of(positions):
        return jnp.sum((positions[:, None] >= doc_ends[None, :]).astype(jnp.int32), axis=1)

    key_docs = jnp.where(key_positions >= 0, doc_of(key_positions), -1)
    query_ids = jnp.stack([doc_of(own_positions), own_positions // BLOCK])
    key_ids = jnp.stack([key_docs, key_positions // BLOCK], axis=1)

    gate_pair = fill_rows(*hold((gate_pair, gate_near), token_span))
    first_plane, first_mine = place_rows(*hold((first_pair, first_far), gate_pair), seq_index)
    first_x = to_x(first_plane)
    gate_far = to_z(hold(gate_pair, first_plane), 2)
    normed_one = norm_rows(hold(token_span, first_plane), gain_one)
    normed_other = cross_left(normed_one)
    up_pair = fill_rows(up_pair, to_z(hold(up_other, first_plane), 1))
    down_pair = fill_rows(down_pair, to_z(hold(down_other, first_plane), 1))
    cot_first = gather_first(*hold((cot_in[:, :middle], cot_in[:, middle:]), up_pair))
    gate_plane, gate_mine = place_rows(
        *hold((gate_pair, gate_far), cot_first[2:], down_pair, normed_one), seq_index
    )
    first_mine = fill_rows(*hold((first_mine, first_x), gate_plane))
    first_weights = first_mine, to_core(first_mine)
    gate_x = to_x(hold(gate_plane, first_mine))
    up_far = to_z(hold(up_pair, gate_plane), 2)
    cot_wait = gather_second(*hold(cot_first, first_mine))
    raw = project(normed_one, first_weights, 0, heads_width, jnp.float32)
    query_rot, own_kv = dense_call(
        rope_kernel,
        "rope",
        [
            ((group_rows, query_width), jnp.bfloat16),
            ((group_rows, 2 * key_width), jnp.bfloat16),
        ],
        [],
        (raw, cos_wide, sin_wide),
    )
    cot_span = take_rows(*hold(cot_wait, own_kv))
    up_plane, up_mine = place_rows(*hold((up_pair, up_far), cot_span), seq_index)
    early_kv = lax.ppermute(hold(own_kv, up_plane), "seq", [(0, 2), (1, 3)])
    gate_mine = fill_rows(*hold((gate_mine, gate_x), up_plane))
    gate_weights = gate_mine, to_core(gate_mine)
    up_x = to_x(hold(up_plane, gate_mine))
    attended_low, log_total = dense_call(
        functools.partial(attend_kernel, score_scale),
        "attend",
        [
            ((group_rows, query_width), jnp.bfloat16),
            ((query_heads, group_rows), jnp.float32),
        ],
        [pltpu.VMEM((2 * group_rows, group_rows // 2), jnp.float32)],
        (query_rot, early_kv, own_kv, query_ids, key_ids),
    )
    attended_other = cross_right(attended_low, 1)
    down_far = to_z(hold(down_pair, log_total), 2)
    branch = scatter_first(
        *project_back([attended_low], [first_weights], heads_width)
    )
    branch = scatter_middle(*branch)
    branch = scatter_second(*branch)
    down_plane, down_mine = place_rows(*hold((down_pair, down_far), branch[:2]), seq_index)
    up_mine = fill_rows(*hold((up_mine, up_x), down_plane))
    up_weights = up_mine, to_core(up_mine)
    down_x = to_x(hold(down_plane, up_mine))
    residual, two_one, two_two = dense_call(
        residual_kernel,
        "residual",
        [(row_shape, jnp.float32)] + [(half_shape, jnp.bfloat16)] * 2,
        [],
        (*hold(branch, up_mine), tokens_in, gain_two),
    )
    two_wait = gather_second(*gather_first(two_one, two_two))
    span_two = take_rows(*two_wait)
    span_other = cross_left(span_two)
    cot_other = cross_left(cot_span, log_total)
    hidden_low, gate_slope, up_slope = hidden_units(span_two, gate_weights, up_weights)
    hidden_other = cross_right(hidden_low, 1)
    down_mine = fill_rows(*hold((down_mine, down_x), hidden_low))
    down_weights = down_mine, to_core(down_mine)

    down_parts = hold((cot_span, cot_other, hidden_low, hidden_other), down_mine)
    down_give = outer(*down_parts, 1)
    down_back = to_x(down_give)
    down_keep = outer(*hold(down_parts, down_give), 0)
    mlp_parts = project_back([hold(hidden_low, down_keep)], [down_weights])
    grad_gate_pre, grad_up_pre = hidden_grads(
        hold(cot_span, mlp_parts), down_weights, gate_slope, up_slope
    )
    gate_other = cross_right(grad_gate_pre, 1)
    up_other = cross_right(grad_up_pre, 1)
    branch_mlp = scatter_first(*mlp_parts)
    back_parts = project_back(
        [grad_gate_pre, grad_up_pre], [gate_weights, up_weights]
    )
    branch_mlp = scatter_middle(*hold(branch_mlp, back_parts))
    normed_back = scatter_first(*hold(back_parts, branch_mlp))
    down_keep, down_give = far_halves(where, hold((down_keep, down_back), branch_mlp))
    down_far = to_z(down_give, 2)
    gate_parts = hold((span_two, span_other, grad_gate_pre, gate_other), down_give)
    gate_give = outer(*gate_parts, 1)
    gate_back = to_x(gate_give)
    normed_back = scatter_second(*scatter_middle(*hold(normed_back, gate_give)))
    gate_keep = outer(*hold(gate_parts, normed_back[:2]), 0)
    up_parts = hold((span_two, span_other, grad_up_pre, up_other), gate_keep)
    up_give = outer(*up_parts, 1)
    up_keep = outer(*hold(up_parts, up_give), 0)
    grad_residual, gain_two_term, grad_one, grad_two = dense_call(
        residual_grad_kernel,
        "residual_grad",
        [(row_shape, jnp.float32), ((1, D), jnp.float32)] + [(half_shape, jnp.bfloat16)] * 2,
        [],
        (*hold(normed_back, up_keep), residual, gain_two, cot_in),
    )
    grad_wait = gather_first(grad_one, grad_two)
    down_own, down_other = near_halves(where, *hold((down_keep, down_far), grad_wait[2:]))
    gate_keep, gate_give = far_halves(where, hold((gate_keep, gate_back), down_other))
    gate_far = to_z(gate_give, 2)
    up_back = to_x(hold(up_give, gate_give))
    grad_wait = gather_second(*hold(grad_wait, gate_give))
    grad_span = take_rows(*grad_wait)
    down_near = to_z(hold(down_other, grad_span), 1)
    gate_own, gate_other = near_halves(where, *hold((gate_keep, gate_far), grad_span))
    gate_near = to_z(gate_other, 1)
    span_grad_other = cross_left(grad_span)
    grad_attended = project(
        hold(grad_span, gate_other), first_weights, heads_width, query_width, jnp.bfloat16
    )
    grad_query, grad_early, grad_own = dense_call(
        functools.partial(attend_back_kernel, score_scale),
        "attend_back",
        [
            ((group_rows, query_width), jnp.bfloat16),
            ((group_rows, 2 * key_width), jnp.bfloat16),
            ((group_rows, 2 * key_width), jnp.float32),
        ],
        [
            pltpu.VMEM((2 * group_rows, group_rows), jnp.float32),
            pltpu.VMEM((2 * group_rows, GROUP * group_rows), jnp.bfloat16),
            pltpu.VMEM((2 * group_rows, GROUP * group_rows), jnp.bfloat16),
        ],
        (
            query_rot,
            early_kv,
            own_kv,
            query_ids,
            key_ids,
            log_total,
            grad_attended,
            cos_wide,
            sin_wide,
        ),
    )
    up_terms = hold((up_keep, up_back), grad_early, down_near, gate_near)
    late_kv = lax.ppermute(hold(grad_early, up_terms[1]), "seq", [(2, 0), (3, 1)])
    out_parts = hold((grad_span, span_grad_other, attended_low, attended_other), up_terms[1])
    branch_mlp = scatter_second(*hold(branch_mlp, up_terms[1]))
    out_give = outer(*out_parts, 1)
    out_back = to_x(out_give)
    out_keep = outer(*out_parts, 0)
    both_keep, both_give = far_halves(where, up_terms, hold((out_keep, out_back), late_kv, branch_mlp[2:]))
    both_far = to_z(both_give, 2)
    (grad_raw,) = dense_call(
        join_kernel,
        "join",
        [((group_rows, heads_width), jnp.bfloat16)],
        [],
        (grad_query, grad_own, hold(late_kv, both_give), cos_wide, sin_wide),
    )
    raw_other = cross_right(grad_raw, 2)
    first_parts = project_back([grad_raw], [first_weights])
    first_back = scatter_first(*first_parts)
    heads_parts = hold((normed_one, normed_other, grad_raw, raw_other), first_parts)
    heads_give = outer(*heads_parts, 1)
    heads_back = to_x(heads_give)
    heads_keep = outer(*heads_parts, 0)
    units = w_gate.shape[1]
    (gain_one_term,) = dense_call(
        gain_kernel,
        "gain",
        [((1, D), jnp.float32)],
        [],
        (*hold(first_parts, heads_keep), token_span),
    )
    gain_rows = jnp.concatenate([gain_one_term, gain_two_term], axis=0)
    gain_rows = gain_rows[:, :middle] + to_core(gain_rows[:, middle:])
    gain_rows = gain_rows + to_tp(gain_rows)
    first_back = scatter_middle(*hold(first_back, gain_rows))
    heads_keep, heads_give = far_halves(where, hold((heads_keep, heads_back), first_back))
    heads_far = to_z(heads_give, 2)
    gain_rows = hold(gain_rows, heads_give)
    gain_rows = gain_rows[:, :quarter] + to_x(gain_rows[:, quarter:])
    both_own, both_other = near_halves(where, *hold((both_keep, both_far), heads_give, gain_rows))
    both_near = to_z(both_other, 1)
    first_back = scatter_second(*hold(first_back, both_other))
    (grad_rows,) = dense_call(
        token_grad_kernel,
        "token_grad",
        [(row_shape, jnp.float32)],
        [],
        (*first_back, tokens_in, gain_one, grad_residual),
    )
    gain_blocks = hold(gain_rows, both_other).reshape(2, 4, block_rows)
    gain_pair = [
        lax.dynamic_index_in_dim(gain_blocks, seq_index ^ k, 1, keepdims=False) for k in range(4)
    ]
    gain_half = jnp.stack(gain_pair[:2]) + to_z(jnp.stack(gain_pair[2:]), 2)
    gain_grads = gain_half[0] + to_z(gain_half[1], 1)
    heads_own, heads_other = near_halves(
        where, *hold((heads_keep, heads_far), grad_rows, both_near)
    )
    heads_near = to_z(heads_other, 1)
    (grad_down,) = join_halves(where, *hold((down_own, down_near), heads_other), (units,), True)
    (grad_gate,) = join_halves(where, *hold((gate_own, gate_near), grad_down), (units,))
    (mixed,) = dense_call(
        mixed_kernel,
        "mixed",
        [(row_shape, jnp.bfloat16)],
        [],
        (*hold(branch_mlp, grad_gate), residual),
    )
    both_own, both_near = hold((both_own, both_near), grad_gate)
    (grad_up,) = join_halves(
        where,
        *hold((both_own[:, :hidden_width], both_near[:, :hidden_width]), heads_other),
        (units,),
    )
    (grad_out,) = join_halves(
        where, both_own[:, hidden_width:], both_near[:, hidden_width:], (w_out.shape[0],), True
    )
    grad_query_w, grad_key_w, grad_value_w = join_halves(
        where,
        *hold((heads_own, heads_near), grad_out, grad_up),
        (2 * query_width, 2 * key_width, 2 * key_width),
    )
    mixed_out = columns_out(mixed)
    grad_tokens = columns_out(hold(grad_rows, grad_out))
    return (
        mixed_out,
        grad_tokens,
        grad_query_w,
        grad_key_w,
        grad_value_w,
        grad_out,
        grad_gate,
        grad_up,
        grad_down,
        gain_grads,
    )


def solution(mesh):
    halves = mesh.shape["seq"] == 4 and mesh.shape["tp"] == 2 and mesh.shape["fsdp"] == 4
    plan = half_plan if halves else per_device
    in_specs = (
        P(("fsdp", "seq", "tp"), None),
        P("fsdp", None),
        P(("fsdp", "seq"), "tp"),
        P(("fsdp", "seq"), "tp"),
        P(("fsdp", "seq"), "tp"),
        P("tp", ("fsdp", "seq")),
        P(("fsdp", "seq"), "tp"),
        P(("fsdp", "seq"), "tp"),
        P("tp", ("fsdp", "seq")),
        P(None, ("fsdp", "seq")),
        P(("fsdp", "seq", "tp"), None),
    )
    out_specs = (
        P(("fsdp", "seq", "tp"), None),
        P(("fsdp", "seq", "tp"), None),
        P(("fsdp", "seq"), "tp"),
        P(("fsdp", "seq"), "tp"),
        P(("fsdp", "seq"), "tp"),
        P("tp", ("fsdp", "seq")),
        P(("fsdp", "seq"), "tp"),
        P(("fsdp", "seq"), "tp"),
        P("tp", ("fsdp", "seq")),
        P(None, ("fsdp", "seq")),
    )
    return jax.shard_map(
        plan, mesh=mesh, in_specs=in_specs, out_specs=out_specs, check_vma=False
    )
```

```python
import functools
import math

import jax
import jax.numpy as jnp
from jax import lax
from jax.experimental import pallas as pl
from jax.experimental.pallas import tpu as pltpu
from jax.sharding import PartitionSpec as P

D = 2560
HEAD_DIM = 80
BLOCK = 256
DOCS = 3
GROUP = 4


norm_eps = 1e-05
rope_base = 10000.0
mask_fill = -1000000000.0


def rope_tables(positions):
    half_dim = HEAD_DIM // 2
    freq_row = rope_base ** (-jnp.arange(half_dim, dtype=jnp.float32) * 2.0 / HEAD_DIM)
    angles = positions.astype(jnp.float32)[:, None] * freq_row[None, :]
    return (jnp.cos(angles), jnp.sin(angles))


def rotate(values, cos_tab, sin_tab):
    half_dim = HEAD_DIM // 2
    first_half = values[..., :half_dim]
    second_half = values[..., half_dim:]
    cos_wide = cos_tab[:, None, :]
    sin_wide = sin_tab[:, None, :]
    return jnp.concatenate(
        [
            first_half * cos_wide - second_half * sin_wide,
            second_half * cos_wide + first_half * sin_wide,
        ],
        axis=-1,
    )


def document_ids(lengths, positions):
    doc_ends = jnp.cumsum(lengths)
    return jnp.sum((positions[:, None] >= doc_ends[None, : DOCS - 1]).astype(jnp.int32), axis=1)


def rms_scale(row_values):
    return lax.rsqrt(jnp.mean(row_values * row_values, axis=-1, keepdims=True) + norm_eps)


def per_device(
    tokens, doc_lengths, w_query, w_key, w_value, w_out, w_gate, w_up, w_down, norm_gains, cotangent
):
    tp_count = lax.axis_size("tp")
    seq_count = lax.axis_size("seq")
    tp_index = lax.axis_index("tp")
    seq_index = lax.axis_index("seq")
    local_rows = tokens.shape[0]
    span_len = local_rows * tp_count
    seq_length = span_len * seq_count
    score_scale = 1.0 / math.sqrt(HEAD_DIM)
    key_step = math.gcd(512, seq_length)
    gathered = (
        lax.all_gather(w_query, ("fsdp", "seq"), axis=0, tiled=True),
        lax.all_gather(w_key, ("fsdp", "seq"), axis=0, tiled=True),
        lax.all_gather(w_value, ("fsdp", "seq"), axis=0, tiled=True),
        lax.all_gather(w_out, ("fsdp", "seq"), axis=1, tiled=True),
        lax.all_gather(w_gate, ("fsdp", "seq"), axis=0, tiled=True),
        lax.all_gather(w_up, ("fsdp", "seq"), axis=0, tiled=True),
        lax.all_gather(w_down, ("fsdp", "seq"), axis=1, tiled=True),
        lax.all_gather(norm_gains, ("fsdp", "seq"), axis=1, tiled=True),
    )
    query_full, key_full, value_full, out_full, gate_full, up_full, down_full, gains_low = gathered
    gain_one = gains_low[0].astype(jnp.float32)
    gain_two = gains_low[1].astype(jnp.float32)
    query_heads = query_full.shape[1] // HEAD_DIM
    kv_local = key_full.shape[1] // HEAD_DIM
    span_in = lax.all_gather(tokens, "tp", axis=0, tiled=True)
    span_float = span_in.astype(jnp.float32)
    inv_one = rms_scale(span_float)
    normed_one = (span_float * inv_one * gain_one).astype(jnp.bfloat16)
    span_start = seq_index * span_len
    positions = span_start + jnp.arange(span_len, dtype=jnp.int32)
    cos_tab, sin_tab = rope_tables(positions)
    query_raw = jnp.dot(normed_one, query_full, preferred_element_type=jnp.float32).reshape(
        span_len, query_heads, HEAD_DIM
    )
    key_raw = jnp.dot(normed_one, key_full, preferred_element_type=jnp.float32).reshape(
        span_len, kv_local, HEAD_DIM
    )
    value_raw = jnp.dot(normed_one, value_full, preferred_element_type=jnp.float32).reshape(
        span_len, kv_local, HEAD_DIM
    )
    query_rot = rotate(query_raw, cos_tab, sin_tab).astype(jnp.bfloat16)
    key_rot = rotate(key_raw, cos_tab, sin_tab).astype(jnp.bfloat16)
    value_low = value_raw.astype(jnp.bfloat16)
    query_group = query_rot.reshape(span_len, kv_local, GROUP, HEAD_DIM)
    key_all, value_all = (
        lax.all_gather(key_rot, "seq", axis=0, tiled=True),
        lax.all_gather(value_low, "seq", axis=0, tiled=True),
    )
    key_positions = jnp.arange(seq_length, dtype=jnp.int32)
    doc_keys = document_ids(doc_lengths[0], key_positions)
    doc_query = lax.dynamic_slice_in_dim(doc_keys, span_start, span_len, 0)
    key_blocks = key_positions // BLOCK
    query_block = positions // BLOCK
    blocks_used = (span_start + span_len + key_step - 1) // key_step
    stat_shape = (kv_local, GROUP, span_len)
    head_shape = (span_len, kv_local, GROUP, HEAD_DIM)

    def masked_scores(block_index):
        key_start = block_index * key_step
        key_part = lax.dynamic_slice_in_dim(key_all, key_start, key_step, 0)
        scores = (
            jnp.einsum("ckgd,nkd->kgcn", query_group, key_part, preferred_element_type=jnp.float32)
            * score_scale
        )
        block_part = lax.dynamic_slice_in_dim(key_blocks, key_start, key_step, 0)
        doc_part = lax.dynamic_slice_in_dim(doc_keys, key_start, key_step, 0)
        allowed = (block_part[None, :] <= query_block[:, None]) & (
            doc_part[None, :] == doc_query[:, None]
        )
        return (jnp.where(allowed[None, None], scores, mask_fill), key_start, key_part)

    def total_step(block_index, carry):
        row_max, row_sum = carry
        scores = masked_scores(block_index)[0]
        new_max = jnp.maximum(row_max, jnp.max(scores, axis=-1))
        row_sum = row_sum * jnp.exp(row_max - new_max) + jnp.sum(
            jnp.exp(scores - new_max[..., None]), axis=-1
        )
        return (new_max, row_sum)

    row_max, row_sum = lax.fori_loop(
        0,
        blocks_used,
        total_step,
        (jnp.full(stat_shape, mask_fill, jnp.float32), jnp.zeros(stat_shape, jnp.float32)),
    )
    log_total = row_max + jnp.log(row_sum)

    def out_step(block_index, running):
        scores, key_start, key_part = masked_scores(block_index)
        attn_prob = jnp.exp(scores - log_total[..., None]).astype(jnp.bfloat16)
        value_part = lax.dynamic_slice_in_dim(value_all, key_start, key_step, 0)
        return running + jnp.einsum(
            "kgcn,nkd->ckgd", attn_prob, value_part, preferred_element_type=jnp.float32
        )

    attended = lax.fori_loop(0, blocks_used, out_step, jnp.zeros(head_shape, jnp.float32))
    attended_low = attended.reshape(span_len, query_heads * HEAD_DIM).astype(jnp.bfloat16)
    attn_branch = lax.psum_scatter(
        jnp.dot(attended_low, out_full, preferred_element_type=jnp.float32).astype(jnp.bfloat16),
        "tp",
        scatter_dimension=0,
        tiled=True,
    ).astype(jnp.float32)
    token_rows = tokens.astype(jnp.float32)
    residual = token_rows + attn_branch
    inv_two = rms_scale(residual)
    normed_two = (residual * inv_two * gain_two).astype(jnp.bfloat16)
    span_two = lax.all_gather(normed_two, "tp", axis=0, tiled=True)
    gate_pre = jnp.dot(span_two, gate_full, preferred_element_type=jnp.float32)
    up_pre = jnp.dot(span_two, up_full, preferred_element_type=jnp.float32)
    sig_gate = jax.nn.sigmoid(gate_pre)
    silu_gate = gate_pre * sig_gate
    hidden_low = (silu_gate * up_pre).astype(jnp.bfloat16)
    mlp_branch = lax.psum_scatter(
        jnp.dot(hidden_low, down_full, preferred_element_type=jnp.float32).astype(jnp.bfloat16),
        "tp",
        scatter_dimension=0,
        tiled=True,
    ).astype(jnp.float32)
    mixed_out = (residual + mlp_branch).astype(jnp.bfloat16)
    cot_span = lax.all_gather(cotangent, "tp", axis=0, tiled=True)
    grad_down_w = jnp.einsum("cf,cd->fd", hidden_low, cot_span, preferred_element_type=jnp.float32)
    grad_hidden = jnp.einsum("cd,fd->cf", cot_span, down_full, preferred_element_type=jnp.float32)
    grad_gate_pre = (
        grad_hidden * up_pre * (sig_gate * (1.0 + gate_pre * (1.0 - sig_gate)))
    ).astype(jnp.bfloat16)
    grad_up_pre = (grad_hidden * silu_gate).astype(jnp.bfloat16)
    grad_gate_w = jnp.einsum(
        "cd,cf->df", span_two, grad_gate_pre, preferred_element_type=jnp.float32
    )
    grad_up_w = jnp.einsum("cd,cf->df", span_two, grad_up_pre, preferred_element_type=jnp.float32)
    grad_normed_two = lax.psum_scatter(
        (
            jnp.einsum("cf,df->cd", grad_gate_pre, gate_full, preferred_element_type=jnp.float32)
            + jnp.einsum("cf,df->cd", grad_up_pre, up_full, preferred_element_type=jnp.float32)
        ).astype(jnp.bfloat16),
        "tp",
        scatter_dimension=0,
        tiled=True,
    ).astype(jnp.float32)
    gain_two_term = jnp.sum(grad_normed_two * residual * inv_two, axis=0)
    scaled_two = grad_normed_two * gain_two
    grad_residual = (
        cotangent.astype(jnp.float32)
        + inv_two * scaled_two
        - residual
        * (inv_two * inv_two * inv_two)
        * jnp.mean(scaled_two * residual, axis=-1, keepdims=True)
    )
    grad_span = lax.all_gather(grad_residual.astype(jnp.bfloat16), "tp", axis=0, tiled=True)
    grad_out_w = jnp.einsum(
        "ce,cd->ed", attended_low, grad_span, preferred_element_type=jnp.float32
    )
    grad_attended = (
        jnp.einsum("cd,ed->ce", grad_span, out_full, preferred_element_type=jnp.float32)
        .astype(jnp.bfloat16)
        .reshape(head_shape)
    )

    def prob_grads(block_index):
        scores, key_start, key_part = masked_scores(block_index)
        probs_full = jnp.exp(scores - log_total[..., None])
        value_part = lax.dynamic_slice_in_dim(value_all, key_start, key_step, 0)
        grad_prob = jnp.einsum(
            "ckgd,nkd->kgcn", grad_attended, value_part, preferred_element_type=jnp.float32
        )
        return (probs_full, grad_prob, key_start, key_part)

    def delta_step(block_index, running):
        grads_here = prob_grads(block_index)
        return running + jnp.sum(grads_here[0] * grads_here[1], axis=-1)

    row_delta = lax.fori_loop(0, blocks_used, delta_step, jnp.zeros(stat_shape, jnp.float32))

    def grad_step(block_index, carry):
        query_acc, key_acc, value_acc = carry
        probs_full, grad_prob, key_start, key_part = prob_grads(block_index)
        grad_scores = (probs_full * (grad_prob - row_delta[..., None])).astype(jnp.bfloat16)
        query_acc = query_acc + jnp.einsum(
            "kgcn,nkd->ckgd", grad_scores, key_part, preferred_element_type=jnp.float32
        )
        key_term = (
            jnp.einsum(
                "kgcn,ckgd->nkd", grad_scores, query_group, preferred_element_type=jnp.float32
            )
            * score_scale
        )
        value_term = jnp.einsum(
            "kgcn,ckgd->nkd",
            probs_full.astype(jnp.bfloat16),
            grad_attended,
            preferred_element_type=jnp.float32,
        )
        key_old = lax.dynamic_slice_in_dim(key_acc, key_start, key_step, 0)
        value_old = lax.dynamic_slice_in_dim(value_acc, key_start, key_step, 0)
        key_acc = lax.dynamic_update_slice_in_dim(key_acc, key_old + key_term, key_start, 0)
        value_acc = lax.dynamic_update_slice_in_dim(value_acc, value_old + value_term, key_start, 0)
        return (query_acc, key_acc, value_acc)

    kv_zeros = jnp.zeros((seq_length, kv_local, HEAD_DIM), jnp.float32)
    query_acc, key_acc, value_acc = lax.fori_loop(
        0, blocks_used, grad_step, (jnp.zeros(head_shape, jnp.float32), kv_zeros, kv_zeros)
    )
    key_own, value_own = (
        lax.psum_scatter(
            key_acc.astype(jnp.bfloat16), "seq", scatter_dimension=0, tiled=True
        ).astype(jnp.float32),
        lax.psum_scatter(
            value_acc.astype(jnp.bfloat16), "seq", scatter_dimension=0, tiled=True
        ).astype(jnp.float32),
    )
    grad_query_rot = (query_acc * score_scale).reshape(span_len, query_heads, HEAD_DIM)
    grad_query_raw = (
        rotate(grad_query_rot, cos_tab, -sin_tab)
        .reshape(span_len, query_heads * HEAD_DIM)
        .astype(jnp.bfloat16)
    )
    grad_key_raw = (
        rotate(key_own, cos_tab, -sin_tab)
        .reshape(span_len, kv_local * HEAD_DIM)
        .astype(jnp.bfloat16)
    )
    grad_value_raw = value_own.reshape(span_len, kv_local * HEAD_DIM).astype(jnp.bfloat16)
    grad_query_w = jnp.einsum(
        "cd,ce->de", normed_one, grad_query_raw, preferred_element_type=jnp.float32
    )
    grad_key_w = jnp.einsum(
        "cd,ce->de", normed_one, grad_key_raw, preferred_element_type=jnp.float32
    )
    grad_value_w = jnp.einsum(
        "cd,ce->de", normed_one, grad_value_raw, preferred_element_type=jnp.float32
    )
    normed_part = jnp.einsum(
        "ce,de->cd", grad_query_raw, query_full, preferred_element_type=jnp.float32
    )
    normed_part = normed_part + jnp.einsum(
        "ce,de->cd", grad_key_raw, key_full, preferred_element_type=jnp.float32
    )
    normed_part = normed_part + jnp.einsum(
        "ce,de->cd", grad_value_raw, value_full, preferred_element_type=jnp.float32
    )
    gain_one_term = jnp.sum(normed_part * span_float * inv_one, axis=0)
    gain_block = jnp.broadcast_to(jnp.stack([gain_one_term, gain_two_term])[None], (tp_count, 2, D))
    grad_normed_one, gains_summed = (
        lax.psum_scatter(
            normed_part.astype(jnp.bfloat16), "tp", scatter_dimension=0, tiled=True
        ).astype(jnp.float32),
        lax.psum_scatter(
            gain_block.astype(jnp.bfloat16), "tp", scatter_dimension=0, tiled=True
        ).astype(jnp.float32),
    )
    gains_total = gains_summed[0]
    inv_rows = lax.dynamic_slice_in_dim(inv_one, tp_index * local_rows, local_rows, 0)
    scaled_one = grad_normed_one * gain_one
    grad_tokens = (
        grad_residual
        + inv_rows * scaled_one
        - token_rows
        * (inv_rows * inv_rows * inv_rows)
        * jnp.mean(scaled_one * token_rows, axis=-1, keepdims=True)
    )
    summed = (
        lax.psum_scatter(
            grad_query_w.astype(jnp.bfloat16), ("fsdp", "seq"), scatter_dimension=0, tiled=True
        ).astype(jnp.float32),
        lax.psum_scatter(
            grad_key_w.astype(jnp.bfloat16), ("fsdp", "seq"), scatter_dimension=0, tiled=True
        ).astype(jnp.float32),
        lax.psum_scatter(
            grad_value_w.astype(jnp.bfloat16), ("fsdp", "seq"), scatter_dimension=0, tiled=True
        ).astype(jnp.float32),
        lax.psum_scatter(
            grad_out_w.astype(jnp.bfloat16), ("fsdp", "seq"), scatter_dimension=1, tiled=True
        ).astype(jnp.float32),
        lax.psum_scatter(
            grad_gate_w.astype(jnp.bfloat16), ("fsdp", "seq"), scatter_dimension=0, tiled=True
        ).astype(jnp.float32),
        lax.psum_scatter(
            grad_up_w.astype(jnp.bfloat16), ("fsdp", "seq"), scatter_dimension=0, tiled=True
        ).astype(jnp.float32),
        lax.psum_scatter(
            grad_down_w.astype(jnp.bfloat16), ("fsdp", "seq"), scatter_dimension=1, tiled=True
        ).astype(jnp.float32),
        lax.psum_scatter(
            gains_total.astype(jnp.bfloat16), ("fsdp", "seq"), scatter_dimension=1, tiled=True
        ).astype(jnp.float32),
    )
    return (
        mixed_out,
        grad_tokens,
        summed[0],
        summed[1],
        summed[2],
        summed[3],
        summed[4],
        summed[5],
        summed[6],
        summed[7],
    )


VMEM_BYTES = 48 * 1024 * 1024
SMALL_COST = pl.CostEstimate(flops=1024, bytes_accessed=4096, transcendentals=0)


def to_core(value):
    return lax.ppermute(value, "fsdp", [(i, i ^ 1) for i in range(4)])


def to_x(value):
    return lax.ppermute(value, "fsdp", [(i, i ^ 2) for i in range(4)])


def to_z(value, step):
    return lax.ppermute(value, "seq", [(i, i ^ step) for i in range(4)])


def to_tp(value):
    return lax.ppermute(value, "tp", [(0, 1), (1, 0)])


def hold(value, *events):
    return lax.optimization_barrier((value, events))[0]


def float_of(value):
    return value.astype(jnp.float32)


def low_of(value):
    return value.astype(jnp.bfloat16)


def rows_dot(left, right):
    return lax.dot_general(left, right, (((0,), (0,)), ((), ())), preferred_element_type=jnp.float32)


def cols_dot(left, right):
    return lax.dot_general(left, right, (((1,), (1,)), ((), ())), preferred_element_type=jnp.float32)


def place_kernel(rows, place, pair, pair_far, plane, mine, held, read_sems, sems):
    reads = [
        pltpu.make_async_copy(
            (pair, pair_far)[k // 2].at[pl.ds((k % 2) * rows, rows), :], held.at[k], read_sems.at[k]
        )
        for k in range(4)
    ]
    for copy in reads:
        copy.start()
    writes = []
    for k, read in enumerate(reads):
        read.wait()
        start = pl.multiple_of((place[0] ^ k) * rows, 16)
        for i, target in enumerate((plane, mine)):
            write = pltpu.make_async_copy(
                held.at[k], target.at[pl.ds(start, rows), :], sems.at[2 * k + i]
            )
            write.start()
            writes.append(write)
    for write in writes:
        write.wait()


def place_rows(pair, pair_far, place):
    rows, columns = pair.shape[0] // 2, pair.shape[1]
    anywhere = pl.BlockSpec(memory_space=pl.ANY)
    return pl.pallas_call(
        lambda *refs: place_kernel(rows, *refs),
        out_shape=(
            jax.ShapeDtypeStruct((4 * rows, columns), jnp.bfloat16),
            jax.ShapeDtypeStruct((8 * rows, columns), jnp.bfloat16),
        ),
        in_specs=[pl.BlockSpec(memory_space=pltpu.SMEM)] + [anywhere] * 2,
        out_specs=(anywhere, anywhere),
        scratch_shapes=[
            pltpu.VMEM((4, rows, columns), jnp.bfloat16),
            pltpu.SemaphoreType.DMA((4,)),
            pltpu.SemaphoreType.DMA((8,)),
        ],
        cost_estimate=SMALL_COST,
        name="place_rows",
    )(place.reshape(1), pair, pair_far)


def fill_kernel(rows, part, start, across, first, mine, held, read_sems, sems):
    columns = pl.ds(start, mine.shape[1])
    reads = [
        pltpu.make_async_copy(
            across.at[pl.ds(k * part, part), columns], held.at[k], read_sems.at[k]
        )
        for k in range(rows // part)
    ]
    for copy in reads:
        copy.start()
    writes = []
    for k, read in enumerate(reads):
        read.wait()
        write = pltpu.make_async_copy(
            held.at[k], mine.at[pl.ds(rows + k * part, part), :], sems.at[k]
        )
        write.start()
        writes.append(write)
    for write in writes:
        write.wait()


def fill_rows(mine, across, start=0):
    rows, columns = across.shape[0], mine.shape[1]
    part = 128 if rows % 128 == 0 else 32
    anywhere = pl.BlockSpec(memory_space=pl.ANY)
    return pl.pallas_call(
        lambda *refs: fill_kernel(rows, part, start, *refs),
        out_shape=jax.ShapeDtypeStruct(mine.shape, mine.dtype),
        in_specs=[anywhere] * 2,
        out_specs=anywhere,
        scratch_shapes=[
            pltpu.VMEM((rows // part, part, columns), jnp.bfloat16),
            pltpu.SemaphoreType.DMA((rows // part,)),
            pltpu.SemaphoreType.DMA((rows // part,)),
        ],
        input_output_aliases={1: 0},
        cost_estimate=SMALL_COST,
        name="fill_rows",
    )(across, mine)


def take_rows_kernel(one, two, one_near, one_far, two_tp, two_far, out, sems):
    n, half = one.shape
    left, right = pl.ds(0, half), pl.ds(half, half)
    moves = [
        (one, pl.ds(0, n), left),
        (two, pl.ds(0, n), right),
        (one_near, pl.ds(2 * n, n), left),
        (one_far.at[pl.ds(0, n), :], pl.ds(n, n), left),
        (one_far.at[pl.ds(n, n), :], pl.ds(3 * n, n), left),
        (two_tp, pl.ds(n, n), right),
        (two_far, pl.ds(2 * n, 2 * n), right),
    ]
    copies = [
        pltpu.make_async_copy(source, out.at[rows, columns], sems.at[k])
        for k, (source, rows, columns) in enumerate(moves)
    ]
    for copy in copies:
        copy.start()
    for copy in copies:
        copy.wait()


def take_rows(*pieces):
    rows, half = pieces[0].shape
    return pl.pallas_call(
        take_rows_kernel,
        out_shape=jax.ShapeDtypeStruct((4 * rows, 2 * half), pieces[0].dtype),
        in_specs=[pl.BlockSpec(memory_space=pl.ANY)] * 6,
        out_specs=pl.BlockSpec(memory_space=pltpu.VMEM),
        scratch_shapes=[pltpu.SemaphoreType.DMA((7,))],
        compiler_params=pltpu.CompilerParams(vmem_limit_bytes=VMEM_BYTES),
        cost_estimate=SMALL_COST,
        name="take_rows",
    )(*pieces)


def dense_call(kernel, name, outs, scratch, args):
    whole = pl.BlockSpec(memory_space=pltpu.VMEM)
    return pl.pallas_call(
        kernel,
        out_shape=[jax.ShapeDtypeStruct(shape, kind) for shape, kind in outs],
        in_specs=[whole] * len(args),
        out_specs=[whole] * len(outs),
        scratch_shapes=scratch,
        compiler_params=pltpu.CompilerParams(vmem_limit_bytes=VMEM_BYTES),
        cost_estimate=SMALL_COST,
        name=name,
    )(*args)


def turned(value, cos_wide, sin_wide):
    half = HEAD_DIM // 2
    swapped = jnp.concatenate([value[:, half:], value[:, :half]], axis=1)
    return value * cos_wide + swapped * sin_wide


def rope_kernel(raw, cos_wide, sin_wide, query, kv):
    cos, sin = cos_wide[...], sin_wide[...]
    query_width, kv_width = query.shape[1], kv.shape[1] // 2
    for start in range(0, query_width, HEAD_DIM):
        columns = slice(start, start + HEAD_DIM)
        query[:, columns] = turned(raw[:, columns], cos, sin).astype(jnp.bfloat16)
    for start in range(0, kv_width, HEAD_DIM):
        columns = slice(query_width + start, query_width + start + HEAD_DIM)
        kv[:, start : start + HEAD_DIM] = turned(raw[:, columns], cos, sin).astype(jnp.bfloat16)
    values = raw[:, query_width + kv_width : query_width + 2 * kv_width]
    kv[:, kv_width:] = values.astype(jnp.bfloat16)


def pair_of(early, own, index):
    columns = slice(index * HEAD_DIM, (index + 1) * HEAD_DIM)
    return jnp.concatenate([early[:, columns], own[:, columns]], axis=0)


def attend_kernel(scale, query, early, own, query_ids, key_ids, attended, log_total, fill):
    kv_local = own.shape[1] // HEAD_DIM // 2
    rows_total = query.shape[0]
    half_rows = rows_total // 2
    for part in range(2):
        rows = slice(part * half_rows, (part + 1) * half_rows)
        allowed = (key_ids[:, 0:1] == query_ids[0:1, rows]) & (
            key_ids[:, 1:2] <= query_ids[1:2, rows]
        )
        fill[...] = jnp.where(allowed, 0.0, mask_fill)
        for kv in range(kv_local):
            keys = pair_of(early, own, kv)
            values = pair_of(early, own, kv_local + kv)
            for member in range(GROUP):
                head = kv * GROUP + member
                columns = slice(head * HEAD_DIM, (head + 1) * HEAD_DIM)
                scores = cols_dot(keys, query[rows, columns]) + fill[...]
                top = jnp.max(scores, axis=0, keepdims=True)
                weights = jnp.exp((scores - top) * scale)
                total = jnp.sum(weights, axis=0, keepdims=True)
                probs = (weights * (1.0 / total)).astype(jnp.bfloat16)
                attended[rows, columns] = rows_dot(values, probs).T.astype(jnp.bfloat16)
                log_total[head : head + 1, rows] = top * scale + jnp.log(total)


def attend_back_kernel(
    scale,
    query,
    early,
    own,
    query_ids,
    key_ids,
    log_total,
    grad_attended,
    cos_wide,
    sin_wide,
    grad_query,
    grad_early,
    grad_own,
    fill,
    all_probs,
    all_grads,
):
    kv_local = own.shape[1] // HEAD_DIM // 2
    rows_total = query.shape[0]
    half_rows = rows_total // 2
    for part in range(2):
        rows = slice(part * half_rows, (part + 1) * half_rows)
        allowed = (key_ids[:, 0:1] == query_ids[0:1, rows]) & (
            key_ids[:, 1:2] <= query_ids[1:2, rows]
        )
        fill[:, rows] = jnp.where(allowed, 0.0, mask_fill)
    for kv in range(kv_local):
        keys = pair_of(early, own, kv)
        values = pair_of(early, own, kv_local + kv)
        queries, outs = [], []
        for part in range(2):
            rows = slice(part * half_rows, (part + 1) * half_rows)
            cos, sin = cos_wide[rows, :], -sin_wide[rows, :]
            for member in range(GROUP):
                head = kv * GROUP + member
                columns = slice(head * HEAD_DIM, (head + 1) * HEAD_DIM)
                place = (part * GROUP + member) * half_rows
                where = slice(place, place + half_rows)
                one_query, one_out = query[rows, columns], grad_attended[rows, columns]
                queries.append(one_query)
                outs.append(one_out)
                scores = cols_dot(keys, one_query) + fill[:, rows]
                probs = jnp.exp(scores * scale - log_total[head : head + 1, rows])
                grad_probs = cols_dot(values, one_out)
                delta = jnp.sum(probs * grad_probs, axis=0, keepdims=True)
                grads = (probs * (grad_probs - delta)).astype(jnp.bfloat16)
                all_probs[:, where] = probs.astype(jnp.bfloat16)
                all_grads[:, where] = grads
                turned_grad = rows_dot(keys, grads).T * scale
                grad_query[rows, columns] = turned(turned_grad, cos, sin).astype(jnp.bfloat16)
        grad_keys = (
            jnp.dot(
                all_grads[...], jnp.concatenate(queries, axis=0), preferred_element_type=jnp.float32
            )
            * scale
        )
        grad_values = jnp.dot(
            all_probs[...], jnp.concatenate(outs, axis=0), preferred_element_type=jnp.float32
        )
        for start, grad in ((kv, grad_keys), (kv_local + kv, grad_values)):
            columns = slice(start * HEAD_DIM, (start + 1) * HEAD_DIM)
            grad_early[:, columns] = grad[:rows_total].astype(jnp.bfloat16)
            grad_own[:, columns] = grad[rows_total:]


def join_kernel(grad_query, grad_own, late, cos_wide, sin_wide, grad_raw):
    cos, sin = cos_wide[...], -sin_wide[...]
    query_width, kv_width = grad_query.shape[1], grad_own.shape[1] // 2
    grad_raw[:, :query_width] = grad_query[...]
    for start in range(0, kv_width, HEAD_DIM):
        columns = slice(start, start + HEAD_DIM)
        grad = grad_own[:, columns] + late[:, columns].astype(jnp.float32)
        grad_raw[:, query_width + start : query_width + start + HEAD_DIM] = turned(
            grad, cos, sin
        ).astype(jnp.bfloat16)
    values = grad_own[:, kv_width:] + late[:, kv_width:].astype(jnp.float32)
    used = query_width + 2 * kv_width
    grad_raw[:, query_width + kv_width : used] = values.astype(jnp.bfloat16)
    spare = grad_raw.shape[1] - used
    grad_raw[:, used:] = jnp.zeros((grad_raw.shape[0], spare), jnp.bfloat16)


def tiled_call(kernel, name, steps, in_specs, outs, args):
    return pl.pallas_call(
        kernel,
        grid=(steps,),
        out_shape=[jax.ShapeDtypeStruct(shape, kind) for shape, kind, _, _ in outs],
        in_specs=[pl.BlockSpec(block, index) for block, index in in_specs],
        out_specs=[pl.BlockSpec(block, index) for _, _, block, index in outs],
        compiler_params=pltpu.CompilerParams(vmem_limit_bytes=VMEM_BYTES),
        cost_estimate=SMALL_COST,
        name=name,
    )(*args)


def fixed(step):
    return (0, 0)


def by_row(step):
    return (step, 0)


def by_column(step):
    return (0, step)


def split_dot(left, mine, other):
    depth = mine.shape[0]
    first = jnp.dot(left[:, :depth], mine[...], preferred_element_type=jnp.float32)
    return first + jnp.dot(left[:, depth:], other[...], preferred_element_type=jnp.float32)


def project_kernel(start, left, mine, other, out):
    columns = slice(start, start + out.shape[1])
    depth = mine.shape[0]
    first = jnp.dot(left[:, :depth], mine[:, columns], preferred_element_type=jnp.float32)
    second = jnp.dot(left[:, depth:], other[:, columns], preferred_element_type=jnp.float32)
    out[...] = (first + second).astype(out.dtype)


def project(left, weights, start, columns, kind):
    mine, other = weights
    rows, depth = left.shape[0], mine.shape[0]
    tiled = start == 0 and columns % 512 == 0
    tile = 512 if tiled else columns
    block = (depth, tile) if tiled else mine.shape
    (out,) = tiled_call(
        functools.partial(project_kernel, start),
        "project",
        columns // tile,
        [(left.shape, fixed), (block, by_column), (block, by_column)],
        [((rows, columns), kind, (rows, tile), by_column)],
        (left, mine, other),
    )
    return out


def hidden_kernel(normed, gate_m, gate_o, up_m, up_o, hidden, gate_slope, up_slope):
    gate_pre = split_dot(normed, gate_m, gate_o)
    up_pre = split_dot(normed, up_m, up_o)
    sig_gate = 1.0 / (1.0 + jnp.exp(-gate_pre))
    silu_gate = gate_pre * sig_gate
    hidden[...] = (silu_gate * up_pre).astype(jnp.bfloat16)
    gate_slope[...] = up_pre * (sig_gate * (1.0 + gate_pre * (1.0 - sig_gate)))
    up_slope[...] = silu_gate


def hidden_units(normed, gate_weights, up_weights):
    rows = normed.shape[0]
    depth, columns = gate_weights[0].shape
    tile = 256
    outs = [
        ((rows, columns), kind, (rows, tile), by_column)
        for kind in (jnp.bfloat16, jnp.float32, jnp.float32)
    ]
    return tiled_call(
        hidden_kernel,
        "hidden_units",
        columns // tile,
        [(normed.shape, fixed)] + [((depth, tile), by_column)] * 4,
        outs,
        (normed, *gate_weights, *up_weights),
    )


def hidden_grad_kernel(cot, down_m, down_o, gate_slope, up_slope, gate_grad, up_grad):
    grad_hidden = split_dot(cot, down_m, down_o)
    gate_grad[...] = (grad_hidden * gate_slope[...]).astype(jnp.bfloat16)
    up_grad[...] = (grad_hidden * up_slope[...]).astype(jnp.bfloat16)


def hidden_grads(cot, down_weights, gate_slope, up_slope):
    rows = cot.shape[0]
    depth, columns = down_weights[0].shape
    tile = 256
    out = ((rows, columns), jnp.bfloat16, (rows, tile), by_column)
    return tiled_call(
        hidden_grad_kernel,
        "hidden_grads",
        columns // tile,
        [(cot.shape, fixed)]
        + [((depth, tile), by_column)] * 2
        + [((rows, tile), by_column)] * 2,
        [out] * 2,
        (cot, *down_weights, gate_slope, up_slope),
    )


def back_kernel(count, start, *refs):
    lefts, weights, outs = refs[:count], refs[count : 3 * count], refs[3 * count :]
    columns = slice(start, start + lefts[0].shape[1])
    sums = []
    for half in range(2):
        terms = [
            cols_dot(left[...], weights[2 * i + half][:, columns]) for i, left in enumerate(lefts)
        ]
        sums.append(sum(terms).astype(jnp.bfloat16))
    one, two = sums
    one_keep, one_send, two_keep, two_send = outs
    n = one.shape[0] // 4
    one_keep[:n, :], one_send[:n, :] = one[:n], one[n : 2 * n]
    one_keep[n:, :], one_send[n:, :] = one[2 * n : 3 * n], one[3 * n :]
    two_keep[...], two_send[...] = two[: 2 * n], two[2 * n :]


def project_back(lefts, weights, start=0):
    rows, width = lefts[0].shape
    depth = weights[0][0].shape[0]
    tile = 256
    flat = [half for pair in weights for half in pair]
    return tiled_call(
        functools.partial(back_kernel, len(lefts), start),
        "project_back",
        depth // tile,
        [((rows, width), fixed)] * len(lefts) + [((tile, flat[0].shape[1]), by_row)] * len(flat),
        [((rows // 2, depth), jnp.bfloat16, (rows // 2, tile), by_column)] * 4,
        (*lefts, *flat),
    )


def outer_kernel(left, left_other, right, *refs):
    others, out = refs[:-1], refs[-1]
    total = rows_dot(left[...], right[...])
    rows = left.shape[0] // len(others)
    for i, other in enumerate(others):
        total = total + rows_dot(left_other[i * rows : (i + 1) * rows, :], other[...])
    out[...] = total.astype(jnp.bfloat16)


def outer(left, left_others, right, right_others, index):
    rows, width = left.shape[0], right.shape[1]
    left_other = left_others[index]
    depth = left_other.shape[1]
    tile = 256 if width % 256 == 0 else width
    (out,) = tiled_call(
        outer_kernel,
        "outer",
        width // tile,
        [((rows, depth), lambda step: (0, index)), ((rows, depth), fixed)]
        + [((rows, tile), by_column)]
        + [((other.shape[0], tile), by_column) for other in right_others],
        [((depth, width), jnp.bfloat16, (depth, tile), by_column)],
        (left, left_other, right, *right_others),
    )
    return out


def norm_kernel(rows, gain, out):
    value = rows[...].astype(jnp.float32)
    scale = lax.rsqrt(jnp.mean(value * value, axis=1, keepdims=True) + norm_eps)
    out[...] = (value * scale * gain[...]).astype(jnp.bfloat16)


def norm_rows(rows, gain):
    count, width = rows.shape
    tile = count // 4
    (out,) = tiled_call(
        norm_kernel,
        "norm_rows",
        4,
        [((tile, width), by_row), ((1, width), fixed)],
        [((count, width), jnp.bfloat16, (tile, width), by_row)],
        (rows, gain.reshape(1, width)),
    )
    return out


def take_wide_kernel(own, from_near, from_tp, out, sems):
    n = own.shape[0]
    moves = [
        (own, pl.ds(0, n)),
        (from_tp.at[pl.ds(0, n), :], pl.ds(n, n)),
        (from_near, pl.ds(2 * n, n)),
        (from_tp.at[pl.ds(n, n), :], pl.ds(3 * n, n)),
    ]
    copies = [
        pltpu.make_async_copy(source, out.at[rows, :], sems.at[k])
        for k, (source, rows) in enumerate(moves)
    ]
    for copy in copies:
        copy.start()
    for copy in copies:
        copy.wait()


def take_wide(own, from_near, from_tp):
    return pl.pallas_call(
        take_wide_kernel,
        out_shape=jax.ShapeDtypeStruct((4 * own.shape[0], own.shape[1]), own.dtype),
        in_specs=[pl.BlockSpec(memory_space=pl.ANY)] * 3,
        out_specs=pl.BlockSpec(memory_space=pltpu.VMEM),
        scratch_shapes=[pltpu.SemaphoreType.DMA((4,))],
        compiler_params=pltpu.CompilerParams(vmem_limit_bytes=VMEM_BYTES),
        cost_estimate=SMALL_COST,
        name="take_wide",
    )(own, from_near, from_tp)


def rows_call(fn, name, where, steps, ins, outs):
    def kernel(where_ref, *refs):
        values = [ref[...].astype(jnp.float32) for ref in refs[: len(ins)]]
        for ref, value in zip(refs[len(ins) :], fn(*values)):
            ref[...] = value.astype(ref.dtype)

    def spec(rows, columns, place):
        return pl.BlockSpec((rows, columns), lambda step, ref: (place(step, ref), 0))

    return pl.pallas_call(
        kernel,
        grid_spec=pltpu.PrefetchScalarGridSpec(
            num_scalar_prefetch=1,
            grid=(steps,),
            in_specs=[spec(rows, array.shape[1], place) for array, rows, place in ins],
            out_specs=[spec(rows, shape[1], place) for shape, _, rows, place in outs],
        ),
        out_shape=[jax.ShapeDtypeStruct(shape, kind) for shape, kind, _, _ in outs],
        compiler_params=pltpu.CompilerParams(vmem_limit_bytes=VMEM_BYTES),
        cost_estimate=SMALL_COST,
        name=name,
    )(where, *[array for array, _, _ in ins])


def far_halves(where, *terms):
    rows = terms[0][0].shape[0] // 4
    columns = sum(own.shape[1] for own, _ in terms)
    keep, give = (lambda step, ref: 2 * ref[0] + step), (lambda step, ref: 2 - 2 * ref[0] + step)
    out = ((2 * rows, columns), jnp.bfloat16, rows, lambda step, ref: step)
    count = len(terms)

    def sums(*values):
        pairs = [values[2 * i] + values[2 * i + 1] for i in range(2 * count)]
        if count == 1:
            return pairs
        return jnp.concatenate(pairs[:count], axis=1), jnp.concatenate(pairs[count:], axis=1)

    return rows_call(
        sums,
        "far_halves",
        where,
        2,
        [(array, rows, place) for place in (keep, give) for pair in terms for array in pair],
        [out, out],
    )


def near_halves(where, pair, from_far):
    rows, columns = pair.shape[0] // 2, pair.shape[1]
    keep, give = (lambda step, ref: ref[1]), (lambda step, ref: 1 - ref[1])
    out = ((rows, columns), jnp.bfloat16, rows, lambda step, ref: 0)
    return rows_call(
        lambda a, b, c, d: (a + b, c + d),
        "near_halves",
        where,
        1,
        [(array, rows, place) for place in (keep, give) for array in (pair, from_far)],
        [out, out],
    )


def join_halves_kernel(turn, where, own, received, *outs):
    first = where[1] == 0
    low_part = jnp.where(first, own[...], received[...]).astype(jnp.float32)
    high_part = jnp.where(first, received[...], own[...]).astype(jnp.float32)
    start = 0
    for out in outs:
        width = out.shape[0] if turn else out.shape[1]
        if len(outs) == 1:
            size = own.shape[1]
            rest = width - size
        else:
            size = rest = width // 2
        left, right = low_part[:, start : start + size], high_part[:, start : start + rest]
        if turn:
            out[:size, :] = left.T
            out[size:, :] = right.T
        else:
            out[:, :size] = left
            out[:, size:] = right
        start += size


def join_halves(where, own, received, widths, turn=False):
    rows = own.shape[0]
    shapes = [(width, rows) if turn else (rows, width) for width in widths]
    whole = pl.BlockSpec(memory_space=pltpu.VMEM)
    return pl.pallas_call(
        functools.partial(join_halves_kernel, turn),
        out_shape=[jax.ShapeDtypeStruct(shape, jnp.float32) for shape in shapes],
        in_specs=[pl.BlockSpec(memory_space=pltpu.SMEM), whole, whole],
        out_specs=[whole] * len(shapes),
        compiler_params=pltpu.CompilerParams(vmem_limit_bytes=VMEM_BYTES),
        cost_estimate=SMALL_COST,
        name="join_halves",
    )(where, own, received)


def split_halves_kernel(plan, where, *refs):
    arrays, pairs, other = refs[: len(plan)], refs[len(plan) : -1], refs[-1]
    rows = other.shape[0]
    first = where[1] == 0
    offset = 0
    filled = [0] * len(pairs)
    for index, (array, (target, size, turn)) in enumerate(zip(arrays, plan)):
        value = array[...]
        if turn:
            value = value.astype(jnp.float32).T.astype(jnp.bfloat16)
        low_part, high_part = value[:, :size], value[:, size:]
        missing = size - high_part.shape[1]
        if missing:
            high_part = jnp.concatenate(
                [high_part, jnp.zeros((rows, missing), jnp.bfloat16)], axis=1
            )
        start = filled[target]
        pair = pairs[target]
        pair[:rows, start : start + size] = jnp.where(first, low_part, high_part)
        other[:, offset + start : offset + start + size] = jnp.where(first, high_part, low_part)
        filled[target] = start + size
        if index + 1 == len(plan) or plan[index + 1][0] != target:
            spare = pair.shape[1] - filled[target]
            if spare:
                pair[:rows, filled[target] :] = jnp.zeros((rows, spare), jnp.bfloat16)
                end = offset + pair.shape[1]
                other[:, end - spare : end] = jnp.zeros((rows, spare), jnp.bfloat16)
            offset += pair.shape[1]


def split_halves(where, arrays, plan, widths):
    rows = D // 16
    whole = pl.BlockSpec(memory_space=pltpu.VMEM)
    return pl.pallas_call(
        functools.partial(split_halves_kernel, plan),
        out_shape=[jax.ShapeDtypeStruct((2 * rows, width), jnp.bfloat16) for width in widths]
        + [jax.ShapeDtypeStruct((rows, sum(widths)), jnp.bfloat16)],
        in_specs=[pl.BlockSpec(memory_space=pltpu.SMEM)] + [whole] * len(arrays),
        out_specs=[whole] * (len(widths) + 1),
        compiler_params=pltpu.CompilerParams(vmem_limit_bytes=VMEM_BYTES),
        cost_estimate=SMALL_COST,
        name="split_halves",
    )(where, *arrays)


def pair_kernel(first, second, out):
    n = first.shape[0]
    out[:n, :] = first[...]
    out[n:, :] = second[...]


def pair_rows(first, second):
    rows, columns = first.shape
    (out,) = dense_call(
        pair_kernel, "pair_rows", [((2 * rows, columns), first.dtype)], [], (first, second)
    )
    return out


def middle_kernel(one, got_one, two, got_two, next_one, next_two, sum_one, sum_two):
    n = sum_one.shape[0]
    for keep, got, later, total in (
        (one, got_one, next_one, sum_one),
        (two, got_two, next_two, sum_two),
    ):
        both = keep[...].astype(jnp.float32) + got[...].astype(jnp.float32)
        total[...] = both[:n]
        later[...] = both[n:].astype(jnp.bfloat16)


def scatter_middle(one, got_one, two, got_two):
    rows, columns = one.shape[0] // 2, one.shape[1]
    return dense_call(
        middle_kernel,
        "scatter_middle",
        [((rows, columns), jnp.bfloat16)] * 2 + [((rows, columns), jnp.float32)] * 2,
        [],
        (one, got_one, two, got_two),
    )


def summed(sum_one, sum_two, last_one, last_two):
    one = sum_one[...] + last_one[...].astype(jnp.float32)
    two = sum_two[...] + last_two[...].astype(jnp.float32)
    return jnp.concatenate([one, two], axis=1)


def store_halves(value, one, two):
    half = one.shape[1]
    one[...] = value[:, :half].astype(one.dtype)
    two[...] = value[:, half:].astype(two.dtype)


def residual_kernel(sum_one, sum_two, last_one, last_two, rows, gain, residual, one, two):
    value = rows[...].astype(jnp.float32) + summed(sum_one, sum_two, last_one, last_two)
    residual[...] = value
    scale = lax.rsqrt(jnp.mean(value * value, axis=1, keepdims=True) + norm_eps)
    store_halves(value * scale * gain[...], one, two)


def norm_grad(grad, value, gain):
    scale = lax.rsqrt(jnp.mean(value * value, axis=1, keepdims=True) + norm_eps)
    scaled = grad * gain
    inner = jnp.mean(scaled * value, axis=1, keepdims=True)
    gain_term = jnp.sum(grad * value * scale, axis=0, keepdims=True)
    return scale * scaled - value * (scale * scale * scale) * inner, gain_term


def residual_grad_kernel(
    sum_one, sum_two, last_one, last_two, residual, gain, cot, grad, gain_term, one, two
):
    back, term = norm_grad(summed(sum_one, sum_two, last_one, last_two), residual[...], gain[...])
    value = cot[...].astype(jnp.float32) + back
    grad[...] = value
    gain_term[...] = term
    store_halves(value, one, two)


def token_grad_kernel(
    sum_one, sum_two, last_one, last_two, rows, gain, grad_residual, grad
):
    value = rows[...].astype(jnp.float32)
    back, _ = norm_grad(summed(sum_one, sum_two, last_one, last_two), value, gain[...])
    grad[...] = grad_residual[...] + back


def gain_kernel(one_keep, one_send, two_keep, two_send, rows, out):
    n, half = one_keep.shape[0] // 2, one_keep.shape[1]
    low_half, high_half = slice(0, n), slice(n, 2 * n)
    ones = (one_keep, low_half), (one_send, low_half), (one_keep, high_half), (one_send, high_half)
    twos = (two_keep, low_half), (two_keep, high_half), (two_send, low_half), (two_send, high_half)
    left = right = 0.0
    for k in range(4):
        value = rows[k * n : (k + 1) * n, :].astype(jnp.float32)
        scale = lax.rsqrt(jnp.mean(value * value, axis=1, keepdims=True) + norm_eps)
        value = value * scale
        one = ones[k][0][ones[k][1], :].astype(jnp.float32)
        two = twos[k][0][twos[k][1], :].astype(jnp.float32)
        left = left + jnp.sum(one * value[:, :half], axis=0, keepdims=True)
        right = right + jnp.sum(two * value[:, half:], axis=0, keepdims=True)
    out[:, :half] = left
    out[:, half:] = right


def mixed_kernel(sum_one, sum_two, last_one, last_two, residual, mixed):
    total = residual[...] + summed(sum_one, sum_two, last_one, last_two)
    mixed[...] = total.astype(jnp.bfloat16)


def half_plan(
    tokens, doc_lengths, w_query, w_key, w_value, w_out, w_gate, w_up, w_down, norm_gains, cotangent
):
    fsdp_index = lax.axis_index("fsdp")
    seq_index = lax.axis_index("seq")
    tp_index = lax.axis_index("tp")
    near = seq_index % 2
    far = seq_index // 2
    local_rows = tokens.shape[0]
    group_rows = 4 * local_rows
    middle = D // 2
    quarter = D // 4
    block_rows = D // 16
    score_scale = 1.0 / math.sqrt(HEAD_DIM)

    def columns_in(value):
        return jnp.concatenate(
            [
                lax.dynamic_slice_in_dim(value, (fsdp_index ^ k) * quarter, quarter, 1)
                for k in (0, 2, 1, 3)
            ],
            axis=1,
        )

    def columns_out(value):
        pieces = []
        for block in range(4):
            k = fsdp_index ^ block
            place = (k // 2) + (k % 2) * 2
            pieces.append(lax.dynamic_slice_in_dim(value, place * quarter, quarter, 1))
        return jnp.concatenate(pieces, axis=1)

    def gather_first(one, two):
        return one, two, to_z(one, 1), to_tp(two)

    def gather_second(one, two, one_near, two_tp):
        one_far = to_tp(pair_rows(one, one_near))
        two_far = to_z(pair_rows(two, two_tp), 1)
        return one, two, one_near, one_far, two_tp, two_far

    def scatter_first(one_keep, one_send, two_keep, two_send):
        return one_keep, to_tp(one_send), two_keep, to_z(two_send, 1)

    def scatter_second(next_one, next_two, sum_one, sum_two):
        return sum_one, sum_two, to_z(next_one, 1), to_tp(next_two)

    where = jnp.stack([far, near]).astype(jnp.int32)
    query_width = w_query.shape[1] // 2
    key_width = w_key.shape[1] // 2
    query_heads = query_width // HEAD_DIM
    heads_width = -(-(query_width + 2 * key_width) // 128) * 128
    hidden_width = -(-(w_gate.shape[1] // 2) // 128) * 128
    row_shape = (local_rows, D)
    half_shape = (local_rows, middle)

    def cross_left(value, *events):
        first, second = value[:, middle : middle + quarter], value[:, middle + quarter :]
        return to_core(hold(first, events)), to_core(hold(second, events))

    def cross_right(value, count):
        rows = value.shape[0] // count
        return tuple(to_core(value[i * rows : (i + 1) * rows]) for i in range(count))

    tokens_in = columns_in(tokens)
    cot_in = columns_in(cotangent)
    first_width = heads_width + query_width
    plan = ((0, query_width, False), (0, key_width, False), (0, key_width, False))
    spare = heads_width - query_width - 2 * key_width
    first_pair, first_other = split_halves(
        where,
        (w_query, w_key, w_value, jnp.zeros((block_rows, 2 * spare), jnp.bfloat16), w_out),
        (*plan, (0, spare, False), (0, query_width, True)),
        (first_width,),
    )
    gain_stack = norm_gains[None]
    gain_stack = jnp.concatenate([gain_stack, to_z(gain_stack, 1)], axis=0)
    first_near = to_z(first_other, 1)
    token_wait = gather_first(tokens_in[:, :middle], tokens_in[:, middle:])
    gain_far = to_z(hold(gain_stack, token_wait[2:]), 2)
    gain_stack = jnp.concatenate([gain_stack, gain_far], axis=0)
    first_pair = fill_rows(*hold((first_pair, first_near), gain_stack))
    first_far = to_z(first_pair, 2)
    token_wait = gather_second(*hold(token_wait, first_pair))
    gate_pair, gate_other = split_halves(
        where, (w_gate,), ((0, hidden_width, False),), (hidden_width,)
    )
    up_pair, up_other = split_halves(where, (w_up,), ((0, hidden_width, False),), (hidden_width,))
    down_pair, down_other = split_halves(
        where, (w_down,), ((0, hidden_width, True),), (hidden_width,)
    )
    gate_near = to_z(hold(gate_other, first_pair), 1)
    token_wait = hold(token_wait, gate_other, up_other, down_other)
    gain_plane = jnp.concatenate(
        [
            lax.dynamic_index_in_dim(gain_stack, seq_index ^ k, 0, keepdims=False)
            for k in range(4)
        ],
        axis=1,
    )
    gain_mine = jnp.concatenate([gain_plane, to_x(gain_plane)], axis=1)
    gains = float_of(jnp.concatenate([gain_mine, to_core(gain_mine)], axis=1))
    gain_one = gains[0:1]
    gain_two = gains[1:2]
    token_span = take_rows(*hold(token_wait, gains))

    row_ids = jnp.arange(local_rows, dtype=jnp.int32)
    own_positions = jnp.concatenate(
        [
            far * (2 * 2 * local_rows)
            + (near ^ i) * (2 * local_rows)
            + (tp_index ^ j) * local_rows
            + row_ids
            for i in range(2)
            for j in range(2)
        ]
    )
    cos_tab, sin_tab = rope_tables(own_positions)
    cos_wide = jnp.concatenate([cos_tab, cos_tab], axis=1)
    sin_wide = jnp.concatenate([-sin_tab, sin_tab], axis=1)
    key_positions = jnp.concatenate([own_positions - group_rows, own_positions])
    doc_ends = jnp.cumsum(doc_lengths[0])[: DOCS - 1]

    def doc_of(positions):
        return jnp.sum((positions[:, None] >= doc_ends[None, :]).astype(jnp.int32), axis=1)

    key_docs = jnp.where(key_positions >= 0, doc_of(key_positions), -1)
    query_ids = jnp.stack([doc_of(own_positions), own_positions // BLOCK])
    key_ids = jnp.stack([key_docs, key_positions // BLOCK], axis=1)

    gate_pair = fill_rows(*hold((gate_pair, gate_near), token_span))
    first_plane, first_mine = place_rows(*hold((first_pair, first_far), gate_pair), seq_index)
    first_x = to_x(first_plane)
    gate_far = to_z(hold(gate_pair, first_plane), 2)
    normed_one = norm_rows(hold(token_span, first_plane), gain_one)
    normed_other = cross_left(normed_one)
    up_pair = fill_rows(up_pair, to_z(hold(up_other, first_plane), 1))
    down_pair = fill_rows(down_pair, to_z(hold(down_other, first_plane), 1))
    cot_first = gather_first(*hold((cot_in[:, :middle], cot_in[:, middle:]), up_pair))
    gate_plane, gate_mine = place_rows(
        *hold((gate_pair, gate_far), cot_first[2:], down_pair, normed_one), seq_index
    )
    first_mine = fill_rows(*hold((first_mine, first_x), gate_plane))
    first_weights = first_mine, to_core(first_mine)
    gate_x = to_x(hold(gate_plane, first_mine))
    up_far = to_z(hold(up_pair, gate_plane), 2)
    cot_wait = gather_second(*hold(cot_first, first_mine))
    raw = project(normed_one, first_weights, 0, heads_width, jnp.float32)
    query_rot, own_kv = dense_call(
        rope_kernel,
        "rope",
        [
            ((group_rows, query_width), jnp.bfloat16),
            ((group_rows, 2 * key_width), jnp.bfloat16),
        ],
        [],
        (raw, cos_wide, sin_wide),
    )
    cot_span = take_rows(*hold(cot_wait, own_kv))
    up_plane, up_mine = place_rows(*hold((up_pair, up_far), cot_span), seq_index)
    early_kv = lax.ppermute(hold(own_kv, up_plane), "seq", [(0, 2), (1, 3)])
    gate_mine = fill_rows(*hold((gate_mine, gate_x), up_plane))
    gate_weights = gate_mine, to_core(gate_mine)
    up_x = to_x(hold(up_plane, gate_mine))
    attended_low, log_total = dense_call(
        functools.partial(attend_kernel, score_scale),
        "attend",
        [
            ((group_rows, query_width), jnp.bfloat16),
            ((query_heads, group_rows), jnp.float32),
        ],
        [pltpu.VMEM((2 * group_rows, group_rows // 2), jnp.float32)],
        (query_rot, early_kv, own_kv, query_ids, key_ids),
    )
    attended_other = cross_right(attended_low, 1)
    down_far = to_z(hold(down_pair, log_total), 2)
    branch = scatter_first(
        *project_back([hold(attended_low, normed_other)], [first_weights], heads_width)
    )
    branch = scatter_middle(*hold(branch, attended_other))
    branch = scatter_second(*branch)
    down_plane, down_mine = place_rows(*hold((down_pair, down_far), branch[:2]), seq_index)
    up_mine = fill_rows(*hold((up_mine, up_x), down_plane))
    up_weights = up_mine, to_core(up_mine)
    down_x = to_x(hold(down_plane, up_mine))
    residual, two_one, two_two = dense_call(
        residual_kernel,
        "residual",
        [(row_shape, jnp.float32)] + [(half_shape, jnp.bfloat16)] * 2,
        [],
        (*hold(branch, up_mine), tokens_in, gain_two),
    )
    two_wait = gather_second(*gather_first(two_one, two_two))
    span_two = take_rows(*two_wait)
    span_other = cross_left(span_two)
    cot_other = cross_left(cot_span, log_total)
    hidden_low, gate_slope, up_slope = hidden_units(
        hold(span_two, cot_other), gate_weights, up_weights
    )
    hidden_other = cross_right(hidden_low, 1)
    down_mine = fill_rows(*hold((down_mine, down_x), hidden_low))
    down_weights = down_mine, to_core(down_mine)

    down_parts = hold((cot_span, cot_other, hidden_low, hidden_other), down_mine, span_other)
    down_give = outer(*down_parts, 1)
    down_back = to_x(down_give)
    down_keep = outer(*hold(down_parts, down_give), 0)
    mlp_parts = project_back([hold(hidden_low, down_keep)], [down_weights])
    grad_gate_pre, grad_up_pre = hidden_grads(
        hold(cot_span, mlp_parts), down_weights, gate_slope, up_slope
    )
    gate_other = cross_right(grad_gate_pre, 1)
    up_other = cross_right(grad_up_pre, 1)
    branch_mlp = scatter_first(*mlp_parts)
    back_parts = project_back(
        [grad_gate_pre, grad_up_pre], [gate_weights, up_weights]
    )
    branch_mlp = scatter_middle(*hold(branch_mlp, back_parts))
    normed_back = scatter_first(*hold(back_parts, branch_mlp))
    down_keep, down_give = far_halves(where, hold((down_keep, down_back), branch_mlp))
    down_far = to_z(down_give, 2)
    gate_parts = hold((span_two, span_other, grad_gate_pre, gate_other), down_give)
    gate_give = outer(*gate_parts, 1)
    gate_back = to_x(gate_give)
    normed_back = scatter_second(*scatter_middle(*hold(normed_back, gate_give)))
    gate_keep = outer(*hold(gate_parts, normed_back[:2]), 0)
    up_parts = hold((span_two, span_other, grad_up_pre, up_other), gate_keep)
    up_give = outer(*up_parts, 1)
    up_keep = outer(*hold(up_parts, up_give), 0)
    grad_residual, gain_two_term, grad_one, grad_two = dense_call(
        residual_grad_kernel,
        "residual_grad",
        [(row_shape, jnp.float32), ((1, D), jnp.float32)] + [(half_shape, jnp.bfloat16)] * 2,
        [],
        (*hold(normed_back, up_keep), residual, gain_two, cot_in),
    )
    grad_wait = gather_first(grad_one, grad_two)
    down_own, down_other = near_halves(where, *hold((down_keep, down_far), grad_wait[2:]))
    gate_keep, gate_give = far_halves(where, hold((gate_keep, gate_back), down_other))
    gate_far = to_z(gate_give, 2)
    up_back = to_x(hold(up_give, gate_give))
    grad_wait = gather_second(*hold(grad_wait, gate_give))
    grad_span = take_rows(*grad_wait)
    down_near = to_z(hold(down_other, grad_span), 1)
    span_grad_other = cross_left(grad_span)
    grad_attended = project(grad_span, first_weights, heads_width, query_width, jnp.bfloat16)
    grad_query, grad_early, grad_own = dense_call(
        functools.partial(attend_back_kernel, score_scale),
        "attend_back",
        [
            ((group_rows, query_width), jnp.bfloat16),
            ((group_rows, 2 * key_width), jnp.bfloat16),
            ((group_rows, 2 * key_width), jnp.float32),
        ],
        [
            pltpu.VMEM((2 * group_rows, group_rows), jnp.float32),
            pltpu.VMEM((2 * group_rows, GROUP * group_rows), jnp.bfloat16),
            pltpu.VMEM((2 * group_rows, GROUP * group_rows), jnp.bfloat16),
        ],
        (
            query_rot,
            early_kv,
            own_kv,
            query_ids,
            key_ids,
            log_total,
            grad_attended,
            cos_wide,
            sin_wide,
        ),
    )
    gate_own, gate_other = near_halves(where, *hold((gate_keep, gate_far), grad_early))
    up_terms = hold((up_keep, up_back), gate_other, down_near)
    late_kv = lax.ppermute(hold(grad_early, up_terms[1]), "seq", [(2, 0), (3, 1)])
    out_parts = hold((grad_span, span_grad_other, attended_low, attended_other), up_terms[1])
    gate_near = to_z(hold(gate_other, up_terms[1]), 1)
    out_give = outer(*out_parts, 1)
    out_back = to_x(out_give)
    out_keep = outer(*out_parts, 0)
    both_keep, both_give = far_halves(where, up_terms, hold((out_keep, out_back), late_kv, gate_near))
    both_far = to_z(both_give, 2)
    branch_mlp = scatter_second(*hold(branch_mlp, both_give))
    (grad_raw,) = dense_call(
        join_kernel,
        "join",
        [((group_rows, heads_width), jnp.bfloat16)],
        [],
        (grad_query, grad_own, hold(late_kv, both_give), cos_wide, sin_wide),
    )
    raw_other = cross_right(grad_raw, 2)
    first_parts = project_back([grad_raw], [first_weights])
    first_back = scatter_first(*first_parts)
    heads_parts = hold((normed_one, normed_other, grad_raw, raw_other), first_parts)
    heads_give = outer(*heads_parts, 1)
    heads_back = to_x(heads_give)
    heads_keep = outer(*heads_parts, 0)
    units = w_gate.shape[1]
    (gain_one_term,) = dense_call(
        gain_kernel,
        "gain",
        [((1, D), jnp.float32)],
        [],
        (*hold(first_parts, heads_keep), token_span),
    )
    gain_rows = jnp.concatenate([gain_one_term, gain_two_term], axis=0)
    gain_rows = gain_rows[:, :middle] + to_core(gain_rows[:, middle:])
    gain_rows = gain_rows + to_tp(gain_rows)
    first_back = scatter_middle(*hold(first_back, gain_rows))
    heads_keep, heads_give = far_halves(where, hold((heads_keep, heads_back), first_back))
    heads_far = to_z(heads_give, 2)
    gain_rows = hold(gain_rows, heads_give)
    gain_rows = gain_rows[:, :quarter] + to_x(gain_rows[:, quarter:])
    both_own, both_other = near_halves(
        where, *hold((both_keep, both_far), heads_give, gain_rows, branch_mlp[2:])
    )
    both_near = to_z(both_other, 1)
    first_back = scatter_second(*hold(first_back, both_other))
    (grad_rows,) = dense_call(
        token_grad_kernel,
        "token_grad",
        [(row_shape, jnp.float32)],
        [],
        (*first_back, tokens_in, gain_one, grad_residual),
    )
    gain_blocks = hold(gain_rows, both_other).reshape(2, 4, block_rows)
    gain_pair = [
        lax.dynamic_index_in_dim(gain_blocks, seq_index ^ k, 1, keepdims=False) for k in range(4)
    ]
    gain_half = jnp.stack(gain_pair[:2]) + to_z(jnp.stack(gain_pair[2:]), 2)
    gain_grads = gain_half[0] + to_z(gain_half[1], 1)
    heads_own, heads_other = near_halves(
        where, *hold((heads_keep, heads_far), grad_rows, both_near)
    )
    heads_near = to_z(heads_other, 1)
    (grad_down,) = join_halves(where, *hold((down_own, down_near), heads_other), (units,), True)
    (grad_gate,) = join_halves(where, *hold((gate_own, gate_near), grad_down), (units,))
    (mixed,) = dense_call(
        mixed_kernel,
        "mixed",
        [(row_shape, jnp.bfloat16)],
        [],
        (*hold(branch_mlp, grad_gate), residual),
    )
    both_own, both_near = hold((both_own, both_near), grad_gate)
    (grad_up,) = join_halves(
        where,
        *hold((both_own[:, :hidden_width], both_near[:, :hidden_width]), heads_other),
        (units,),
    )
    (grad_out,) = join_halves(
        where, both_own[:, hidden_width:], both_near[:, hidden_width:], (w_out.shape[0],), True
    )
    grad_query_w, grad_key_w, grad_value_w = join_halves(
        where,
        *hold((heads_own, heads_near), grad_out, grad_up),
        (2 * query_width, 2 * key_width, 2 * key_width),
    )
    mixed_out = columns_out(mixed)
    grad_tokens = columns_out(hold(grad_rows, grad_out))
    return (
        mixed_out,
        grad_tokens,
        grad_query_w,
        grad_key_w,
        grad_value_w,
        grad_out,
        grad_gate,
        grad_up,
        grad_down,
        gain_grads,
    )


def solution(mesh):
    halves = mesh.shape["seq"] == 4 and mesh.shape["tp"] == 2 and mesh.shape["fsdp"] == 4
    plan = half_plan if halves else per_device
    in_specs = (
        P(("fsdp", "seq", "tp"), None),
        P("fsdp", None),
        P(("fsdp", "seq"), "tp"),
        P(("fsdp", "seq"), "tp"),
        P(("fsdp", "seq"), "tp"),
        P("tp", ("fsdp", "seq")),
        P(("fsdp", "seq"), "tp"),
        P(("fsdp", "seq"), "tp"),
        P("tp", ("fsdp", "seq")),
        P(None, ("fsdp", "seq")),
        P(("fsdp", "seq", "tp"), None),
    )
    out_specs = (
        P(("fsdp", "seq", "tp"), None),
        P(("fsdp", "seq", "tp"), None),
        P(("fsdp", "seq"), "tp"),
        P(("fsdp", "seq"), "tp"),
        P(("fsdp", "seq"), "tp"),
        P("tp", ("fsdp", "seq")),
        P(("fsdp", "seq"), "tp"),
        P(("fsdp", "seq"), "tp"),
        P("tp", ("fsdp", "seq")),
        P(None, ("fsdp", "seq")),
    )
    return jax.shard_map(
        plan, mesh=mesh, in_specs=in_specs, out_specs=out_specs, check_vma=False
    )
```

```python
import functools
import math

import jax
import jax.numpy as jnp
from jax import lax
from jax.experimental import pallas as pl
from jax.experimental.pallas import tpu as pltpu
from jax.sharding import PartitionSpec as P

D = 2560
HEAD_DIM = 80
BLOCK = 256
DOCS = 3
GROUP = 4


norm_eps = 1e-05
rope_base = 10000.0
mask_fill = -1000000000.0


def rope_tables(positions):
    half_dim = HEAD_DIM // 2
    freq_row = rope_base ** (-jnp.arange(half_dim, dtype=jnp.float32) * 2.0 / HEAD_DIM)
    angles = positions.astype(jnp.float32)[:, None] * freq_row[None, :]
    return (jnp.cos(angles), jnp.sin(angles))


def rotate(values, cos_tab, sin_tab):
    half_dim = HEAD_DIM // 2
    first_half = values[..., :half_dim]
    second_half = values[..., half_dim:]
    cos_wide = cos_tab[:, None, :]
    sin_wide = sin_tab[:, None, :]
    return jnp.concatenate(
        [
            first_half * cos_wide - second_half * sin_wide,
            second_half * cos_wide + first_half * sin_wide,
        ],
        axis=-1,
    )


def document_ids(lengths, positions):
    doc_ends = jnp.cumsum(lengths)
    return jnp.sum((positions[:, None] >= doc_ends[None, : DOCS - 1]).astype(jnp.int32), axis=1)


def rms_scale(row_values):
    return lax.rsqrt(jnp.mean(row_values * row_values, axis=-1, keepdims=True) + norm_eps)


def per_device(
    tokens, doc_lengths, w_query, w_key, w_value, w_out, w_gate, w_up, w_down, norm_gains, cotangent
):
    tp_count = lax.axis_size("tp")
    seq_count = lax.axis_size("seq")
    tp_index = lax.axis_index("tp")
    seq_index = lax.axis_index("seq")
    local_rows = tokens.shape[0]
    span_len = local_rows * tp_count
    seq_length = span_len * seq_count
    score_scale = 1.0 / math.sqrt(HEAD_DIM)
    key_step = math.gcd(512, seq_length)
    gathered = (
        lax.all_gather(w_query, ("fsdp", "seq"), axis=0, tiled=True),
        lax.all_gather(w_key, ("fsdp", "seq"), axis=0, tiled=True),
        lax.all_gather(w_value, ("fsdp", "seq"), axis=0, tiled=True),
        lax.all_gather(w_out, ("fsdp", "seq"), axis=1, tiled=True),
        lax.all_gather(w_gate, ("fsdp", "seq"), axis=0, tiled=True),
        lax.all_gather(w_up, ("fsdp", "seq"), axis=0, tiled=True),
        lax.all_gather(w_down, ("fsdp", "seq"), axis=1, tiled=True),
        lax.all_gather(norm_gains, ("fsdp", "seq"), axis=1, tiled=True),
    )
    query_full, key_full, value_full, out_full, gate_full, up_full, down_full, gains_low = gathered
    gain_one = gains_low[0].astype(jnp.float32)
    gain_two = gains_low[1].astype(jnp.float32)
    query_heads = query_full.shape[1] // HEAD_DIM
    kv_local = key_full.shape[1] // HEAD_DIM
    span_in = lax.all_gather(tokens, "tp", axis=0, tiled=True)
    span_float = span_in.astype(jnp.float32)
    inv_one = rms_scale(span_float)
    normed_one = (span_float * inv_one * gain_one).astype(jnp.bfloat16)
    span_start = seq_index * span_len
    positions = span_start + jnp.arange(span_len, dtype=jnp.int32)
    cos_tab, sin_tab = rope_tables(positions)
    query_raw = jnp.dot(normed_one, query_full, preferred_element_type=jnp.float32).reshape(
        span_len, query_heads, HEAD_DIM
    )
    key_raw = jnp.dot(normed_one, key_full, preferred_element_type=jnp.float32).reshape(
        span_len, kv_local, HEAD_DIM
    )
    value_raw = jnp.dot(normed_one, value_full, preferred_element_type=jnp.float32).reshape(
        span_len, kv_local, HEAD_DIM
    )
    query_rot = rotate(query_raw, cos_tab, sin_tab).astype(jnp.bfloat16)
    key_rot = rotate(key_raw, cos_tab, sin_tab).astype(jnp.bfloat16)
    value_low = value_raw.astype(jnp.bfloat16)
    query_group = query_rot.reshape(span_len, kv_local, GROUP, HEAD_DIM)
    key_all, value_all = (
        lax.all_gather(key_rot, "seq", axis=0, tiled=True),
        lax.all_gather(value_low, "seq", axis=0, tiled=True),
    )
    key_positions = jnp.arange(seq_length, dtype=jnp.int32)
    doc_keys = document_ids(doc_lengths[0], key_positions)
    doc_query = lax.dynamic_slice_in_dim(doc_keys, span_start, span_len, 0)
    key_blocks = key_positions // BLOCK
    query_block = positions // BLOCK
    blocks_used = (span_start + span_len + key_step - 1) // key_step
    stat_shape = (kv_local, GROUP, span_len)
    head_shape = (span_len, kv_local, GROUP, HEAD_DIM)

    def masked_scores(block_index):
        key_start = block_index * key_step
        key_part = lax.dynamic_slice_in_dim(key_all, key_start, key_step, 0)
        scores = (
            jnp.einsum("ckgd,nkd->kgcn", query_group, key_part, preferred_element_type=jnp.float32)
            * score_scale
        )
        block_part = lax.dynamic_slice_in_dim(key_blocks, key_start, key_step, 0)
        doc_part = lax.dynamic_slice_in_dim(doc_keys, key_start, key_step, 0)
        allowed = (block_part[None, :] <= query_block[:, None]) & (
            doc_part[None, :] == doc_query[:, None]
        )
        return (jnp.where(allowed[None, None], scores, mask_fill), key_start, key_part)

    def total_step(block_index, carry):
        row_max, row_sum = carry
        scores = masked_scores(block_index)[0]
        new_max = jnp.maximum(row_max, jnp.max(scores, axis=-1))
        row_sum = row_sum * jnp.exp(row_max - new_max) + jnp.sum(
            jnp.exp(scores - new_max[..., None]), axis=-1
        )
        return (new_max, row_sum)

    row_max, row_sum = lax.fori_loop(
        0,
        blocks_used,
        total_step,
        (jnp.full(stat_shape, mask_fill, jnp.float32), jnp.zeros(stat_shape, jnp.float32)),
    )
    log_total = row_max + jnp.log(row_sum)

    def out_step(block_index, running):
        scores, key_start, key_part = masked_scores(block_index)
        attn_prob = jnp.exp(scores - log_total[..., None]).astype(jnp.bfloat16)
        value_part = lax.dynamic_slice_in_dim(value_all, key_start, key_step, 0)
        return running + jnp.einsum(
            "kgcn,nkd->ckgd", attn_prob, value_part, preferred_element_type=jnp.float32
        )

    attended = lax.fori_loop(0, blocks_used, out_step, jnp.zeros(head_shape, jnp.float32))
    attended_low = attended.reshape(span_len, query_heads * HEAD_DIM).astype(jnp.bfloat16)
    attn_branch = lax.psum_scatter(
        jnp.dot(attended_low, out_full, preferred_element_type=jnp.float32).astype(jnp.bfloat16),
        "tp",
        scatter_dimension=0,
        tiled=True,
    ).astype(jnp.float32)
    token_rows = tokens.astype(jnp.float32)
    residual = token_rows + attn_branch
    inv_two = rms_scale(residual)
    normed_two = (residual * inv_two * gain_two).astype(jnp.bfloat16)
    span_two = lax.all_gather(normed_two, "tp", axis=0, tiled=True)
    gate_pre = jnp.dot(span_two, gate_full, preferred_element_type=jnp.float32)
    up_pre = jnp.dot(span_two, up_full, preferred_element_type=jnp.float32)
    sig_gate = jax.nn.sigmoid(gate_pre)
    silu_gate = gate_pre * sig_gate
    hidden_low = (silu_gate * up_pre).astype(jnp.bfloat16)
    mlp_branch = lax.psum_scatter(
        jnp.dot(hidden_low, down_full, preferred_element_type=jnp.float32).astype(jnp.bfloat16),
        "tp",
        scatter_dimension=0,
        tiled=True,
    ).astype(jnp.float32)
    mixed_out = (residual + mlp_branch).astype(jnp.bfloat16)
    cot_span = lax.all_gather(cotangent, "tp", axis=0, tiled=True)
    grad_down_w = jnp.einsum("cf,cd->fd", hidden_low, cot_span, preferred_element_type=jnp.float32)
    grad_hidden = jnp.einsum("cd,fd->cf", cot_span, down_full, preferred_element_type=jnp.float32)
    grad_gate_pre = (
        grad_hidden * up_pre * (sig_gate * (1.0 + gate_pre * (1.0 - sig_gate)))
    ).astype(jnp.bfloat16)
    grad_up_pre = (grad_hidden * silu_gate).astype(jnp.bfloat16)
    grad_gate_w = jnp.einsum(
        "cd,cf->df", span_two, grad_gate_pre, preferred_element_type=jnp.float32
    )
    grad_up_w = jnp.einsum("cd,cf->df", span_two, grad_up_pre, preferred_element_type=jnp.float32)
    grad_normed_two = lax.psum_scatter(
        (
            jnp.einsum("cf,df->cd", grad_gate_pre, gate_full, preferred_element_type=jnp.float32)
            + jnp.einsum("cf,df->cd", grad_up_pre, up_full, preferred_element_type=jnp.float32)
        ).astype(jnp.bfloat16),
        "tp",
        scatter_dimension=0,
        tiled=True,
    ).astype(jnp.float32)
    gain_two_term = jnp.sum(grad_normed_two * residual * inv_two, axis=0)
    scaled_two = grad_normed_two * gain_two
    grad_residual = (
        cotangent.astype(jnp.float32)
        + inv_two * scaled_two
        - residual
        * (inv_two * inv_two * inv_two)
        * jnp.mean(scaled_two * residual, axis=-1, keepdims=True)
    )
    grad_span = lax.all_gather(grad_residual.astype(jnp.bfloat16), "tp", axis=0, tiled=True)
    grad_out_w = jnp.einsum(
        "ce,cd->ed", attended_low, grad_span, preferred_element_type=jnp.float32
    )
    grad_attended = (
        jnp.einsum("cd,ed->ce", grad_span, out_full, preferred_element_type=jnp.float32)
        .astype(jnp.bfloat16)
        .reshape(head_shape)
    )

    def prob_grads(block_index):
        scores, key_start, key_part = masked_scores(block_index)
        probs_full = jnp.exp(scores - log_total[..., None])
        value_part = lax.dynamic_slice_in_dim(value_all, key_start, key_step, 0)
        grad_prob = jnp.einsum(
            "ckgd,nkd->kgcn", grad_attended, value_part, preferred_element_type=jnp.float32
        )
        return (probs_full, grad_prob, key_start, key_part)

    def delta_step(block_index, running):
        grads_here = prob_grads(block_index)
        return running + jnp.sum(grads_here[0] * grads_here[1], axis=-1)

    row_delta = lax.fori_loop(0, blocks_used, delta_step, jnp.zeros(stat_shape, jnp.float32))

    def grad_step(block_index, carry):
        query_acc, key_acc, value_acc = carry
        probs_full, grad_prob, key_start, key_part = prob_grads(block_index)
        grad_scores = (probs_full * (grad_prob - row_delta[..., None])).astype(jnp.bfloat16)
        query_acc = query_acc + jnp.einsum(
            "kgcn,nkd->ckgd", grad_scores, key_part, preferred_element_type=jnp.float32
        )
        key_term = (
            jnp.einsum(
                "kgcn,ckgd->nkd", grad_scores, query_group, preferred_element_type=jnp.float32
            )
            * score_scale
        )
        value_term = jnp.einsum(
            "kgcn,ckgd->nkd",
            probs_full.astype(jnp.bfloat16),
            grad_attended,
            preferred_element_type=jnp.float32,
        )
        key_old = lax.dynamic_slice_in_dim(key_acc, key_start, key_step, 0)
        value_old = lax.dynamic_slice_in_dim(value_acc, key_start, key_step, 0)
        key_acc = lax.dynamic_update_slice_in_dim(key_acc, key_old + key_term, key_start, 0)
        value_acc = lax.dynamic_update_slice_in_dim(value_acc, value_old + value_term, key_start, 0)
        return (query_acc, key_acc, value_acc)

    kv_zeros = jnp.zeros((seq_length, kv_local, HEAD_DIM), jnp.float32)
    query_acc, key_acc, value_acc = lax.fori_loop(
        0, blocks_used, grad_step, (jnp.zeros(head_shape, jnp.float32), kv_zeros, kv_zeros)
    )
    key_own, value_own = (
        lax.psum_scatter(
            key_acc.astype(jnp.bfloat16), "seq", scatter_dimension=0, tiled=True
        ).astype(jnp.float32),
        lax.psum_scatter(
            value_acc.astype(jnp.bfloat16), "seq", scatter_dimension=0, tiled=True
        ).astype(jnp.float32),
    )
    grad_query_rot = (query_acc * score_scale).reshape(span_len, query_heads, HEAD_DIM)
    grad_query_raw = (
        rotate(grad_query_rot, cos_tab, -sin_tab)
        .reshape(span_len, query_heads * HEAD_DIM)
        .astype(jnp.bfloat16)
    )
    grad_key_raw = (
        rotate(key_own, cos_tab, -sin_tab)
        .reshape(span_len, kv_local * HEAD_DIM)
        .astype(jnp.bfloat16)
    )
    grad_value_raw = value_own.reshape(span_len, kv_local * HEAD_DIM).astype(jnp.bfloat16)
    grad_query_w = jnp.einsum(
        "cd,ce->de", normed_one, grad_query_raw, preferred_element_type=jnp.float32
    )
    grad_key_w = jnp.einsum(
        "cd,ce->de", normed_one, grad_key_raw, preferred_element_type=jnp.float32
    )
    grad_value_w = jnp.einsum(
        "cd,ce->de", normed_one, grad_value_raw, preferred_element_type=jnp.float32
    )
    normed_part = jnp.einsum(
        "ce,de->cd", grad_query_raw, query_full, preferred_element_type=jnp.float32
    )
    normed_part = normed_part + jnp.einsum(
        "ce,de->cd", grad_key_raw, key_full, preferred_element_type=jnp.float32
    )
    normed_part = normed_part + jnp.einsum(
        "ce,de->cd", grad_value_raw, value_full, preferred_element_type=jnp.float32
    )
    gain_one_term = jnp.sum(normed_part * span_float * inv_one, axis=0)
    gain_block = jnp.broadcast_to(jnp.stack([gain_one_term, gain_two_term])[None], (tp_count, 2, D))
    grad_normed_one, gains_summed = (
        lax.psum_scatter(
            normed_part.astype(jnp.bfloat16), "tp", scatter_dimension=0, tiled=True
        ).astype(jnp.float32),
        lax.psum_scatter(
            gain_block.astype(jnp.bfloat16), "tp", scatter_dimension=0, tiled=True
        ).astype(jnp.float32),
    )
    gains_total = gains_summed[0]
    inv_rows = lax.dynamic_slice_in_dim(inv_one, tp_index * local_rows, local_rows, 0)
    scaled_one = grad_normed_one * gain_one
    grad_tokens = (
        grad_residual
        + inv_rows * scaled_one
        - token_rows
        * (inv_rows * inv_rows * inv_rows)
        * jnp.mean(scaled_one * token_rows, axis=-1, keepdims=True)
    )
    summed = (
        lax.psum_scatter(
            grad_query_w.astype(jnp.bfloat16), ("fsdp", "seq"), scatter_dimension=0, tiled=True
        ).astype(jnp.float32),
        lax.psum_scatter(
            grad_key_w.astype(jnp.bfloat16), ("fsdp", "seq"), scatter_dimension=0, tiled=True
        ).astype(jnp.float32),
        lax.psum_scatter(
            grad_value_w.astype(jnp.bfloat16), ("fsdp", "seq"), scatter_dimension=0, tiled=True
        ).astype(jnp.float32),
        lax.psum_scatter(
            grad_out_w.astype(jnp.bfloat16), ("fsdp", "seq"), scatter_dimension=1, tiled=True
        ).astype(jnp.float32),
        lax.psum_scatter(
            grad_gate_w.astype(jnp.bfloat16), ("fsdp", "seq"), scatter_dimension=0, tiled=True
        ).astype(jnp.float32),
        lax.psum_scatter(
            grad_up_w.astype(jnp.bfloat16), ("fsdp", "seq"), scatter_dimension=0, tiled=True
        ).astype(jnp.float32),
        lax.psum_scatter(
            grad_down_w.astype(jnp.bfloat16), ("fsdp", "seq"), scatter_dimension=1, tiled=True
        ).astype(jnp.float32),
        lax.psum_scatter(
            gains_total.astype(jnp.bfloat16), ("fsdp", "seq"), scatter_dimension=1, tiled=True
        ).astype(jnp.float32),
    )
    return (
        mixed_out,
        grad_tokens,
        summed[0],
        summed[1],
        summed[2],
        summed[3],
        summed[4],
        summed[5],
        summed[6],
        summed[7],
    )


VMEM_BYTES = 48 * 1024 * 1024
SMALL_COST = pl.CostEstimate(flops=1024, bytes_accessed=4096, transcendentals=0)


def to_core(value):
    return lax.ppermute(value, "fsdp", [(i, i ^ 1) for i in range(4)])


def to_x(value):
    return lax.ppermute(value, "fsdp", [(i, i ^ 2) for i in range(4)])


def to_z(value, step):
    return lax.ppermute(value, "seq", [(i, i ^ step) for i in range(4)])


def to_tp(value):
    return lax.ppermute(value, "tp", [(0, 1), (1, 0)])


def hold(value, *events):
    return lax.optimization_barrier((value, events))[0]


def float_of(value):
    return value.astype(jnp.float32)


def low_of(value):
    return value.astype(jnp.bfloat16)


def rows_dot(left, right):
    return lax.dot_general(left, right, (((0,), (0,)), ((), ())), preferred_element_type=jnp.float32)


def cols_dot(left, right):
    return lax.dot_general(left, right, (((1,), (1,)), ((), ())), preferred_element_type=jnp.float32)


def place_kernel(rows, place, pair, pair_far, plane, mine, held, read_sems, sems):
    reads = [
        pltpu.make_async_copy(
            (pair, pair_far)[k // 2].at[pl.ds((k % 2) * rows, rows), :], held.at[k], read_sems.at[k]
        )
        for k in range(4)
    ]
    for copy in reads:
        copy.start()
    writes = []
    for k, read in enumerate(reads):
        read.wait()
        start = pl.multiple_of((place[0] ^ k) * rows, 16)
        for i, target in enumerate((plane, mine)):
            write = pltpu.make_async_copy(
                held.at[k], target.at[pl.ds(start, rows), :], sems.at[2 * k + i]
            )
            write.start()
            writes.append(write)
    for write in writes:
        write.wait()


def place_rows(pair, pair_far, place):
    rows, columns = pair.shape[0] // 2, pair.shape[1]
    anywhere = pl.BlockSpec(memory_space=pl.ANY)
    return pl.pallas_call(
        lambda *refs: place_kernel(rows, *refs),
        out_shape=(
            jax.ShapeDtypeStruct((4 * rows, columns), jnp.bfloat16),
            jax.ShapeDtypeStruct((8 * rows, columns), jnp.bfloat16),
        ),
        in_specs=[pl.BlockSpec(memory_space=pltpu.SMEM)] + [anywhere] * 2,
        out_specs=(anywhere, anywhere),
        scratch_shapes=[
            pltpu.VMEM((4, rows, columns), jnp.bfloat16),
            pltpu.SemaphoreType.DMA((4,)),
            pltpu.SemaphoreType.DMA((8,)),
        ],
        cost_estimate=SMALL_COST,
        name="place_rows",
    )(place.reshape(1), pair, pair_far)


def fill_kernel(rows, part, start, across, first, mine, held, read_sems, sems):
    columns = pl.ds(start, mine.shape[1])
    reads = [
        pltpu.make_async_copy(
            across.at[pl.ds(k * part, part), columns], held.at[k], read_sems.at[k]
        )
        for k in range(rows // part)
    ]
    for copy in reads:
        copy.start()
    writes = []
    for k, read in enumerate(reads):
        read.wait()
        write = pltpu.make_async_copy(
            held.at[k], mine.at[pl.ds(rows + k * part, part), :], sems.at[k]
        )
        write.start()
        writes.append(write)
    for write in writes:
        write.wait()


def fill_rows(mine, across, start=0):
    rows, columns = across.shape[0], mine.shape[1]
    part = 128 if rows % 128 == 0 else 32
    anywhere = pl.BlockSpec(memory_space=pl.ANY)
    return pl.pallas_call(
        lambda *refs: fill_kernel(rows, part, start, *refs),
        out_shape=jax.ShapeDtypeStruct(mine.shape, mine.dtype),
        in_specs=[anywhere] * 2,
        out_specs=anywhere,
        scratch_shapes=[
            pltpu.VMEM((rows // part, part, columns), jnp.bfloat16),
            pltpu.SemaphoreType.DMA((rows // part,)),
            pltpu.SemaphoreType.DMA((rows // part,)),
        ],
        input_output_aliases={1: 0},
        cost_estimate=SMALL_COST,
        name="fill_rows",
    )(across, mine)


def take_rows_kernel(one, two, one_near, one_far, two_tp, two_far, out, sems):
    n, half = one.shape
    left, right = pl.ds(0, half), pl.ds(half, half)
    moves = [
        (one, pl.ds(0, n), left),
        (two, pl.ds(0, n), right),
        (one_near, pl.ds(2 * n, n), left),
        (one_far.at[pl.ds(0, n), :], pl.ds(n, n), left),
        (one_far.at[pl.ds(n, n), :], pl.ds(3 * n, n), left),
        (two_tp, pl.ds(n, n), right),
        (two_far, pl.ds(2 * n, 2 * n), right),
    ]
    copies = [
        pltpu.make_async_copy(source, out.at[rows, columns], sems.at[k])
        for k, (source, rows, columns) in enumerate(moves)
    ]
    for copy in copies:
        copy.start()
    for copy in copies:
        copy.wait()


def take_rows(*pieces):
    rows, half = pieces[0].shape
    return pl.pallas_call(
        take_rows_kernel,
        out_shape=jax.ShapeDtypeStruct((4 * rows, 2 * half), pieces[0].dtype),
        in_specs=[pl.BlockSpec(memory_space=pl.ANY)] * 6,
        out_specs=pl.BlockSpec(memory_space=pltpu.VMEM),
        scratch_shapes=[pltpu.SemaphoreType.DMA((7,))],
        compiler_params=pltpu.CompilerParams(vmem_limit_bytes=VMEM_BYTES),
        cost_estimate=SMALL_COST,
        name="take_rows",
    )(*pieces)


def dense_call(kernel, name, outs, scratch, args):
    whole = pl.BlockSpec(memory_space=pltpu.VMEM)
    return pl.pallas_call(
        kernel,
        out_shape=[jax.ShapeDtypeStruct(shape, kind) for shape, kind in outs],
        in_specs=[whole] * len(args),
        out_specs=[whole] * len(outs),
        scratch_shapes=scratch,
        compiler_params=pltpu.CompilerParams(vmem_limit_bytes=VMEM_BYTES),
        cost_estimate=SMALL_COST,
        name=name,
    )(*args)


def turned(value, cos_wide, sin_wide):
    half = HEAD_DIM // 2
    swapped = jnp.concatenate([value[:, half:], value[:, :half]], axis=1)
    return value * cos_wide + swapped * sin_wide


def rope_kernel(raw, cos_wide, sin_wide, query, kv):
    cos, sin = cos_wide[...], sin_wide[...]
    query_width, kv_width = query.shape[1], kv.shape[1] // 2
    for start in range(0, query_width, HEAD_DIM):
        columns = slice(start, start + HEAD_DIM)
        query[:, columns] = turned(raw[:, columns], cos, sin).astype(jnp.bfloat16)
    for start in range(0, kv_width, HEAD_DIM):
        columns = slice(query_width + start, query_width + start + HEAD_DIM)
        kv[:, start : start + HEAD_DIM] = turned(raw[:, columns], cos, sin).astype(jnp.bfloat16)
    values = raw[:, query_width + kv_width : query_width + 2 * kv_width]
    kv[:, kv_width:] = values.astype(jnp.bfloat16)


def pair_of(early, own, index):
    columns = slice(index * HEAD_DIM, (index + 1) * HEAD_DIM)
    return jnp.concatenate([early[:, columns], own[:, columns]], axis=0)


def attend_kernel(scale, query, early, own, query_ids, key_ids, attended, log_total, fill):
    kv_local = own.shape[1] // HEAD_DIM // 2
    rows_total = query.shape[0]
    half_rows = rows_total // 2
    for part in range(2):
        rows = slice(part * half_rows, (part + 1) * half_rows)
        allowed = (key_ids[:, 0:1] == query_ids[0:1, rows]) & (
            key_ids[:, 1:2] <= query_ids[1:2, rows]
        )
        fill[...] = jnp.where(allowed, 0.0, mask_fill)
        for kv in range(kv_local):
            keys = pair_of(early, own, kv)
            values = pair_of(early, own, kv_local + kv)
            for member in range(GROUP):
                head = kv * GROUP + member
                columns = slice(head * HEAD_DIM, (head + 1) * HEAD_DIM)
                scores = cols_dot(keys, query[rows, columns]) + fill[...]
                top = jnp.max(scores, axis=0, keepdims=True)
                weights = jnp.exp((scores - top) * scale)
                total = jnp.sum(weights, axis=0, keepdims=True)
                probs = (weights * (1.0 / total)).astype(jnp.bfloat16)
                attended[rows, columns] = rows_dot(values, probs).T.astype(jnp.bfloat16)
                log_total[head : head + 1, rows] = top * scale + jnp.log(total)


def attend_back_kernel(
    scale,
    query,
    early,
    own,
    query_ids,
    key_ids,
    log_total,
    grad_attended,
    cos_wide,
    sin_wide,
    grad_query,
    grad_early,
    grad_own,
    fill,
    all_probs,
    all_grads,
):
    kv_local = own.shape[1] // HEAD_DIM // 2
    rows_total = query.shape[0]
    half_rows = rows_total // 2
    for part in range(2):
        rows = slice(part * half_rows, (part + 1) * half_rows)
        allowed = (key_ids[:, 0:1] == query_ids[0:1, rows]) & (
            key_ids[:, 1:2] <= query_ids[1:2, rows]
        )
        fill[:, rows] = jnp.where(allowed, 0.0, mask_fill)
    for kv in range(kv_local):
        keys = pair_of(early, own, kv)
        values = pair_of(early, own, kv_local + kv)
        queries, outs = [], []
        for part in range(2):
            rows = slice(part * half_rows, (part + 1) * half_rows)
            cos, sin = cos_wide[rows, :], -sin_wide[rows, :]
            for member in range(GROUP):
                head = kv * GROUP + member
                columns = slice(head * HEAD_DIM, (head + 1) * HEAD_DIM)
                place = (part * GROUP + member) * half_rows
                where = slice(place, place + half_rows)
                one_query, one_out = query[rows, columns], grad_attended[rows, columns]
                queries.append(one_query)
                outs.append(one_out)
                scores = cols_dot(keys, one_query) + fill[:, rows]
                probs = jnp.exp(scores * scale - log_total[head : head + 1, rows])
                grad_probs = cols_dot(values, one_out)
                delta = jnp.sum(probs * grad_probs, axis=0, keepdims=True)
                grads = (probs * (grad_probs - delta)).astype(jnp.bfloat16)
                all_probs[:, where] = probs.astype(jnp.bfloat16)
                all_grads[:, where] = grads
                turned_grad = rows_dot(keys, grads).T * scale
                grad_query[rows, columns] = turned(turned_grad, cos, sin).astype(jnp.bfloat16)
        grad_keys = (
            jnp.dot(
                all_grads[...], jnp.concatenate(queries, axis=0), preferred_element_type=jnp.float32
            )
            * scale
        )
        grad_values = jnp.dot(
            all_probs[...], jnp.concatenate(outs, axis=0), preferred_element_type=jnp.float32
        )
        for start, grad in ((kv, grad_keys), (kv_local + kv, grad_values)):
            columns = slice(start * HEAD_DIM, (start + 1) * HEAD_DIM)
            grad_early[:, columns] = grad[:rows_total].astype(jnp.bfloat16)
            grad_own[:, columns] = grad[rows_total:]


def join_kernel(grad_query, grad_own, late, cos_wide, sin_wide, grad_raw):
    cos, sin = cos_wide[...], -sin_wide[...]
    query_width, kv_width = grad_query.shape[1], grad_own.shape[1] // 2
    grad_raw[:, :query_width] = grad_query[...]
    for start in range(0, kv_width, HEAD_DIM):
        columns = slice(start, start + HEAD_DIM)
        grad = grad_own[:, columns] + late[:, columns].astype(jnp.float32)
        grad_raw[:, query_width + start : query_width + start + HEAD_DIM] = turned(
            grad, cos, sin
        ).astype(jnp.bfloat16)
    values = grad_own[:, kv_width:] + late[:, kv_width:].astype(jnp.float32)
    used = query_width + 2 * kv_width
    grad_raw[:, query_width + kv_width : used] = values.astype(jnp.bfloat16)
    spare = grad_raw.shape[1] - used
    grad_raw[:, used:] = jnp.zeros((grad_raw.shape[0], spare), jnp.bfloat16)


def tiled_call(kernel, name, steps, in_specs, outs, args):
    return pl.pallas_call(
        kernel,
        grid=(steps,),
        out_shape=[jax.ShapeDtypeStruct(shape, kind) for shape, kind, _, _ in outs],
        in_specs=[pl.BlockSpec(block, index) for block, index in in_specs],
        out_specs=[pl.BlockSpec(block, index) for _, _, block, index in outs],
        compiler_params=pltpu.CompilerParams(vmem_limit_bytes=VMEM_BYTES),
        cost_estimate=SMALL_COST,
        name=name,
    )(*args)


def fixed(step):
    return (0, 0)


def by_row(step):
    return (step, 0)


def by_column(step):
    return (0, step)


def split_dot(left, mine, other):
    depth = mine.shape[0]
    first = jnp.dot(left[:, :depth], mine[...], preferred_element_type=jnp.float32)
    return first + jnp.dot(left[:, depth:], other[...], preferred_element_type=jnp.float32)


def project_kernel(start, left, mine, other, out):
    columns = slice(start, start + out.shape[1])
    depth = mine.shape[0]
    first = jnp.dot(left[:, :depth], mine[:, columns], preferred_element_type=jnp.float32)
    second = jnp.dot(left[:, depth:], other[:, columns], preferred_element_type=jnp.float32)
    out[...] = (first + second).astype(out.dtype)


def project(left, weights, start, columns, kind):
    mine, other = weights
    rows, depth = left.shape[0], mine.shape[0]
    tiled = start == 0 and columns % 512 == 0
    tile = 512 if tiled else columns
    block = (depth, tile) if tiled else mine.shape
    (out,) = tiled_call(
        functools.partial(project_kernel, start),
        "project",
        columns // tile,
        [(left.shape, fixed), (block, by_column), (block, by_column)],
        [((rows, columns), kind, (rows, tile), by_column)],
        (left, mine, other),
    )
    return out


def hidden_kernel(normed, gate_m, gate_o, up_m, up_o, hidden, gate_slope, up_slope):
    gate_pre = split_dot(normed, gate_m, gate_o)
    up_pre = split_dot(normed, up_m, up_o)
    sig_gate = 1.0 / (1.0 + jnp.exp(-gate_pre))
    silu_gate = gate_pre * sig_gate
    hidden[...] = (silu_gate * up_pre).astype(jnp.bfloat16)
    gate_slope[...] = up_pre * (sig_gate * (1.0 + gate_pre * (1.0 - sig_gate)))
    up_slope[...] = silu_gate


def hidden_units(normed, gate_weights, up_weights):
    rows = normed.shape[0]
    depth, columns = gate_weights[0].shape
    tile = 256
    outs = [
        ((rows, columns), kind, (rows, tile), by_column)
        for kind in (jnp.bfloat16, jnp.float32, jnp.float32)
    ]
    return tiled_call(
        hidden_kernel,
        "hidden_units",
        columns // tile,
        [(normed.shape, fixed)] + [((depth, tile), by_column)] * 4,
        outs,
        (normed, *gate_weights, *up_weights),
    )


def hidden_grad_kernel(cot, down_m, down_o, gate_slope, up_slope, gate_grad, up_grad):
    grad_hidden = split_dot(cot, down_m, down_o)
    gate_grad[...] = (grad_hidden * gate_slope[...]).astype(jnp.bfloat16)
    up_grad[...] = (grad_hidden * up_slope[...]).astype(jnp.bfloat16)


def hidden_grads(cot, down_weights, gate_slope, up_slope):
    rows = cot.shape[0]
    depth, columns = down_weights[0].shape
    tile = 256
    out = ((rows, columns), jnp.bfloat16, (rows, tile), by_column)
    return tiled_call(
        hidden_grad_kernel,
        "hidden_grads",
        columns // tile,
        [(cot.shape, fixed)]
        + [((depth, tile), by_column)] * 2
        + [((rows, tile), by_column)] * 2,
        [out] * 2,
        (cot, *down_weights, gate_slope, up_slope),
    )


def back_kernel(count, start, *refs):
    lefts, weights, outs = refs[:count], refs[count : 3 * count], refs[3 * count :]
    columns = slice(start, start + lefts[0].shape[1])
    sums = []
    for half in range(2):
        terms = [
            cols_dot(left[...], weights[2 * i + half][:, columns]) for i, left in enumerate(lefts)
        ]
        sums.append(sum(terms).astype(jnp.bfloat16))
    one, two = sums
    one_keep, one_send, two_keep, two_send = outs
    n = one.shape[0] // 4
    one_keep[:n, :], one_send[:n, :] = one[:n], one[n : 2 * n]
    one_keep[n:, :], one_send[n:, :] = one[2 * n : 3 * n], one[3 * n :]
    two_keep[...], two_send[...] = two[: 2 * n], two[2 * n :]


def project_back(lefts, weights, start=0):
    rows, width = lefts[0].shape
    depth = weights[0][0].shape[0]
    tile = 256
    flat = [half for pair in weights for half in pair]
    return tiled_call(
        functools.partial(back_kernel, len(lefts), start),
        "project_back",
        depth // tile,
        [((rows, width), fixed)] * len(lefts) + [((tile, flat[0].shape[1]), by_row)] * len(flat),
        [((rows // 2, depth), jnp.bfloat16, (rows // 2, tile), by_column)] * 4,
        (*lefts, *flat),
    )


def outer_kernel(left, left_other, right, *refs):
    others, out = refs[:-1], refs[-1]
    total = rows_dot(left[...], right[...])
    rows = left.shape[0] // len(others)
    for i, other in enumerate(others):
        total = total + rows_dot(left_other[i * rows : (i + 1) * rows, :], other[...])
    out[...] = total.astype(jnp.bfloat16)


def outer(left, left_others, right, right_others, index):
    rows, width = left.shape[0], right.shape[1]
    left_other = left_others[index]
    depth = left_other.shape[1]
    tile = 256 if width % 256 == 0 else width
    (out,) = tiled_call(
        outer_kernel,
        "outer",
        width // tile,
        [((rows, depth), lambda step: (0, index)), ((rows, depth), fixed)]
        + [((rows, tile), by_column)]
        + [((other.shape[0], tile), by_column) for other in right_others],
        [((depth, width), jnp.bfloat16, (depth, tile), by_column)],
        (left, left_other, right, *right_others),
    )
    return out


def norm_kernel(rows, gain, out):
    value = rows[...].astype(jnp.float32)
    scale = lax.rsqrt(jnp.mean(value * value, axis=1, keepdims=True) + norm_eps)
    out[...] = (value * scale * gain[...]).astype(jnp.bfloat16)


def norm_rows(rows, gain):
    count, width = rows.shape
    tile = count // 4
    (out,) = tiled_call(
        norm_kernel,
        "norm_rows",
        4,
        [((tile, width), by_row), ((1, width), fixed)],
        [((count, width), jnp.bfloat16, (tile, width), by_row)],
        (rows, gain.reshape(1, width)),
    )
    return out


def take_wide_kernel(own, from_near, from_tp, out, sems):
    n = own.shape[0]
    moves = [
        (own, pl.ds(0, n)),
        (from_tp.at[pl.ds(0, n), :], pl.ds(n, n)),
        (from_near, pl.ds(2 * n, n)),
        (from_tp.at[pl.ds(n, n), :], pl.ds(3 * n, n)),
    ]
    copies = [
        pltpu.make_async_copy(source, out.at[rows, :], sems.at[k])
        for k, (source, rows) in enumerate(moves)
    ]
    for copy in copies:
        copy.start()
    for copy in copies:
        copy.wait()


def take_wide(own, from_near, from_tp):
    return pl.pallas_call(
        take_wide_kernel,
        out_shape=jax.ShapeDtypeStruct((4 * own.shape[0], own.shape[1]), own.dtype),
        in_specs=[pl.BlockSpec(memory_space=pl.ANY)] * 3,
        out_specs=pl.BlockSpec(memory_space=pltpu.VMEM),
        scratch_shapes=[pltpu.SemaphoreType.DMA((4,))],
        compiler_params=pltpu.CompilerParams(vmem_limit_bytes=VMEM_BYTES),
        cost_estimate=SMALL_COST,
        name="take_wide",
    )(own, from_near, from_tp)


def rows_call(fn, name, where, steps, ins, outs):
    def kernel(where_ref, *refs):
        values = [ref[...].astype(jnp.float32) for ref in refs[: len(ins)]]
        for ref, value in zip(refs[len(ins) :], fn(*values)):
            ref[...] = value.astype(ref.dtype)

    def spec(rows, columns, place):
        return pl.BlockSpec((rows, columns), lambda step, ref: (place(step, ref), 0))

    return pl.pallas_call(
        kernel,
        grid_spec=pltpu.PrefetchScalarGridSpec(
            num_scalar_prefetch=1,
            grid=(steps,),
            in_specs=[spec(rows, array.shape[1], place) for array, rows, place in ins],
            out_specs=[spec(rows, shape[1], place) for shape, _, rows, place in outs],
        ),
        out_shape=[jax.ShapeDtypeStruct(shape, kind) for shape, kind, _, _ in outs],
        compiler_params=pltpu.CompilerParams(vmem_limit_bytes=VMEM_BYTES),
        cost_estimate=SMALL_COST,
        name=name,
    )(where, *[array for array, _, _ in ins])


def far_halves(where, *terms):
    rows = terms[0][0].shape[0] // 4
    columns = sum(own.shape[1] for own, _ in terms)
    keep, give = (lambda step, ref: 2 * ref[0] + step), (lambda step, ref: 2 - 2 * ref[0] + step)
    out = ((2 * rows, columns), jnp.bfloat16, rows, lambda step, ref: step)
    count = len(terms)

    def sums(*values):
        pairs = [values[2 * i] + values[2 * i + 1] for i in range(2 * count)]
        if count == 1:
            return pairs
        return jnp.concatenate(pairs[:count], axis=1), jnp.concatenate(pairs[count:], axis=1)

    return rows_call(
        sums,
        "far_halves",
        where,
        2,
        [(array, rows, place) for place in (keep, give) for pair in terms for array in pair],
        [out, out],
    )


def near_halves(where, pair, from_far):
    rows, columns = pair.shape[0] // 2, pair.shape[1]
    keep, give = (lambda step, ref: ref[1]), (lambda step, ref: 1 - ref[1])
    out = ((rows, columns), jnp.bfloat16, rows, lambda step, ref: 0)
    return rows_call(
        lambda a, b, c, d: (a + b, c + d),
        "near_halves",
        where,
        1,
        [(array, rows, place) for place in (keep, give) for array in (pair, from_far)],
        [out, out],
    )


def join_halves_kernel(turn, where, own, received, *outs):
    first = where[1] == 0
    low_part = jnp.where(first, own[...], received[...]).astype(jnp.float32)
    high_part = jnp.where(first, received[...], own[...]).astype(jnp.float32)
    start = 0
    for out in outs:
        width = out.shape[0] if turn else out.shape[1]
        if len(outs) == 1:
            size = own.shape[1]
            rest = width - size
        else:
            size = rest = width // 2
        left, right = low_part[:, start : start + size], high_part[:, start : start + rest]
        if turn:
            out[:size, :] = left.T
            out[size:, :] = right.T
        else:
            out[:, :size] = left
            out[:, size:] = right
        start += size


def join_halves(where, own, received, widths, turn=False):
    rows = own.shape[0]
    shapes = [(width, rows) if turn else (rows, width) for width in widths]
    whole = pl.BlockSpec(memory_space=pltpu.VMEM)
    return pl.pallas_call(
        functools.partial(join_halves_kernel, turn),
        out_shape=[jax.ShapeDtypeStruct(shape, jnp.float32) for shape in shapes],
        in_specs=[pl.BlockSpec(memory_space=pltpu.SMEM), whole, whole],
        out_specs=[whole] * len(shapes),
        compiler_params=pltpu.CompilerParams(vmem_limit_bytes=VMEM_BYTES),
        cost_estimate=SMALL_COST,
        name="join_halves",
    )(where, own, received)


def split_halves_kernel(plan, where, *refs):
    arrays, pairs, other = refs[: len(plan)], refs[len(plan) : -1], refs[-1]
    rows = other.shape[0]
    first = where[1] == 0
    offset = 0
    filled = [0] * len(pairs)
    for index, (array, (target, size, turn)) in enumerate(zip(arrays, plan)):
        value = array[...]
        if turn:
            value = value.astype(jnp.float32).T.astype(jnp.bfloat16)
        low_part, high_part = value[:, :size], value[:, size:]
        missing = size - high_part.shape[1]
        if missing:
            high_part = jnp.concatenate(
                [high_part, jnp.zeros((rows, missing), jnp.bfloat16)], axis=1
            )
        start = filled[target]
        pair = pairs[target]
        pair[:rows, start : start + size] = jnp.where(first, low_part, high_part)
        other[:, offset + start : offset + start + size] = jnp.where(first, high_part, low_part)
        filled[target] = start + size
        if index + 1 == len(plan) or plan[index + 1][0] != target:
            spare = pair.shape[1] - filled[target]
            if spare:
                pair[:rows, filled[target] :] = jnp.zeros((rows, spare), jnp.bfloat16)
                end = offset + pair.shape[1]
                other[:, end - spare : end] = jnp.zeros((rows, spare), jnp.bfloat16)
            offset += pair.shape[1]


def split_halves(where, arrays, plan, widths):
    rows = D // 16
    whole = pl.BlockSpec(memory_space=pltpu.VMEM)
    return pl.pallas_call(
        functools.partial(split_halves_kernel, plan),
        out_shape=[jax.ShapeDtypeStruct((2 * rows, width), jnp.bfloat16) for width in widths]
        + [jax.ShapeDtypeStruct((rows, sum(widths)), jnp.bfloat16)],
        in_specs=[pl.BlockSpec(memory_space=pltpu.SMEM)] + [whole] * len(arrays),
        out_specs=[whole] * (len(widths) + 1),
        compiler_params=pltpu.CompilerParams(vmem_limit_bytes=VMEM_BYTES),
        cost_estimate=SMALL_COST,
        name="split_halves",
    )(where, *arrays)


def pair_kernel(first, second, out):
    n = first.shape[0]
    out[:n, :] = first[...]
    out[n:, :] = second[...]


def pair_rows(first, second):
    rows, columns = first.shape
    (out,) = dense_call(
        pair_kernel, "pair_rows", [((2 * rows, columns), first.dtype)], [], (first, second)
    )
    return out


def middle_kernel(one, got_one, two, got_two, next_one, next_two, sum_one, sum_two):
    n = sum_one.shape[0]
    for keep, got, later, total in (
        (one, got_one, next_one, sum_one),
        (two, got_two, next_two, sum_two),
    ):
        both = keep[...].astype(jnp.float32) + got[...].astype(jnp.float32)
        total[...] = both[:n]
        later[...] = both[n:].astype(jnp.bfloat16)


def scatter_middle(one, got_one, two, got_two):
    rows, columns = one.shape[0] // 2, one.shape[1]
    return dense_call(
        middle_kernel,
        "scatter_middle",
        [((rows, columns), jnp.bfloat16)] * 2 + [((rows, columns), jnp.float32)] * 2,
        [],
        (one, got_one, two, got_two),
    )


def summed(sum_one, sum_two, last_one, last_two):
    one = sum_one[...] + last_one[...].astype(jnp.float32)
    two = sum_two[...] + last_two[...].astype(jnp.float32)
    return jnp.concatenate([one, two], axis=1)


def store_halves(value, one, two):
    half = one.shape[1]
    one[...] = value[:, :half].astype(one.dtype)
    two[...] = value[:, half:].astype(two.dtype)


def residual_kernel(sum_one, sum_two, last_one, last_two, rows, gain, residual, one, two):
    value = rows[...].astype(jnp.float32) + summed(sum_one, sum_two, last_one, last_two)
    residual[...] = value
    scale = lax.rsqrt(jnp.mean(value * value, axis=1, keepdims=True) + norm_eps)
    store_halves(value * scale * gain[...], one, two)


def norm_grad(grad, value, gain):
    scale = lax.rsqrt(jnp.mean(value * value, axis=1, keepdims=True) + norm_eps)
    scaled = grad * gain
    inner = jnp.mean(scaled * value, axis=1, keepdims=True)
    gain_term = jnp.sum(grad * value * scale, axis=0, keepdims=True)
    return scale * scaled - value * (scale * scale * scale) * inner, gain_term


def residual_grad_kernel(
    sum_one, sum_two, last_one, last_two, residual, gain, cot, grad, gain_term, one, two
):
    back, term = norm_grad(summed(sum_one, sum_two, last_one, last_two), residual[...], gain[...])
    value = cot[...].astype(jnp.float32) + back
    grad[...] = value
    gain_term[...] = term
    store_halves(value, one, two)


def token_grad_kernel(
    sum_one, sum_two, last_one, last_two, rows, gain, grad_residual, grad
):
    value = rows[...].astype(jnp.float32)
    back, _ = norm_grad(summed(sum_one, sum_two, last_one, last_two), value, gain[...])
    grad[...] = grad_residual[...] + back


def gain_kernel(one_keep, one_send, two_keep, two_send, rows, out):
    n, half = one_keep.shape[0] // 2, one_keep.shape[1]
    low_half, high_half = slice(0, n), slice(n, 2 * n)
    ones = (one_keep, low_half), (one_send, low_half), (one_keep, high_half), (one_send, high_half)
    twos = (two_keep, low_half), (two_keep, high_half), (two_send, low_half), (two_send, high_half)
    left = right = 0.0
    for k in range(4):
        value = rows[k * n : (k + 1) * n, :].astype(jnp.float32)
        scale = lax.rsqrt(jnp.mean(value * value, axis=1, keepdims=True) + norm_eps)
        value = value * scale
        one = ones[k][0][ones[k][1], :].astype(jnp.float32)
        two = twos[k][0][twos[k][1], :].astype(jnp.float32)
        left = left + jnp.sum(one * value[:, :half], axis=0, keepdims=True)
        right = right + jnp.sum(two * value[:, half:], axis=0, keepdims=True)
    out[:, :half] = left
    out[:, half:] = right


def mixed_kernel(sum_one, sum_two, last_one, last_two, residual, mixed):
    total = residual[...] + summed(sum_one, sum_two, last_one, last_two)
    mixed[...] = total.astype(jnp.bfloat16)


def half_plan(
    tokens, doc_lengths, w_query, w_key, w_value, w_out, w_gate, w_up, w_down, norm_gains, cotangent
):
    fsdp_index = lax.axis_index("fsdp")
    seq_index = lax.axis_index("seq")
    tp_index = lax.axis_index("tp")
    near = seq_index % 2
    far = seq_index // 2
    local_rows = tokens.shape[0]
    group_rows = 4 * local_rows
    middle = D // 2
    quarter = D // 4
    block_rows = D // 16
    score_scale = 1.0 / math.sqrt(HEAD_DIM)

    def columns_in(value):
        return jnp.concatenate(
            [
                lax.dynamic_slice_in_dim(value, (fsdp_index ^ k) * quarter, quarter, 1)
                for k in (0, 2, 1, 3)
            ],
            axis=1,
        )

    def columns_out(value):
        pieces = []
        for block in range(4):
            k = fsdp_index ^ block
            place = (k // 2) + (k % 2) * 2
            pieces.append(lax.dynamic_slice_in_dim(value, place * quarter, quarter, 1))
        return jnp.concatenate(pieces, axis=1)

    def gather_first(one, two):
        return one, two, to_z(one, 1), to_tp(two)

    def gather_second(one, two, one_near, two_tp):
        one_far = to_tp(pair_rows(one, one_near))
        two_far = to_z(pair_rows(two, two_tp), 1)
        return one, two, one_near, one_far, two_tp, two_far

    def scatter_first(one_keep, one_send, two_keep, two_send):
        return one_keep, to_tp(one_send), two_keep, to_z(two_send, 1)

    def scatter_second(next_one, next_two, sum_one, sum_two):
        return sum_one, sum_two, to_z(next_one, 1), to_tp(next_two)

    where = jnp.stack([far, near]).astype(jnp.int32)
    query_width = w_query.shape[1] // 2
    key_width = w_key.shape[1] // 2
    query_heads = query_width // HEAD_DIM
    heads_width = -(-(query_width + 2 * key_width) // 128) * 128
    hidden_width = -(-(w_gate.shape[1] // 2) // 128) * 128
    row_shape = (local_rows, D)
    half_shape = (local_rows, middle)

    def cross_left(value, *events):
        first, second = value[:, middle : middle + quarter], value[:, middle + quarter :]
        return to_core(hold(first, events)), to_core(hold(second, events))

    def cross_right(value, count):
        rows = value.shape[0] // count
        return tuple(to_core(value[i * rows : (i + 1) * rows]) for i in range(count))

    tokens_in = columns_in(tokens)
    cot_in = columns_in(cotangent)
    first_width = heads_width + query_width
    plan = ((0, query_width, False), (0, key_width, False), (0, key_width, False))
    spare = heads_width - query_width - 2 * key_width
    first_pair, first_other = split_halves(
        where,
        (w_query, w_key, w_value, jnp.zeros((block_rows, 2 * spare), jnp.bfloat16), w_out),
        (*plan, (0, spare, False), (0, query_width, True)),
        (first_width,),
    )
    gain_stack = norm_gains[None]
    gain_stack = jnp.concatenate([gain_stack, to_z(gain_stack, 1)], axis=0)
    first_near = to_z(first_other, 1)
    token_wait = gather_first(tokens_in[:, :middle], tokens_in[:, middle:])
    gain_far = to_z(hold(gain_stack, token_wait[2:]), 2)
    gain_stack = jnp.concatenate([gain_stack, gain_far], axis=0)
    first_pair = fill_rows(*hold((first_pair, first_near), gain_stack))
    first_far = to_z(first_pair, 2)
    token_wait = gather_second(*hold(token_wait, first_pair))
    gate_pair, gate_other = split_halves(
        where, (w_gate,), ((0, hidden_width, False),), (hidden_width,)
    )
    up_pair, up_other = split_halves(where, (w_up,), ((0, hidden_width, False),), (hidden_width,))
    down_pair, down_other = split_halves(
        where, (w_down,), ((0, hidden_width, True),), (hidden_width,)
    )
    gate_near = to_z(hold(gate_other, first_pair), 1)
    token_wait = hold(token_wait, gate_other, up_other, down_other)
    gain_plane = jnp.concatenate(
        [
            lax.dynamic_index_in_dim(gain_stack, seq_index ^ k, 0, keepdims=False)
            for k in range(4)
        ],
        axis=1,
    )
    gain_mine = jnp.concatenate([gain_plane, to_x(gain_plane)], axis=1)
    gains = float_of(jnp.concatenate([gain_mine, to_core(gain_mine)], axis=1))
    gain_one = gains[0:1]
    gain_two = gains[1:2]
    token_span = take_rows(*hold(token_wait, gains))

    row_ids = jnp.arange(local_rows, dtype=jnp.int32)
    own_positions = jnp.concatenate(
        [
            far * (2 * 2 * local_rows)
            + (near ^ i) * (2 * local_rows)
            + (tp_index ^ j) * local_rows
            + row_ids
            for i in range(2)
            for j in range(2)
        ]
    )
    cos_tab, sin_tab = rope_tables(own_positions)
    cos_wide = jnp.concatenate([cos_tab, cos_tab], axis=1)
    sin_wide = jnp.concatenate([-sin_tab, sin_tab], axis=1)
    key_positions = jnp.concatenate([own_positions - group_rows, own_positions])
    doc_ends = jnp.cumsum(doc_lengths[0])[: DOCS - 1]

    def doc_of(positions):
        return jnp.sum((positions[:, None] >= doc_ends[None, :]).astype(jnp.int32), axis=1)

    key_docs = jnp.where(key_positions >= 0, doc_of(key_positions), -1)
    query_ids = jnp.stack([doc_of(own_positions), own_positions // BLOCK])
    key_ids = jnp.stack([key_docs, key_positions // BLOCK], axis=1)

    gate_pair = fill_rows(*hold((gate_pair, gate_near), token_span))
    first_plane, first_mine = place_rows(*hold((first_pair, first_far), gate_pair), seq_index)
    first_x = to_x(first_plane)
    gate_far = to_z(hold(gate_pair, first_plane), 2)
    normed_one = norm_rows(hold(token_span, first_plane), gain_one)
    normed_other = cross_left(normed_one)
    up_pair = fill_rows(up_pair, to_z(hold(up_other, first_plane), 1))
    down_pair = fill_rows(down_pair, to_z(hold(down_other, first_plane), 1))
    cot_first = gather_first(*hold((cot_in[:, :middle], cot_in[:, middle:]), up_pair))
    gate_plane, gate_mine = place_rows(
        *hold((gate_pair, gate_far), cot_first[2:], down_pair, normed_one), seq_index
    )
    first_mine = fill_rows(*hold((first_mine, first_x), gate_plane))
    first_weights = first_mine, to_core(first_mine)
    gate_x = to_x(hold(gate_plane, first_mine))
    up_far = to_z(hold(up_pair, gate_plane), 2)
    cot_wait = gather_second(*hold(cot_first, first_mine))
    raw = project(normed_one, first_weights, 0, heads_width, jnp.float32)
    query_rot, own_kv = dense_call(
        rope_kernel,
        "rope",
        [
            ((group_rows, query_width), jnp.bfloat16),
            ((group_rows, 2 * key_width), jnp.bfloat16),
        ],
        [],
        (raw, cos_wide, sin_wide),
    )
    cot_span = take_rows(*hold(cot_wait, own_kv))
    up_plane, up_mine = place_rows(*hold((up_pair, up_far), cot_span), seq_index)
    early_kv = lax.ppermute(hold(own_kv, up_plane), "seq", [(0, 2), (1, 3)])
    gate_mine = fill_rows(*hold((gate_mine, gate_x), up_plane))
    gate_weights = gate_mine, to_core(gate_mine)
    up_x = to_x(hold(up_plane, gate_mine))
    attended_low, log_total = dense_call(
        functools.partial(attend_kernel, score_scale),
        "attend",
        [
            ((group_rows, query_width), jnp.bfloat16),
            ((query_heads, group_rows), jnp.float32),
        ],
        [pltpu.VMEM((2 * group_rows, group_rows // 2), jnp.float32)],
        (query_rot, early_kv, own_kv, query_ids, key_ids),
    )
    attended_other = cross_right(attended_low, 1)
    down_far = to_z(hold(down_pair, log_total), 2)
    branch = scatter_first(
        *project_back([hold(attended_low, normed_other)], [first_weights], heads_width)
    )
    branch = scatter_middle(*hold(branch, attended_other))
    branch = scatter_second(*branch)
    residual, two_one, two_two = dense_call(
        residual_kernel,
        "residual",
        [(row_shape, jnp.float32)] + [(half_shape, jnp.bfloat16)] * 2,
        [],
        (*branch, tokens_in, gain_two),
    )
    down_plane, down_mine = place_rows(*hold((down_pair, down_far), residual), seq_index)
    up_mine = fill_rows(*hold((up_mine, up_x), down_plane))
    up_weights = up_mine, to_core(up_mine)
    down_x = to_x(hold(down_plane, up_mine))
    two_wait = gather_second(*hold(gather_first(two_one, two_two), up_mine))
    span_two = take_rows(*two_wait)
    span_other = cross_left(span_two)
    cot_other = cross_left(cot_span, log_total)
    hidden_low, gate_slope, up_slope = hidden_units(
        hold(span_two, cot_other, span_other), gate_weights, up_weights
    )
    hidden_other = cross_right(hidden_low, 1)
    down_mine = fill_rows(*hold((down_mine, down_x), hidden_low))
    down_weights = down_mine, to_core(down_mine)

    down_parts = hold((cot_span, cot_other, hidden_low, hidden_other), down_mine)
    down_give = outer(*down_parts, 1)
    down_back = to_x(down_give)
    down_keep = outer(*hold(down_parts, down_give), 0)
    mlp_parts = project_back([hold(hidden_low, down_keep)], [down_weights])
    grad_gate_pre, grad_up_pre = hidden_grads(
        hold(cot_span, mlp_parts), down_weights, gate_slope, up_slope
    )
    gate_other = cross_right(grad_gate_pre, 1)
    up_other = cross_right(grad_up_pre, 1)
    branch_mlp = scatter_first(*mlp_parts)
    back_parts = project_back(
        [grad_gate_pre, grad_up_pre], [gate_weights, up_weights]
    )
    branch_mlp = scatter_middle(*hold(branch_mlp, back_parts))
    normed_back = scatter_first(*hold(back_parts, branch_mlp))
    down_keep, down_give = far_halves(where, hold((down_keep, down_back), branch_mlp))
    down_far = to_z(down_give, 2)
    gate_parts = hold((span_two, span_other, grad_gate_pre, gate_other), down_give)
    gate_give = outer(*gate_parts, 1)
    gate_back = to_x(gate_give)
    normed_back = scatter_second(*scatter_middle(*hold(normed_back, gate_give)))
    gate_keep = outer(*hold(gate_parts, normed_back[:2]), 0)
    up_parts = hold((span_two, span_other, grad_up_pre, up_other), gate_keep)
    up_give = outer(*up_parts, 1)
    up_keep = outer(*hold(up_parts, up_give), 0)
    grad_residual, gain_two_term, grad_one, grad_two = dense_call(
        residual_grad_kernel,
        "residual_grad",
        [(row_shape, jnp.float32), ((1, D), jnp.float32)] + [(half_shape, jnp.bfloat16)] * 2,
        [],
        (*hold(normed_back, up_keep), residual, gain_two, cot_in),
    )
    grad_wait = gather_first(grad_one, grad_two)
    down_own, down_other = near_halves(where, *hold((down_keep, down_far), grad_wait[2:]))
    gate_keep, gate_give = far_halves(where, hold((gate_keep, gate_back), down_other))
    gate_far = to_z(gate_give, 2)
    up_back = to_x(hold(up_give, gate_give))
    grad_wait = gather_second(*hold(grad_wait, gate_give))
    grad_span = take_rows(*grad_wait)
    down_near = to_z(hold(down_other, grad_span), 1)
    span_grad_other = cross_left(grad_span)
    grad_attended = project(grad_span, first_weights, heads_width, query_width, jnp.bfloat16)
    grad_query, grad_early, grad_own = dense_call(
        functools.partial(attend_back_kernel, score_scale),
        "attend_back",
        [
            ((group_rows, query_width), jnp.bfloat16),
            ((group_rows, 2 * key_width), jnp.bfloat16),
            ((group_rows, 2 * key_width), jnp.float32),
        ],
        [
            pltpu.VMEM((2 * group_rows, group_rows), jnp.float32),
            pltpu.VMEM((2 * group_rows, GROUP * group_rows), jnp.bfloat16),
            pltpu.VMEM((2 * group_rows, GROUP * group_rows), jnp.bfloat16),
        ],
        (
            query_rot,
            early_kv,
            own_kv,
            query_ids,
            key_ids,
            log_total,
            grad_attended,
            cos_wide,
            sin_wide,
        ),
    )
    gate_own, gate_other = near_halves(where, *hold((gate_keep, gate_far), grad_early))
    up_terms = hold((up_keep, up_back), gate_other, down_near)
    late_kv = lax.ppermute(hold(grad_early, up_terms[1]), "seq", [(2, 0), (3, 1)])
    out_parts = hold((grad_span, span_grad_other, attended_low, attended_other), up_terms[1])
    gate_near = to_z(hold(gate_other, up_terms[1]), 1)
    out_give = outer(*out_parts, 1)
    out_back = to_x(out_give)
    out_keep = outer(*out_parts, 0)
    both_keep, both_give = far_halves(where, up_terms, hold((out_keep, out_back), late_kv, gate_near))
    both_far = to_z(both_give, 2)
    branch_mlp = scatter_second(*hold(branch_mlp, both_give))
    (grad_raw,) = dense_call(
        join_kernel,
        "join",
        [((group_rows, heads_width), jnp.bfloat16)],
        [],
        (grad_query, grad_own, hold(late_kv, both_give), cos_wide, sin_wide),
    )
    raw_other = cross_right(grad_raw, 2)
    first_parts = project_back([grad_raw], [first_weights])
    first_back = scatter_first(*first_parts)
    heads_parts = hold((normed_one, normed_other, grad_raw, raw_other), first_parts)
    heads_give = outer(*heads_parts, 1)
    heads_back = to_x(heads_give)
    heads_keep = outer(*heads_parts, 0)
    units = w_gate.shape[1]
    (gain_one_term,) = dense_call(
        gain_kernel,
        "gain",
        [((1, D), jnp.float32)],
        [],
        (*hold(first_parts, heads_keep), token_span),
    )
    gain_rows = jnp.concatenate([gain_one_term, gain_two_term], axis=0)
    gain_rows = gain_rows[:, :middle] + to_core(gain_rows[:, middle:])
    gain_rows = gain_rows + to_tp(gain_rows)
    first_back = scatter_middle(*hold(first_back, gain_rows))
    heads_keep, heads_give = far_halves(where, hold((heads_keep, heads_back), first_back))
    heads_far = to_z(heads_give, 2)
    gain_rows = hold(gain_rows, heads_give)
    gain_rows = gain_rows[:, :quarter] + to_x(gain_rows[:, quarter:])
    both_own, both_other = near_halves(
        where, *hold((both_keep, both_far), heads_give, gain_rows, branch_mlp[2:])
    )
    both_near = to_z(both_other, 1)
    first_back = scatter_second(*hold(first_back, both_other))
    (grad_rows,) = dense_call(
        token_grad_kernel,
        "token_grad",
        [(row_shape, jnp.float32)],
        [],
        (*first_back, tokens_in, gain_one, grad_residual),
    )
    gain_blocks = hold(gain_rows, both_other).reshape(2, 4, block_rows)
    gain_pair = [
        lax.dynamic_index_in_dim(gain_blocks, seq_index ^ k, 1, keepdims=False) for k in range(4)
    ]
    gain_half = jnp.stack(gain_pair[:2]) + to_z(jnp.stack(gain_pair[2:]), 2)
    gain_grads = gain_half[0] + to_z(gain_half[1], 1)
    heads_own, heads_other = near_halves(
        where, *hold((heads_keep, heads_far), grad_rows, both_near)
    )
    heads_near = to_z(heads_other, 1)
    (grad_down,) = join_halves(where, *hold((down_own, down_near), heads_other), (units,), True)
    (grad_gate,) = join_halves(where, *hold((gate_own, gate_near), grad_down), (units,))
    (mixed,) = dense_call(
        mixed_kernel,
        "mixed",
        [(row_shape, jnp.bfloat16)],
        [],
        (*hold(branch_mlp, grad_gate), residual),
    )
    both_own, both_near = hold((both_own, both_near), grad_gate)
    (grad_up,) = join_halves(
        where,
        *hold((both_own[:, :hidden_width], both_near[:, :hidden_width]), heads_other),
        (units,),
    )
    (grad_out,) = join_halves(
        where, both_own[:, hidden_width:], both_near[:, hidden_width:], (w_out.shape[0],), True
    )
    grad_query_w, grad_key_w, grad_value_w = join_halves(
        where,
        *hold((heads_own, heads_near), grad_out, grad_up),
        (2 * query_width, 2 * key_width, 2 * key_width),
    )
    mixed_out = columns_out(mixed)
    grad_tokens = columns_out(hold(grad_rows, grad_out))
    return (
        mixed_out,
        grad_tokens,
        grad_query_w,
        grad_key_w,
        grad_value_w,
        grad_out,
        grad_gate,
        grad_up,
        grad_down,
        gain_grads,
    )


def solution(mesh):
    halves = mesh.shape["seq"] == 4 and mesh.shape["tp"] == 2 and mesh.shape["fsdp"] == 4
    plan = half_plan if halves else per_device
    in_specs = (
        P(("fsdp", "seq", "tp"), None),
        P("fsdp", None),
        P(("fsdp", "seq"), "tp"),
        P(("fsdp", "seq"), "tp"),
        P(("fsdp", "seq"), "tp"),
        P("tp", ("fsdp", "seq")),
        P(("fsdp", "seq"), "tp"),
        P(("fsdp", "seq"), "tp"),
        P("tp", ("fsdp", "seq")),
        P(None, ("fsdp", "seq")),
        P(("fsdp", "seq", "tp"), None),
    )
    out_specs = (
        P(("fsdp", "seq", "tp"), None),
        P(("fsdp", "seq", "tp"), None),
        P(("fsdp", "seq"), "tp"),
        P(("fsdp", "seq"), "tp"),
        P(("fsdp", "seq"), "tp"),
        P("tp", ("fsdp", "seq")),
        P(("fsdp", "seq"), "tp"),
        P(("fsdp", "seq"), "tp"),
        P("tp", ("fsdp", "seq")),
        P(None, ("fsdp", "seq")),
    )
    return jax.shard_map(
        plan, mesh=mesh, in_specs=in_specs, out_specs=out_specs, check_vma=False
    )
```
